32 devices in a mesh: dp: 2 (over y), row: 4 (over z), col: 4 (over x, core).
Axes of the slice: x: 2, y: 2, z: 4, core: 2. Of those that a mesh axis runs over, the one named last changes fastest.
Arguments:
- inputs: bfloat16 [2, 8, 512, 2048], P(None, ('dp', 'row'), 'col'), may hold values from -6 to 6
- lengths: int32 [2, 8], P(None, ('dp', 'row')), may hold values from 128 to 512, as said below
- wqkv: bfloat16 [2048, 4096], P(('dp', 'row'), 'col'), may hold values from -0.125 to 0.125
- wo: bfloat16 [2048, 2048], P('col', ('dp', 'row')), may hold values from -0.75 to 0.75
- w1: bfloat16 [2048, 8192], P(('dp', 'row'), 'col'), may hold values from -0.125 to 0.125
- w3: bfloat16 [2048, 8192], P(('dp', 'row'), 'col'), may hold values from -0.125 to 0.125
- w2: bfloat16 [8192, 2048], P('col', ('dp', 'row')), may hold values from -0.0625 to 0.0625
- attn_gain: bfloat16 [2048], P(('dp', 'row')), may hold values from 0.099609375 to 1.8984375
- ffn_gain: bfloat16 [2048], P(('dp', 'row')), may hold values from 0.099609375 to 1.8984375
- cotangent: bfloat16 [2, 8, 512, 2048], P(None, ('dp', 'row'), 'col'), may hold values from -6 to 6
Outputs:
- outputs: bfloat16 [2, 8, 512, 2048], P(None, ('dp', 'row'), 'col')
- input_grad: bfloat16 [2, 8, 512, 2048], P(None, ('dp', 'row'), 'col')
- attn_gain_grad: float32 [2048], P(('dp', 'row'))
- ffn_gain_grad: float32 [2048], P(('dp', 'row'))
- wqkv_grad: float32 [2048, 4096], P(('dp', 'row'), 'col')
- wo_grad: float32 [2048, 2048], P('col', ('dp', 'row'))
- w1_grad: float32 [2048, 8192], P(('dp', 'row'), 'col')
- w3_grad: float32 [2048, 8192], P(('dp', 'row'), 'col')
- w2_grad: float32 [8192, 2048], P('col', ('dp', 'row'))
The draws below stay inside these ranges and needn't reach their ends.
Inputs may be any that keep to these rules, and one draw needn't show every extreme that they name: `lengths`: in every slot one of the 2 micro-batches has length exactly 512; the others lie from 128 to 512.
All inputs are finite; a program needn't handle non-finite values.
Results may differ from the reference program's by a relative error of at most 0.018.
Values may be sent and summed in bfloat16 or wider, within the bound.
No kernel may reach another device: no remote copies, remote signals or barrier semaphores. Data moves between devices by JAX's collectives and lax.ppermute only.
A program may use at most 256 MiB of HBM per device.

```python
import jax
import jax.numpy as jnp
from jax import lax

MODEL_DIM = 2048
HQ = 16
KEY_VALUE_HEADS = 8
HEAD_SIZE = 128
FF = 8192
SEQ = 512
MICRO = 2
QUERY_PER_GROUP = 2
SLOTS = 8


def draw_lengths(key, part):
    key = jax.random.fold_in(key, 7)
    first_key, second_key = jax.random.split(key)
    base = jax.random.randint(first_key, (MICRO, SLOTS), SEQ // 4, SEQ + 1)
    chosen = jax.random.randint(second_key, (SLOTS,), 0, MICRO)
    picked = jnp.arange(MICRO)[:, None] == chosen[None, :]
    return jnp.where(picked, SEQ, base).astype(jnp.int32)


def block_levels(key, extent, shards, smallest, high):
    level = 1.0
    for position, blocks in shards:
        heights = jax.random.uniform(jax.random.fold_in(jax.random.fold_in(key, 6), position), (blocks,), jnp.float32, smallest / len(shards), high / len(shards))
        level = level * jnp.repeat(jnp.exp(heights), extent[position] // blocks).reshape((-1,) + (1,) * (len(extent) - 1 - position))
    return level


def scatter_about(key, extent, deviation, limit, pieces=(), held_as=jnp.bfloat16):
    factor_of = block_levels(key, extent, pieces, -0.22, 0.18) if pieces else 1.0
    drawn = jax.random.normal(key, extent, jnp.float32) * deviation * factor_of
    return jnp.minimum(jnp.maximum(drawn, -limit), limit).astype(held_as)


def setup_inputs(seed: int = 0) -> dict:
    splits = jax.random.split(jax.random.key(seed), 11)
    return {
        "inputs": scatter_about(splits[0], (MICRO, SLOTS, SEQ, MODEL_DIM), 1.0, 6.0, ((1, 8), (2, 4))),
        "lengths": draw_lengths(jax.random.fold_in(splits[10], 71), 0),
        "wqkv": scatter_about(splits[2], (MODEL_DIM, KEY_VALUE_HEADS * (QUERY_PER_GROUP + 2) * HEAD_SIZE), MODEL_DIM ** -0.5, 0.125, ((0, 8), (1, 4))),
        "wo": scatter_about(splits[3], (HQ * HEAD_SIZE, MODEL_DIM), (max(1, HQ * HEAD_SIZE * 16 // SEQ)) ** -0.5, 0.75, ((0, 4), (1, 8))),
        "w1": scatter_about(splits[4], (MODEL_DIM, FF), MODEL_DIM ** -0.5, 0.125, ((0, 8), (1, 4))),
        "w3": scatter_about(splits[5], (MODEL_DIM, FF), MODEL_DIM ** -0.5, 0.125, ((0, 8), (1, 4))),
        "w2": scatter_about(splits[6], (FF, MODEL_DIM), FF ** -0.5, 0.0625, ((0, 4), (1, 8))),
        "attn_gain": jnp.clip(1.0 + 0.18 * jax.random.normal(splits[7], (MODEL_DIM,), jnp.float32), 0.099609375, 1.8984375).astype(jnp.bfloat16),
        "ffn_gain": jnp.clip(1.0 + 0.18 * jax.random.normal(splits[8], (MODEL_DIM,), jnp.float32), 0.099609375, 1.8984375).astype(jnp.bfloat16),
        "cotangent": scatter_about(splits[9], (MICRO, SLOTS, SEQ, MODEL_DIM), 1.0, 6.0, ((1, 8), (2, 4))),
    }


EPS = 1e-05
THETA = 1000000.0
NEGATIVE = -1e+30

@jax.custom_vjp
def low(v):
    return lax.optimization_barrier(v.astype(jnp.bfloat16)).astype(jnp.float32)

@jax.custom_vjp
def lower_precision_back(v):
    return v

def low_keep(v):
    return (low(v), None)

def low_pass(kept, grad):
    return (grad,)

def back_keep(v):
    return (v, None)

def back_low(kept, grad):
    return (low(grad),)
low.defvjp(low_keep, low_pass)
lower_precision_back.defvjp(back_keep, back_low)

def matrix_product(left, right):
    return jnp.dot(left, right, precision=lax.Precision.HIGHEST, preferred_element_type=jnp.float32)

def rms_norm(values, gain):
    inverse = lax.rsqrt(lax.optimization_barrier(jnp.mean(values * values, axis=-1, keepdims=True)) + EPS)
    return values * inverse * gain

def rope_tables(token_rows, head):
    places = jnp.arange(token_rows, dtype=jnp.float32)
    freqs = THETA ** (-jnp.arange(head // 2, dtype=jnp.float32) * 2.0 / head)
    angles = places[:, None] * freqs[None, :]
    return (jnp.cos(angles), jnp.sin(angles))

def rotate(values, cosine, sine):
    half = values.shape[-1] // 2
    first_half = values[..., :half]
    second_half = values[..., half:]
    cos_view = cosine[:, None, None, :]
    sin_view = sine[:, None, None, :]
    return jnp.concatenate([first_half * cos_view - second_half * sin_view, second_half * cos_view + first_half * sin_view], axis=-1)

def layer(source, length, wqkv, wo, w1, w3, w2, attn_gain, ffn_gain):
    token_rows = source.shape[0]
    cosine, sine = rope_tables(token_rows, HEAD_SIZE)
    first_normed = low(rms_norm(source, attn_gain))
    projected_rows = lower_precision_back(matrix_product(first_normed, wqkv)).reshape(token_rows, KEY_VALUE_HEADS, QUERY_PER_GROUP + 2, HEAD_SIZE)
    query = low(rotate(projected_rows[:, :, :QUERY_PER_GROUP], cosine, sine))
    keys = low(rotate(projected_rows[:, :, QUERY_PER_GROUP:QUERY_PER_GROUP + 1], cosine, sine)[:, :, 0])
    values = low(projected_rows[:, :, QUERY_PER_GROUP + 1])
    block = min(token_rows, 512)
    count = token_rows // block
    key_pos = jnp.arange(token_rows, dtype=jnp.int32)
    score_scale = HEAD_SIZE ** (-0.5)

    def one_block(index):
        start = (index * block).astype(jnp.int32)
        query_block = lax.dynamic_slice_in_dim(query, start, block, 0)
        query_pos = start + jnp.arange(block, dtype=jnp.int32)
        scores = jnp.einsum('qgrd,kgd->grqk', query_block, keys, precision=lax.Precision.HIGHEST) * score_scale
        scores = lower_precision_back(scores)
        allowed = (key_pos[None, :] <= query_pos[:, None]) & (key_pos[None, :] < length)
        scores = jnp.where(allowed, scores, NEGATIVE)
        highest = lax.optimization_barrier(jnp.max(scores, axis=-1, keepdims=True))
        expo = jnp.exp(scores - highest)
        probs = low(expo / lax.optimization_barrier(jnp.sum(expo, axis=-1, keepdims=True)))
        attended = jnp.einsum('grqk,kgd->qgrd', probs, values, precision=lax.Precision.HIGHEST)
        return low(lower_precision_back(attended))
    attended = lax.map(jax.checkpoint(one_block), jnp.arange(count, dtype=jnp.int32)).reshape(token_rows, HQ * HEAD_SIZE)
    residual = source + lower_precision_back(matrix_product(attended, wo))
    normed2 = low(rms_norm(residual, ffn_gain))
    gate_val = lower_precision_back(matrix_product(normed2, w1))
    up_val = lower_precision_back(matrix_product(normed2, w3))
    hidden = low(jax.nn.silu(gate_val) * up_val)
    return residual + lower_precision_back(matrix_product(hidden, w2))

def reference(inputs, lengths, wqkv, wo, w1, w3, w2, attn_gain, ffn_gain, cotangent):
    weights = tuple((item.astype(jnp.float32) for item in (wqkv, wo, w1, w3, w2, attn_gain, ffn_gain)))
    total_slots = MICRO * SLOTS
    sources = inputs.reshape(total_slots, SEQ, MODEL_DIM).astype(jnp.float32)
    upstreams = cotangent.reshape(total_slots, SEQ, MODEL_DIM).astype(jnp.float32)
    slot_lengths = lengths.reshape(total_slots).astype(jnp.int32)

    def step(totals, item):
        source, upstream, length = item

        def forward(source_in, *params):
            return layer(source_in, length, *params)
        result, pull = jax.vjp(forward, source, *weights)
        valid = (jnp.arange(SEQ, dtype=jnp.int32) < length).astype(jnp.float32)[:, None]
        grads = pull(upstream * valid)
        totals = tuple((left + right for left, right in zip(totals, grads[1:])))
        return (totals, (result.astype(jnp.bfloat16), grads[0].astype(jnp.bfloat16)))
    zeros = tuple((jnp.zeros_like(item) for item in weights))
    totals, (results, source_grads) = lax.scan(step, zeros, (sources, upstreams, slot_lengths))
    return (results.reshape(inputs.shape), source_grads.reshape(inputs.shape), totals[5], totals[6], totals[0], totals[1], totals[2], totals[3], totals[4])
```

```python
import jax
import jax.numpy as jnp
from jax import lax
from jax.sharding import PartitionSpec as P

HEAD_SIZE = 128
QUERY_PER_GROUP = 2
EPS = 1e-05
THETA = 1000000.0
NEGATIVE = -1e30
CHUNKS = 4
BF = jnp.bfloat16
F32 = jnp.float32


def xchg(value, axis, bit):
    size = lax.axis_size(axis)
    return lax.ppermute(value, axis, [(i, i ^ bit) for i in range(size)])


def dot(left, right, left_dim, right_dim):
    return lax.dot_general(
        left, right, (((left_dim,), (right_dim,)), ((), ())), preferred_element_type=F32
    )


def gather_tokens(own):
    over_x = xchg(own, "col", 2)
    over_y = xchg(own, "dp", 1)
    first = xchg(over_y[:1], "col", 2)
    second = xchg(over_x[1:], "dp", 1)
    diagonal = jnp.concatenate((first, second), axis=0)
    blocks = []
    for block in (own, over_x, over_y, diagonal):
        blocks.extend((block, xchg(block, "col", 1)))
    return jnp.stack(blocks).reshape((2, 4) + own.shape)


def add(left, right):
    return left.astype(F32) + right.astype(F32)


def scatter_tokens(parts):
    parts = parts.reshape((2, 2, 2) + parts.shape[2:])
    quad = add(parts[:, :, 0], xchg(parts[:, :, 1], "col", 1)).astype(BF)
    first, second = quad[:, :, 0], quad[:, :, 1]
    first = add(first[:, 0], xchg(first[:, 1], "col", 2)).astype(BF)
    second = add(second[0], xchg(second[1], "dp", 1)).astype(BF)
    first = add(first[0], xchg(first[1], "dp", 1))
    second = add(second[0], xchg(second[1], "col", 2))
    return jnp.stack((first, second))


def dp_groups():
    size = lax.axis_size("dp")
    return [[i for i in range(size) if i % 2 == low] for low in (0, 1)]


def gather_weight(halves):
    low = lax.axis_index("dp") % 2
    mine = jnp.where(low == 0, halves[0], halves[1])
    sent = jnp.where(low == 0, halves[1], halves[0])
    came = xchg(sent, "dp", 1)
    pair = jnp.where(low == 0, jnp.stack((mine, came)), jnp.stack((came, mine)))
    full = lax.all_gather(pair, "row", axis=1, tiled=True)
    if lax.axis_size("dp") > 2:
        full = lax.all_gather(full, "dp", axis=0, tiled=True, axis_index_groups=dp_groups())
    return full.reshape(-1, full.shape[-1])


def scatter_weight(grad):
    low = lax.axis_index("dp") % 2
    size = lax.axis_size("dp")
    grad = grad.reshape(size, -1, grad.shape[-1])
    if size > 2:
        grad = lax.psum_scatter(
            grad, "dp", scatter_dimension=0, tiled=True, axis_index_groups=dp_groups()
        )
    pair = lax.psum_scatter(grad, "row", scatter_dimension=1, tiled=True)
    mine = jnp.where(low == 0, pair[0], pair[1])
    sent = jnp.where(low == 0, pair[1], pair[0])
    came = xchg(sent, "dp", 1)
    return jnp.where(low == 0, jnp.stack((mine, came)), jnp.stack((came, mine))).astype(F32)


def gather_gains(gains):
    blocks = gains[None]
    rows, size = lax.axis_size("row"), lax.axis_size("dp")
    bit = 1
    while bit < rows:
        blocks = jnp.concatenate((blocks, xchg(blocks, "row", bit)))
        bit *= 2
    bit = 1
    while bit < size:
        blocks = jnp.concatenate((blocks, xchg(blocks, "dp", bit)))
        bit *= 2
    me = lax.axis_index("dp") * rows + lax.axis_index("row")
    order = jnp.arange(rows * size, dtype=jnp.int32) ^ me
    return jnp.take(blocks, order, axis=0).transpose(1, 0, 2).reshape(gains.shape[0], -1)


def scatter_gain(grad):
    rows, size = lax.axis_size("row"), lax.axis_size("dp")
    bit = 1
    while bit < lax.axis_size("col"):
        grad = grad + xchg(grad, "col", bit)
        bit *= 2
    me = lax.axis_index("dp") * rows + lax.axis_index("row")
    order = jnp.arange(rows * size, dtype=jnp.int32) ^ me
    blocks = jnp.take(grad.reshape(rows * size, -1), order, axis=0)
    bit = size // 2
    while bit:
        half = blocks.shape[0] // 2
        blocks = blocks[:half] + xchg(blocks[half:], "dp", bit)
        bit //= 2
    bit = rows // 2
    while bit:
        half = blocks.shape[0] // 2
        blocks = blocks[:half] + xchg(blocks[half:], "row", bit)
        bit //= 2
    return blocks[0]


def rope_tables(positions):
    freqs = THETA ** (-jnp.arange(HEAD_SIZE // 2, dtype=F32) * 2.0 / HEAD_SIZE)
    angles = positions.astype(F32)[:, None] * freqs[None, :]
    return jnp.cos(angles)[:, None, None, :], jnp.sin(angles)[:, None, None, :]


def rotate(values, cosine, sine):
    half = HEAD_SIZE // 2
    first, second = values[..., :half], values[..., half:]
    return jnp.concatenate(
        (first * cosine - second * sine, second * cosine + first * sine), axis=-1
    )


def rms_norm(values, gain):
    inverse = lax.rsqrt(jnp.mean(values * values, axis=-1, keepdims=True) + EPS)
    return values * inverse * gain, inverse


def rms_back(values, inverse, gain, upstream):
    scaled = upstream * gain
    inner = jnp.mean(scaled * values, axis=-1, keepdims=True)
    grad_in = inverse * scaled - values * (inverse * inverse * inverse) * inner
    grad_gain = jnp.sum(upstream * values * inverse, axis=(0, 1))
    return grad_in, grad_gain


def score(query, keys, allowed):
    scores = jnp.einsum("sqgrd,skgd->sgrqk", query, keys, preferred_element_type=F32)
    return jnp.where(allowed, scores * HEAD_SIZE ** (-0.5), NEGATIVE)


def attend(query, keys, values, allowed):
    scores = score(query, keys, allowed)
    highest = jnp.max(scores, axis=-1, keepdims=True)
    expo = jnp.exp(scores - highest)
    total = jnp.sum(expo, axis=-1, keepdims=True)
    probs = (expo / total).astype(BF)
    attended = jnp.einsum("sgrqk,skgd->sqgrd", probs, values, preferred_element_type=F32)
    return attended.astype(BF), highest + jnp.log(total)


def attend_back(query, keys, values, log_totals, grad_out, allowed):
    scale = HEAD_SIZE ** (-0.5)
    probs = jnp.exp(score(query, keys, allowed) - log_totals)
    grad_probs = jnp.einsum("sqgrd,skgd->sgrqk", grad_out, values, preferred_element_type=F32)
    values_grad = jnp.einsum(
        "sgrqk,sqgrd->skgd", probs.astype(BF), grad_out, preferred_element_type=F32
    )
    inner = jnp.sum(probs * grad_probs, axis=-1, keepdims=True)
    grad_scores = (probs * (grad_probs - inner)).astype(BF)
    query_grad = jnp.einsum("sgrqk,skgd->sqgrd", grad_scores, keys, preferred_element_type=F32)
    keys_grad = jnp.einsum("sgrqk,sqgrd->skgd", grad_scores, query, preferred_element_type=F32)
    return query_grad * scale, keys_grad * scale, values_grad


def body(inputs, lengths, wqkv, wo, w1, w3, w2, attn_gain, ffn_gain, cotangent):
    micro, _, rows, width = inputs.shape
    cols = lax.axis_size("col")
    block = (2, cols, micro, rows)
    tokens = 2 * cols * micro * rows
    sequences = 2 * micro
    places = cols * rows
    me = lax.axis_index("col")
    groups = wqkv.shape[1] // ((QUERY_PER_GROUP + 2) * HEAD_SIZE) // 2
    hidden_units = w1.shape[1] // 2
    cut = hidden_units // CHUNKS

    def by_sequence(flat):
        return flat.reshape(block + (-1,)).transpose(0, 2, 1, 3, 4).reshape(sequences, places, -1)

    def by_token(per_sequence):
        return (
            per_sequence.reshape(2, micro, cols, rows, -1)
            .transpose(0, 2, 1, 3, 4)
            .reshape(tokens, -1)
        )

    gains = gather_gains(jnp.stack((attn_gain, ffn_gain))).astype(F32)
    gain_attn, gain_ffn = gains[0], gains[1]
    d = wqkv.shape[0]
    qkv_w = gather_weight(wqkv.reshape(d, 2, -1).transpose(1, 0, 2))
    out_w = gather_weight(wo.reshape(2, -1, d).transpose(0, 2, 1))
    ffn_halves = jnp.concatenate(
        (
            w1.reshape(d, 2, CHUNKS, cut).transpose(1, 2, 0, 3),
            w3.reshape(d, 2, CHUNKS, cut).transpose(1, 2, 0, 3),
            w2.reshape(2, CHUNKS, cut, d).transpose(0, 1, 3, 2),
        ),
        axis=-1,
    )

    source = inputs[:, 0].astype(F32)
    normed1, inverse1 = rms_norm(source, gain_attn)
    attn_rows = gather_tokens(normed1.astype(BF)).reshape(tokens, width)
    all_lengths = jnp.stack((lengths, xchg(lengths, "dp", 1))).reshape(sequences)
    positions = (
        (jnp.arange(cols, dtype=jnp.int32) ^ me)[:, None] * rows
        + jnp.arange(rows, dtype=jnp.int32)[None, :]
    ).reshape(places)
    cosine, sine = rope_tables(positions)
    allowed = (positions[None, None, :] <= positions[None, :, None]) & (
        positions[None, None, :] < all_lengths[:, None, None]
    )
    allowed = allowed[:, None, None]
    projected = by_sequence(dot(attn_rows, qkv_w, 1, 0)).reshape(
        sequences, places, groups, QUERY_PER_GROUP + 2, HEAD_SIZE
    )
    query = rotate(projected[:, :, :, :QUERY_PER_GROUP], cosine, sine).astype(BF)
    keys = rotate(
        projected[:, :, :, QUERY_PER_GROUP : QUERY_PER_GROUP + 1], cosine, sine
    )[:, :, :, 0].astype(BF)
    values = projected[:, :, :, QUERY_PER_GROUP + 1].astype(BF)
    attended, log_totals = attend(query, keys, values, allowed)
    attended = by_token(attended)
    residual = source + scatter_tokens(
        dot(attended, out_w, 1, 1).astype(BF).reshape(block + (width,))
    )

    normed2, inverse2 = rms_norm(residual, gain_ffn)
    ffn_rows = gather_tokens(normed2.astype(BF)).reshape(tokens, width)
    own_places = me * rows + jnp.arange(rows, dtype=jnp.int32)
    valid = (own_places[None, :] < lengths).astype(F32)[:, :, None]
    upstream = cotangent[:, 0].astype(F32) * valid
    piece = gather_tokens(upstream.astype(BF)).reshape(tokens, width)
    hiddens, grad_pairs, pair_ws, down_ws, ffn_grads = [], [], [], [], []
    for chunk in range(CHUNKS):
        weights = gather_weight(ffn_halves[:, chunk])
        pair_w, down_w = weights[:, : 2 * cut], weights[:, 2 * cut :]
        gate_up = dot(ffn_rows, pair_w, 1, 0)
        gate_val, up_val = gate_up[:, :cut], gate_up[:, cut:]
        sigma = jax.nn.sigmoid(gate_val)
        swish = gate_val * sigma
        hidden = (swish * up_val).astype(BF)
        hidden_grad = dot(piece, down_w, 1, 0)
        grad_gate = hidden_grad * up_val * sigma * (1.0 + gate_val * (1.0 - sigma))
        grad_up = hidden_grad * swish
        grad_pair = jnp.concatenate((grad_gate, grad_up), axis=1).astype(BF)
        grads = jnp.concatenate(
            (dot(ffn_rows, grad_pair, 0, 0).astype(BF), dot(piece, hidden, 0, 0).astype(BF)),
            axis=1,
        )
        ffn_grads.append(scatter_weight(grads))
        hiddens.append(hidden)
        grad_pairs.append(grad_pair)
        pair_ws.append(pair_w)
        down_ws.append(down_w)
    normed2_grad = dot(
        jnp.concatenate(grad_pairs, axis=1), jnp.concatenate(pair_ws, axis=1), 1, 1
    )
    normed2_grad = scatter_tokens(normed2_grad.astype(BF).reshape(block + (width,)))
    ffn_out = dot(jnp.concatenate(hiddens, axis=1), jnp.concatenate(down_ws, axis=1), 1, 1)
    result = residual + scatter_tokens(ffn_out.astype(BF).reshape(block + (width,)))

    residual_in, gain2_grad = rms_back(residual, inverse2, gain_ffn, normed2_grad)
    residual_grad = upstream + residual_in
    attn_piece = gather_tokens(residual_grad.astype(BF)).reshape(tokens, width)
    out_grad = dot(attn_piece, attended, 0, 0).astype(BF)
    grad_out = by_sequence(dot(attn_piece, out_w, 1, 0).astype(BF)).reshape(query.shape)
    query_grad, keys_grad, values_grad = attend_back(
        query, keys, values, log_totals, grad_out, allowed
    )
    query_grad = rotate(query_grad, cosine, -sine)
    keys_grad = rotate(keys_grad[:, :, :, None], cosine, -sine)
    grad_proj = by_token(
        jnp.concatenate((query_grad, keys_grad, values_grad[:, :, :, None]), axis=3).astype(BF)
    )
    qkv_grad = dot(attn_rows, grad_proj, 0, 0).astype(BF)
    normed1_grad = scatter_tokens(dot(grad_proj, qkv_w, 1, 1).astype(BF).reshape(block + (width,)))
    source_in, gain1_grad = rms_back(source, inverse1, gain_attn, normed1_grad)
    source_grad = (residual_grad + source_in).astype(BF)

    qkv_shard = scatter_weight(qkv_grad).transpose(1, 0, 2).reshape(wqkv.shape)
    out_shard = scatter_weight(out_grad).transpose(0, 2, 1).reshape(wo.shape)
    ffn = jnp.stack(ffn_grads, axis=1)
    gate_shard = ffn[..., :cut].transpose(2, 0, 1, 3).reshape(w1.shape)
    up_shard = ffn[..., cut : 2 * cut].transpose(2, 0, 1, 3).reshape(w3.shape)
    down_shard = ffn[..., 2 * cut :].transpose(0, 1, 3, 2).reshape(w2.shape)
    return (
        result.astype(BF)[:, None],
        source_grad[:, None],
        scatter_gain(gain1_grad),
        scatter_gain(gain2_grad),
        qkv_shard,
        out_shard,
        gate_shard,
        up_shard,
        down_shard,
    )


def solution(mesh):
    tokens = P(None, ("dp", "row"), "col", None)
    in_specs = (
        tokens,
        P(None, ("dp", "row")),
        P(("dp", "row"), "col"),
        P("col", ("dp", "row")),
        P(("dp", "row"), "col"),
        P(("dp", "row"), "col"),
        P("col", ("dp", "row")),
        P(("dp", "row")),
        P(("dp", "row")),
        tokens,
    )
    out_specs = (
        tokens,
        tokens,
        P(("dp", "row")),
        P(("dp", "row")),
        P(("dp", "row"), "col"),
        P("col", ("dp", "row")),
        P(("dp", "row"), "col"),
        P(("dp", "row"), "col"),
        P("col", ("dp", "row")),
    )
    return jax.shard_map(body, mesh=mesh, in_specs=in_specs, out_specs=out_specs, check_vma=False)
```

```python
import jax
import jax.numpy as jnp
from jax import lax
from jax.experimental import pallas as pl
from jax.experimental.pallas import tpu as pltpu
from jax.sharding import PartitionSpec as P

HEAD_SIZE = 128
QUERY_PER_GROUP = 2
EPS = 1e-05
THETA = 1000000.0
NEGATIVE = -1e30
CHUNKS = 2
BF = jnp.bfloat16
F32 = jnp.float32


def xchg(value, axis, bit):
    size = lax.axis_size(axis)
    return lax.ppermute(value, axis, [(i, i ^ bit) for i in range(size)])


def dot(left, right, left_dim, right_dim):
    return lax.dot_general(
        left, right, (((left_dim,), (right_dim,)), ((), ())), preferred_element_type=F32
    )


def start_gather(owns):
    return [(own, xchg(own, "col", 2), xchg(own, "dp", 1)) for own in owns]


def cross(started):
    return [
        (*blocks, xchg(blocks[1], "dp", 1) if stream % 2 else xchg(blocks[2], "col", 2))
        for stream, blocks in enumerate(started)
    ]


def both_cores(crossed):
    return [
        [item for block in blocks for item in (block, xchg(block, "col", 1))] for blocks in crossed
    ]


def end_gather(started):
    return both_cores(cross(started))


def fenced(started, order):
    came = len(started[0]) - 1
    values = order.fence(*[value for blocks in started for value in blocks[1:]])
    return [(blocks[0], *values[came * m : came * (m + 1)]) for m, blocks in enumerate(started)]


def scatter_core(halves):
    return [xchg(send, "col", 1) for _, send in halves]


def scatter_first(halves, came, order):
    parts = []
    for stream, (keep, _) in enumerate(halves):
        kept, sent = fold(keep, came[stream], (0, 1) if stream % 2 else (0, 2), order)
        parts.append((kept, xchg(sent, "dp", 1) if stream % 2 else xchg(sent, "col", 2)))
    return parts


def scatter_second(parts, order):
    terms = []
    for stream, (keep, came) in enumerate(parts):
        kept, sent = fold(keep, came, (0,), order)
        terms.append((kept, xchg(sent, "col", 2) if stream % 2 else xchg(sent, "dp", 1)))
    return terms


def scatter_tokens(halves, order):
    return scatter_second(scatter_first(halves, scatter_core(halves), order), order)


def dp_groups():
    size = lax.axis_size("dp")
    return [[i for i in range(size) if i % 2 == low] for low in (0, 1)]


def gather_weight(mine, sent, low, order):
    pair = paired(mine, xchg(sent, "dp", 1), low, order)
    full = lax.all_gather(pair, "row", axis=1, tiled=True)
    if lax.axis_size("dp") > 2:
        full = lax.all_gather(full, "dp", axis=0, tiled=True, axis_index_groups=dp_groups())
    return full.reshape(-1, full.shape[-1])


def start_scatter(grad):
    size, rows = lax.axis_size("dp"), lax.axis_size("row")
    grad = grad.reshape((size, rows) + grad.shape[1:])
    if size > 2:
        grad = lax.psum_scatter(
            grad, "dp", scatter_dimension=0, tiled=True, axis_index_groups=dp_groups()
        )
    return grad


def end_scatter(pair):
    sent = lax.dynamic_index_in_dim(pair, 1 - lax.axis_index("dp") % 2, 0, keepdims=False)
    return pair, xchg(sent, "dp", 1)


def scatter_weight(grad):
    grad = start_scatter(grad)
    grad = grad.reshape(2, -1, grad.shape[-1])
    return end_scatter(lax.psum_scatter(grad, "row", scatter_dimension=1, tiled=True))


class Chain:
    def __init__(self, grad):
        self.grad = start_scatter(grad)
        self.rows = lax.axis_size("row")
        self.step = 1
        self.came = ()
        far = self.rows - 1
        self.send(self.block(far), self.block(-far))

    def place(self, offset):
        return jnp.clip(lax.axis_index("row") + offset, 0, self.rows - 1).astype(jnp.int32)

    def block(self, offset):
        return lax.dynamic_index_in_dim(self.grad, self.place(offset), 1, keepdims=False)

    def send(self, up, down):
        far = self.rows - self.step
        self.came = (
            lax.ppermute(up, "row", [(i, i + 1) for i in range(self.step)]),
            lax.ppermute(down, "row", [(i, i - 1) for i in range(far, self.rows)]),
        )

    def advance(self, order):
        self.step += 1
        far = self.rows - self.step
        places = jnp.stack((self.place(far), self.place(-far)))
        _, _, n, d = self.grad.shape
        part = pl.BlockSpec((1, n, d), lambda p, at: (p, 0, 0))

        def picked(which):
            return pl.BlockSpec((1, 1, n, d), lambda p, at: (p, at[which], 0, 0))

        def kernel(at_ref, up_ref, down_ref, first_ref, second_ref, *out_refs):
            if far:
                out_refs[0][...] = add(first_ref[0], up_ref[...]).astype(BF)
                out_refs[1][...] = add(second_ref[0], down_ref[...]).astype(BF)
            else:
                out_refs[0][...] = (add(first_ref[0], up_ref[...]) + down_ref[...].astype(F32)).astype(BF)

        count = 2 if far else 1
        outs = order.call(
            kernel,
            (2,),
            [part, part, picked(0), picked(1)],
            [part] * count,
            [shaped(2, n, d)] * count,
            (places, *self.came, self.grad, self.grad),
            prefetch=1,
            moved=24 * n * d,
        )
        if far:
            self.send(*outs)
            return None
        return end_scatter(outs[0])


def sum_over_col(value):
    return sum([xchg(value, "col", mask) for mask in range(1, lax.axis_size("col"))], value)


def rope_tables(positions):
    freqs = THETA ** (-jnp.arange(HEAD_SIZE // 2, dtype=F32) * 2.0 / HEAD_SIZE)
    angles = positions.astype(F32)[:, None] * freqs[None, :]
    cosine, sine = jnp.cos(angles), jnp.sin(angles)
    return jnp.concatenate((cosine, cosine), axis=1), jnp.concatenate((-sine, sine), axis=1)


class Order:
    def __init__(self):
        self.last = ()

    def wait(self, *values):
        self.last = self.last + values

    def fence(self, *values):
        return self.call(
            lambda *refs: None,
            (1,),
            [pl.BlockSpec(memory_space=pl.ANY)] * len(values),
            [pl.BlockSpec(memory_space=pl.ANY)] * len(values),
            [shaped(*value.shape, dtype=value.dtype) for value in values],
            values,
            aliases={i: i for i in range(len(values))},
        )

    def call(
        self, kernel, grid, in_specs, out_specs, out_shape, args, scratch=(), flops=0, moved=0, prefetch=0, aliases=None
    ):
        last = [token for token in self.last if all(token is not arg for arg in args)]
        tokens = len(last)
        count = len(args)

        def run(*refs):
            kernel(*refs[:count], *refs[count + tokens :])

        outs = pl.pallas_call(
            run,
            grid_spec=pltpu.PrefetchScalarGridSpec(
                num_scalar_prefetch=prefetch,
                grid=grid,
                in_specs=list(in_specs) + [pl.BlockSpec(memory_space=pl.ANY)] * tokens,
                out_specs=out_specs,
                scratch_shapes=list(scratch),
            ),
            out_shape=out_shape,
            input_output_aliases=aliases or {},
            compiler_params=pltpu.CompilerParams(vmem_limit_bytes=56 * 2**20),
            cost_estimate=pl.CostEstimate(flops=flops, bytes_accessed=moved, transcendentals=0),
        )(*args, *last)
        self.last = (outs[0] if isinstance(outs, (list, tuple)) else outs,)
        return outs


def shaped(*shape, dtype=BF):
    return jax.ShapeDtypeStruct(shape, dtype)


def whole(shape):
    return pl.BlockSpec(shape, lambda *_: (0,) * len(shape))


SCALARS = pl.BlockSpec(memory_space=pltpu.SMEM)


def prepare_attn_kernel(low_ref, qkv_ref, out_ref, gain_ref, mine_ref, sent_ref):
    wide = qkv_ref.shape[1] // 2
    tall = out_ref.shape[0] // 2
    for part, ref in ((low_ref[0], mine_ref), (1 - low_ref[0], sent_ref)):
        columns = qkv_ref[:, pl.ds(pl.multiple_of(part * wide, wide), wide)]
        ref[:, :wide] = (columns.astype(F32) * gain_ref[...]).astype(BF)
        ref[:, wide:] = out_ref[pl.ds(pl.multiple_of(part * tall, tall), tall), :].T


def prepare_attn(low, wqkv, wo, gain, order):
    d = wqkv.shape[0]
    out = shaped(d, wqkv.shape[1] // 2 + wo.shape[0] // 2)
    return order.call(
        prepare_attn_kernel,
        (1,),
        [SCALARS] + [whole(item.shape) for item in (wqkv, wo, gain)],
        [whole(out.shape)] * 2,
        [out, out],
        (low, wqkv, wo, gain),
        moved=4 * (wqkv.size + wo.size),
    )


def prepare_ffn_kernel(chunks, cut, low_ref, w1_ref, w3_ref, w2_ref, gain_ref, *refs):
    units = w1_ref.shape[1] // 2
    gain = gain_ref[...]
    for at, chunk in enumerate(chunks):
        for part, ref in ((low_ref[0], refs[2 * at]), (1 - low_ref[0], refs[2 * at + 1])):
            place = pl.ds(pl.multiple_of(part * units + chunk * cut, cut), cut)
            ref[:, :cut] = (w1_ref[:, place].astype(F32) * gain).astype(BF)
            ref[:, cut : 2 * cut] = (w3_ref[:, place].astype(F32) * gain).astype(BF)
            ref[:, 2 * cut :] = w2_ref[place, :].T


def prepare_ffn(chunks, cut, low, w1, w3, w2, gain, order):
    out = shaped(w1.shape[0], 3 * cut)
    outs = order.call(
        lambda *refs: prepare_ffn_kernel(chunks, cut, *refs),
        (1,),
        [SCALARS] + [whole(item.shape) for item in (w1, w3, w2, gain)],
        [whole(out.shape)] * (2 * len(chunks)),
        [out] * (2 * len(chunks)),
        (low, w1, w3, w2, gain),
        moved=12 * w1.size,
    )
    return [(outs[2 * i], outs[2 * i + 1]) for i in range(len(chunks))]


def paired_kernel(low_ref, mine_ref, came_ref, out_ref):
    out_ref[pl.ds(low_ref[0], 1)] = mine_ref[...][None]
    out_ref[pl.ds(1 - low_ref[0], 1)] = came_ref[...][None]


def paired(mine, came, low, order):
    out = shaped(2, *mine.shape)
    return order.call(
        paired_kernel,
        (1,),
        [SCALARS, whole(mine.shape), whole(mine.shape)],
        whole(out.shape),
        out,
        (low, mine, came),
        moved=8 * mine.size,
    )


def inverse_rms(values):
    return lax.rsqrt(jnp.mean(values * values, axis=-1, keepdims=True) + EPS)


def by_rows(kernel, ins, outs, order, scalars=None):
    def spec(item):
        lead = item.shape[:-2]
        block = lead + (item.shape[-2] // 4, item.shape[-1])
        return pl.BlockSpec(block, lambda l: (0,) * len(lead) + (l, 0))

    extra = [] if scalars is None else [scalars]
    return order.call(
        kernel,
        (4,),
        [SCALARS] * len(extra) + [spec(item) for item in ins],
        [spec(item) for item in outs],
        outs,
        (*extra, *ins),
        moved=4 * sum(item.size for item in (*ins, *outs)),
    )


def first_norm(inputs, order):
    def kernel(in_ref, *out_refs):
        for m, ref in enumerate(out_refs):
            values = in_ref[m].astype(F32)
            ref[...] = (values * inverse_rms(values)).astype(BF)

    return by_rows(kernel, [inputs], [shaped(*inputs.shape[1:])] * inputs.shape[0], order)


def masked(cotangent, scalars, order):
    def kernel(scalar_ref, in_ref, *out_refs):
        for m, ref in enumerate(out_refs):
            rows = ref.shape[0]
            place = scalar_ref[0] + pl.program_id(0) * rows
            places = place + lax.broadcasted_iota(jnp.int32, ref.shape, 0)
            valid = places < scalar_ref[1 + m]
            ref[...] = jnp.where(valid, in_ref[m].astype(F32), 0.0).astype(BF)

    return by_rows(kernel, [cotangent], [shaped(*cotangent.shape[1:])] * cotangent.shape[0], order, scalars)


def fold(keep, came, kept, order):
    others = [i for i in range(keep.shape[0]) if i not in kept]
    shape = (len(kept),) + keep.shape[1:]

    def kernel(keep_ref, came_ref, kept_ref, sent_ref):
        for at, (mine, other) in enumerate(zip(kept, others)):
            sent_ref[at] = add(keep_ref[other], came_ref[other]).astype(BF)
            kept_ref[at] = add(keep_ref[mine], came_ref[mine])

    return by_rows(kernel, [keep, came], [shaped(*shape, dtype=F32), shaped(*shape)], order)


def add(left, right):
    return left.astype(F32) + right.astype(F32)


def total_of(refs):
    return add(refs[0][0], refs[1][0])


def second_norm(inputs, terms, order):
    micro = inputs.shape[0]

    def kernel(in_ref, *refs):
        for m in range(micro):
            values = in_ref[m].astype(F32) + total_of(refs[2 * m : 2 * m + 2])
            refs[2 * micro + m][...] = (values * inverse_rms(values)).astype(BF)
            refs[3 * micro + m][...] = values

    shape = inputs.shape[1:]
    outs = by_rows(
        kernel,
        [inputs] + [item for pair in terms for item in pair],
        [shaped(*shape)] * micro + [shaped(*shape, dtype=F32)] * micro,
        order,
    )
    return outs[:micro], outs[micro:]


def finished(residual, terms, order):
    micro = len(residual)

    def kernel(*refs):
        for m in range(micro):
            refs[-1][m] = (refs[3 * m][...] + total_of(refs[3 * m + 1 : 3 * m + 3])).astype(BF)

    ins = [item for m in range(micro) for item in (residual[m], *terms[m])]
    return by_rows(kernel, ins, [shaped(micro, *residual[0].shape)], order)[0]


def norm_back(values, scaled):
    inverse = inverse_rms(values)
    inner = jnp.mean(scaled * values, axis=-1, keepdims=True)
    return inverse * scaled - values * (inverse * inverse * inverse) * inner


def second_norm_back(residual, upstream, terms, order):
    micro = len(residual)

    def kernel(*refs):
        outs = refs[4 * micro :]
        for m in range(micro):
            residual_ref, upstream_ref = refs[4 * m : 4 * m + 2]
            grad = upstream_ref[...].astype(F32) + norm_back(
                residual_ref[...], total_of(refs[4 * m + 2 : 4 * m + 4])
            )
            outs[m][...] = grad.astype(BF)
            outs[micro + m][...] = grad

    ins = [item for m in range(micro) for item in (residual[m], upstream[m], *terms[m])]
    shape = residual[0].shape
    outs = by_rows(
        kernel, ins, [shaped(*shape)] * micro + [shaped(*shape, dtype=F32)] * micro, order
    )
    return outs[:micro], outs[micro:]


def first_norm_back(inputs, upstream, terms, order):
    micro = inputs.shape[0]

    def kernel(in_ref, *refs):
        for m in range(micro):
            upstream_ref = refs[3 * m]
            grad = upstream_ref[...] + norm_back(
                in_ref[m].astype(F32), total_of(refs[3 * m + 1 : 3 * m + 3])
            )
            refs[-1][m] = grad.astype(BF)

    ins = [inputs] + [item for m in range(micro) for item in (upstream[m], *terms[m])]
    return by_rows(kernel, ins, [shaped(*inputs.shape)], order)[0]


def head_probs(query, keys, me, length, rows):
    places = query.shape[0]
    scores = dot(query, keys, 1, 1) * HEAD_SIZE ** (-0.5)
    queried = lax.broadcasted_iota(jnp.int32, (places, places), 0)
    keyed = lax.broadcasted_iota(jnp.int32, (places, places), 1)
    queried = ((queried // rows) ^ me) * rows + queried % rows
    keyed = ((keyed // rows) ^ me) * rows + keyed % rows
    scores = jnp.where((keyed <= queried) & (keyed < length), scores, NEGATIVE)
    expo = jnp.exp(scores - jnp.max(scores, axis=-1, keepdims=True))
    return expo * (1.0 / jnp.sum(expo, axis=-1, keepdims=True))


def turn(values, cosine, sine):
    return values * cosine + pltpu.roll(values, HEAD_SIZE // 2, 1) * sine


def joined(refs):
    return jnp.concatenate([ref[...] for ref in refs], axis=0)


def put_blocks(value, y, pairs, keep_ref, send_ref):
    rows = keep_ref.shape[1]
    for x in range(pairs):
        start = 2 * x * rows
        keep_ref[y * pairs + x] = value[start : start + rows].astype(BF)
        send_ref[y * pairs + x] = value[start + rows : start + 2 * rows].astype(BF)


def head_at(index):
    return slice(index * HEAD_SIZE, (index + 1) * HEAD_SIZE)


def attend_kernel(count, groups, scalar_ref, *refs):
    blocks = refs[:count]
    cos_ref, sin_ref, w_ref, keep_ref, send_ref, q_ref, k_ref, v_ref, a_ref = refs[count:]
    rows = blocks[0].shape[0]
    cols = count // 2
    span = (QUERY_PER_GROUP + 2) * HEAD_SIZE
    cosine, sine = cos_ref[...], sin_ref[...]
    for y in (0, 1):
        projected = dot(joined(blocks[y * cols : (y + 1) * cols]), w_ref[:, : groups * span], 1, 0)
        for g in range(groups):
            part = projected[:, g * span : (g + 1) * span]
            keys = turn(part[:, -2 * HEAD_SIZE : -HEAD_SIZE], cosine, sine).astype(BF)
            values = part[:, -HEAD_SIZE:].astype(BF)
            k_ref[y, :, head_at(g)] = keys
            v_ref[y, :, head_at(g)] = values
            for r in range(QUERY_PER_GROUP):
                query = turn(part[:, head_at(r)], cosine, sine).astype(BF)
                probs = head_probs(query, keys, scalar_ref[0], scalar_ref[1 + y], rows).astype(BF)
                at = head_at(g * QUERY_PER_GROUP + r)
                q_ref[y, :, at] = query
                a_ref[y, :, at] = dot(probs, values, 1, 0).astype(BF)
        put_blocks(dot(a_ref[y], w_ref[:, groups * span :], 1, 1), y, cols // 2, keep_ref, send_ref)


def attend(blocks, scalars, cosine, sine, weights, groups, order):
    count = len(blocks)
    rows, width = blocks[0].shape
    places = count // 2 * rows
    head = groups * HEAD_SIZE
    sizes = (QUERY_PER_GROUP * head, head, head, QUERY_PER_GROUP * head)
    outs = [(count // 2, rows, width)] * 2 + [(2, places, size) for size in sizes]
    return order.call(
        lambda *refs: attend_kernel(count, groups, *refs),
        (1,),
        [SCALARS] + [whole(item.shape) for item in (*blocks, cosine, sine, weights)],
        [whole(shape) for shape in outs],
        [jax.ShapeDtypeStruct(shape, BF) for shape in outs],
        flops=4 * places * weights.size + 16 * places * places * QUERY_PER_GROUP * head,
        moved=8 * places * width + 2 * weights.size,
        args=(scalars, *blocks, cosine, sine, weights,),
    )


def attend_back_kernel(count, groups, scalar_ref, *refs):
    pieces = refs[:count]
    cos_ref, sin_ref, w_ref, q_ref, k_ref, v_ref, keep_ref, send_ref, grad_ref = refs[count:]
    rows = pieces[0].shape[0]
    cols = count // 2
    span = (QUERY_PER_GROUP + 2) * HEAD_SIZE
    scale = HEAD_SIZE ** (-0.5)
    cosine, sine = cos_ref[...], -sin_ref[...]
    for y in (0, 1):
        piece = joined(pieces[y * cols : (y + 1) * cols])
        grad_out = dot(piece, w_ref[:, groups * span :], 1, 0).astype(BF)
        parts = []
        for g in range(groups):
            keys, values = k_ref[y, :, head_at(g)], v_ref[y, :, head_at(g)]
            keys_grad, values_grad = 0.0, 0.0
            for r in range(QUERY_PER_GROUP):
                at = head_at(g * QUERY_PER_GROUP + r)
                query, upstream = q_ref[y, :, at], grad_out[:, at]
                probs = head_probs(query, keys, scalar_ref[0], scalar_ref[1 + y], rows)
                grad_probs = dot(upstream, values, 1, 1)
                values_grad = values_grad + dot(probs.astype(BF), upstream, 0, 0)
                inner = jnp.sum(probs * grad_probs, axis=-1, keepdims=True)
                grad_scores = (probs * (grad_probs - inner)).astype(BF)
                parts.append(turn(dot(grad_scores, keys, 1, 0) * scale, cosine, sine))
                keys_grad = keys_grad + dot(grad_scores, query, 0, 0)
            parts.extend((turn(keys_grad * scale, cosine, sine), values_grad))
        grad_proj = jnp.concatenate([part.astype(BF) for part in parts], axis=1)
        grad_ref[y] = grad_proj
        put_blocks(dot(grad_proj, w_ref[:, : groups * span], 1, 1), y, cols // 2, keep_ref, send_ref)


def attend_back(pieces, scalars, cosine, sine, weights, saved, groups, order):
    count = len(pieces)
    rows, width = pieces[0].shape
    places = count // 2 * rows
    span = groups * (QUERY_PER_GROUP + 2) * HEAD_SIZE
    outs = [(count // 2, rows, width)] * 2 + [(2, places, span)]
    return order.call(
        lambda *refs: attend_back_kernel(count, groups, *refs),
        (1,),
        [SCALARS] + [whole(item.shape) for item in (*pieces, cosine, sine, weights, *saved)],
        [whole(shape) for shape in outs],
        [jax.ShapeDtypeStruct(shape, BF) for shape in outs],
        flops=4 * places * weights.size + 48 * places * places * groups * HEAD_SIZE,
        moved=8 * places * width + 2 * weights.size,
        args=(scalars, *pieces, cosine, sine, weights, *saved,),
    )


def units_kernel(count, cut, *refs):
    rows_refs, piece_refs = refs[:count], refs[count : 2 * count]
    w_ref, pair_ref, hidden_ref = refs[2 * count :]
    gate_up = dot(joined(rows_refs), w_ref[:, : 2 * cut], 1, 0)
    hidden_grad = dot(joined(piece_refs), w_ref[:, 2 * cut :], 1, 0)
    gate, up = gate_up[:, :cut], gate_up[:, cut:]
    sigma = 1.0 / (1.0 + jnp.exp(-gate))
    swish = gate * sigma
    hidden_ref[...] = (swish * up).astype(BF).reshape(hidden_ref.shape)
    pair_ref[..., :cut] = (
        (hidden_grad * up * sigma * (1.0 + gate * (1.0 - sigma))).astype(BF).reshape(hidden_ref.shape)
    )
    pair_ref[..., cut:] = (hidden_grad * swish).astype(BF).reshape(hidden_ref.shape)


def units(rows, pieces, weights, order):
    count = len(rows)
    places, width = rows[0].shape
    cut = weights.shape[1] // 3
    part = places // 4
    block = pl.BlockSpec((part, width), lambda l: (l, 0))
    return order.call(
        lambda *refs: units_kernel(count, cut, *refs),
        (4,),
        [block] * (2 * count) + [whole(weights.shape)],
        [pl.BlockSpec((count, part, size), lambda l: (0, l, 0)) for size in (2 * cut, cut)],
        [shaped(count, places, size) for size in (2 * cut, cut)],
        flops=2 * count * places * weights.size,
        moved=4 * count * places * width,
        args=(*rows, *pieces, weights),
    )


def grads_kernel(counts, *refs):
    grad_ref = refs[-1]
    size = grad_ref.shape[2]
    start = at = 0
    lefts = refs[sum(n for n, _ in counts) :]
    for n, k in counts:
        rows = joined(refs[start : start + n])
        left = jnp.concatenate([ref[...] for ref in lefts[:k]], axis=0)
        start, lefts = start + n, lefts[k:]
        product = dot(left, rows, 0, 0).astype(BF)
        for block in range(grad_ref.shape[0]):
            grad_ref[block, at : at + product.shape[0]] = product[:, block * size : (block + 1) * size]
        at += product.shape[0]


def weight_grads(products, owners, order, total=None, into=None):
    rows = [block for blocks, _ in products for block in blocks]
    lefts = [left for _, items in products for left in items]
    counts = [(len(blocks), len(items)) for blocks, items in products]
    places, width = rows[0].shape
    tile = width // 4
    part = sum(items[0].shape[1] for _, items in products)
    total = total or part
    at = 0 if into is None else total // part - 1
    tokens = len(products[0][0]) * places
    args = (*rows, *lefts) + (() if into is None else (into,))
    return order.call(
        lambda *refs: grads_kernel(counts, *refs),
        (4,),
        [pl.BlockSpec((places, tile), lambda t: (0, t))] * len(rows)
        + [whole(left.shape) for left in lefts]
        + [pl.BlockSpec(memory_space=pl.ANY)] * (into is not None),
        pl.BlockSpec((owners // 4, part, width // owners), lambda t: (t, at, 0)),
        shaped(owners, total, width // owners),
        flops=2 * tokens * part * width,
        moved=2 * len(products) * tokens * width,
        args=args,
        aliases={} if into is None else {len(args) - 1: 0},
    )


def back_kernel(count, lo, split, added, *refs):
    lefts, weights = refs[:count], refs[count : 2 * count]
    refs = refs[2 * count :]
    total = refs[0][...] if added else None
    refs = refs[1:] if added else refs
    for left, weight in zip(lefts, weights):
        value = left[...].reshape(-1, left.shape[-1])
        product = dot(value, weight[:, lo : lo + value.shape[1]], 1, 1)
        total = product if total is None else total + product
    if split:
        put_blocks(total, 0, refs[0].shape[0], *refs)
    else:
        refs[0][...] = total


def back(lefts, weights, lo, order, before=None, stream=None):
    count, places, depth = lefts[0].shape
    width = weights[0].shape[0]
    added, split = before is not None, stream is not None
    first = 2 * stream if split else 0
    half = pl.BlockSpec((2, places, width), lambda t: (t, 0, 0))
    flat = pl.BlockSpec((4 * places, width), lambda t: (first + t, 0))
    halves = shaped(4, places, width)
    steps = 2 if split else count // 4
    return order.call(
        lambda *refs: back_kernel(len(lefts), lo, split, added, *refs),
        (steps,),
        [pl.BlockSpec((4, places, depth), lambda t: (first + t, 0, 0))] * len(lefts)
        + [whole(weights[0].shape)] * len(weights)
        + ([flat] if added else []),
        [half, half] if split else flat,
        [halves, halves] if split else shaped(count * places, width, dtype=F32),
        flops=8 * steps * places * depth * width * len(lefts),
        moved=16 * steps * places * width,
        args=(*lefts, *weights, *((before,) if added else ())),
    )


def finish_ffn_kernel(count, cut, low_ref, *refs):
    pairs, cames = refs[:count], refs[count : 2 * count]
    w1_ref, w3_ref, gain_ref, grad1_ref, grad3_ref, grad2_ref, sum_ref = refs[2 * count :]
    units = w1_ref.shape[1] // 2
    gain, total = gain_ref[...], 0.0
    for chunk in range(count):
        for part, value in (
            (low_ref[0], pairs[chunk][low_ref[0]]),
            (1 - low_ref[0], cames[chunk][...]),
        ):
            place = pl.ds(pl.multiple_of(part * units + chunk * cut, cut), cut)
            value = value.astype(F32)
            first, second = value[:cut].T, value[cut : 2 * cut].T
            grad2_ref[place, :] = value[2 * cut :]
            grad1_ref[:, place] = first * gain
            grad3_ref[:, place] = second * gain
            product = first * w1_ref[:, place].astype(F32) + second * w3_ref[:, place].astype(F32)
            total = total + jnp.sum(product, axis=1, keepdims=True)
    sum_ref[...] = as_row(total)


def as_row(column):
    return jnp.broadcast_to(column, (column.shape[0], 128)).T[:1]


def finish_ffn(low, parts, w1, w3, w2, gain, order):
    count = len(parts)
    args = [pair for pair, _ in parts] + [came for _, came in parts] + [w1, w3, gain]
    outs = [shaped(*shape, dtype=F32) for shape in (w1.shape, w3.shape, w2.shape, gain.shape[::-1])]
    return order.call(
        lambda *refs: finish_ffn_kernel(count, parts[0][1].shape[0] // 3, *refs),
        (1,),
        [SCALARS] + [whole(item.shape) for item in args],
        [whole(item.shape) for item in outs],
        outs,
        (low, *args),
        moved=24 * w1.size,
    )


def finish_attn_kernel(low_ref, pair_ref, came_ref, w_ref, gain_ref, grad_ref, out_ref, sum_ref):
    wide = w_ref.shape[1] // 2
    tall = out_ref.shape[0] // 2
    gain, total = gain_ref[...], 0.0
    for part, value in ((low_ref[0], pair_ref[low_ref[0]]), (1 - low_ref[0], came_ref[...])):
        columns = pl.ds(pl.multiple_of(part * wide, wide), wide)
        value = value.astype(F32)
        first = value[:wide].T
        grad_ref[:, columns] = first * gain
        out_ref[pl.ds(pl.multiple_of(part * tall, tall), tall), :] = value[wide:]
        total = total + jnp.sum(first * w_ref[:, columns].astype(F32), axis=1, keepdims=True)
    sum_ref[...] = as_row(total)


def finish_attn(low, part, wqkv, wo, gain, order):
    args = [*part, wqkv, gain]
    outs = [shaped(*shape, dtype=F32) for shape in (wqkv.shape, wo.shape, gain.shape[::-1])]
    return order.call(
        finish_attn_kernel,
        (1,),
        [SCALARS] + [whole(item.shape) for item in args],
        [whole(item.shape) for item in outs],
        outs,
        (low, *args),
        moved=12 * wqkv.size,
    )


def body(inputs, lengths, wqkv, wo, w1, w3, w2, attn_gain, ffn_gain, cotangent):
    micro, _, rows, width = inputs.shape
    cols = lax.axis_size("col")
    places = cols * rows
    me = lax.axis_index("col")
    groups = wqkv.shape[1] // ((QUERY_PER_GROUP + 2) * HEAD_SIZE) // 2
    cut = w1.shape[1] // 2 // CHUNKS
    d = wqkv.shape[0]
    owners = width // d
    streams = range(micro)
    inputs, cotangent = inputs[:, 0], cotangent[:, 0]
    order = Order()
    low = (lax.axis_index("dp") % 2).astype(jnp.int32)[None]
    attn_gain, ffn_gain = attn_gain.astype(F32)[:, None], ffn_gain.astype(F32)[:, None]

    def prepared(*chunks):
        return prepare_ffn(chunks, cut, low, w1, w3, w2, ffn_gain, order)

    mine, sent = prepare_attn(low, wqkv, wo, attn_gain, order)
    normed1 = first_norm(inputs, order)
    attn_w = gather_weight(mine, sent, low, order)
    attn_rows = cross(fenced(start_gather(normed1), order))
    ffn_parts = prepared(0)
    attn_rows = both_cores(fenced(attn_rows, order))
    own_scalars = jnp.concatenate(((me * rows).astype(jnp.int32)[None], lengths.reshape(micro)))
    upstream = masked(cotangent, own_scalars, order)
    pieces = start_gather(upstream)
    ffn_ws = [gather_weight(*ffn_parts[0], low, order)]

    positions = (
        (jnp.arange(cols, dtype=jnp.int32) ^ me)[:, None] * rows
        + jnp.arange(rows, dtype=jnp.int32)[None, :]
    ).reshape(places)
    cosine, sine = rope_tables(positions)
    other_lengths = xchg(lengths, "dp", 1)
    scalars = [
        jnp.concatenate((me.astype(jnp.int32)[None], lengths[m], other_lengths[m])) for m in streams
    ]

    def run_attend(m):
        return attend(attn_rows[m], scalars[m], cosine, sine, attn_w, groups, order)

    ahead = [run_attend(0)]
    pieces = end_gather(fenced(pieces, order))
    ahead.append(run_attend(1))
    order.wait(*sum(pieces, []))
    halves = [item[:2] for item in ahead]
    terms = scatter_first(halves, scatter_core(halves), order)
    ffn_parts += prepared(1)
    terms = scatter_second(terms, order)
    normed2, residual = second_norm(inputs, terms, order)
    ffn_rows = start_gather(normed2)
    ffn_ws += [gather_weight(*ffn_parts[1], low, order)]
    ffn_rows = end_gather(ffn_rows)
    all_rows, all_pieces = sum(ffn_rows, []), sum(pieces, [])

    pairs, hiddens = [], []

    def run_units(chunk):
        pair, hidden = units(all_rows, all_pieces, ffn_ws[chunk], order)
        pairs.append(pair)
        hiddens.append(hidden)

    def pair_grads(chunk):
        left = pairs[chunk].reshape(-1, 2 * cut)
        return weight_grads([(all_rows, [left])], owners, order, total=3 * cut)

    def hidden_grads(chunk, into):
        left = hiddens[chunk].reshape(-1, cut)
        return weight_grads([(all_pieces, [left])], owners, order, total=3 * cut, into=into)

    run_units(0)
    ffn_grads = [scatter_weight(hidden_grads(0, pair_grads(0)))]
    early = back(pairs, ffn_ws[:1], 0, order)
    run_units(1)
    halves = [
        back(pairs[1:], ffn_ws[1:], 0, order, before=early, stream=m) for m in streams
    ]
    terms = scatter_first(halves, scatter_core(halves), order)
    part = pair_grads(1)
    terms = scatter_second(terms, order)
    ffn_grads.append(scatter_weight(hidden_grads(1, part)))
    attn_up, residual_grad = second_norm_back(residual, upstream, terms, order)
    attn_pieces = start_gather(attn_up)
    halves = [back(hiddens, ffn_ws, 2 * cut, order, stream=0)]
    attn_pieces = end_gather(fenced(attn_pieces, order))
    halves.append(back(hiddens, ffn_ws, 2 * cut, order, stream=1))
    terms = scatter_first(halves, scatter_core(halves), order)

    keep, send, grad_proj = zip(
        *[
            attend_back(attn_pieces[m], scalars[m], cosine, sine, attn_w, ahead[m][2:5], groups, order)
            for m in streams
        ]
    )
    halves = list(zip(keep, send))
    came = scatter_core(halves)
    order.wait(ffn_grads[0][1])
    attn_grads = weight_grads(
        [
            (sum(attn_rows, []), [grad_proj[m].reshape(2 * places, -1) for m in streams]),
            (sum(attn_pieces, []), [ahead[m][5].reshape(2 * places, -1) for m in streams]),
        ],
        owners,
        order,
    )
    chain = Chain(attn_grads)
    last_terms = scatter_first(halves, came, order)
    chain.advance(order)
    terms = scatter_second(terms, order)
    last_terms = scatter_second(last_terms, order)
    chain.advance(order)
    order.wait(ffn_grads[1][1])
    result = finished(residual, terms, order)
    source_grad = first_norm_back(inputs, residual_grad, last_terms, order)
    attn_part = chain.advance(order)
    w1_grad, w3_grad, w2_grad, ffn_sum = finish_ffn(low, ffn_grads, w1, w3, w2, ffn_gain, order)
    ffn_sum = sum_over_col(ffn_sum)[0]
    wqkv_grad, wo_grad, attn_sum = finish_attn(low, attn_part, wqkv, wo, attn_gain, order)
    attn_sum = sum_over_col(attn_sum)[0]
    return (
        result[:, None],
        source_grad[:, None],
        attn_sum,
        ffn_sum,
        wqkv_grad,
        wo_grad,
        w1_grad,
        w3_grad,
        w2_grad,
    )


def solution(mesh):
    tokens = P(None, ("dp", "row"), "col", None)
    in_specs = (
        tokens,
        P(None, ("dp", "row")),
        P(("dp", "row"), "col"),
        P("col", ("dp", "row")),
        P(("dp", "row"), "col"),
        P(("dp", "row"), "col"),
        P("col", ("dp", "row")),
        P(("dp", "row")),
        P(("dp", "row")),
        tokens,
    )
    out_specs = (
        tokens,
        tokens,
        P(("dp", "row")),
        P(("dp", "row")),
        P(("dp", "row"), "col"),
        P("col", ("dp", "row")),
        P(("dp", "row"), "col"),
        P(("dp", "row"), "col"),
        P("col", ("dp", "row")),
    )
    return jax.shard_map(body, mesh=mesh, in_specs=in_specs, out_specs=out_specs, check_vma=False)
```

```python
import jax
import jax.numpy as jnp
from jax import lax
from jax.experimental import pallas as pl
from jax.experimental.pallas import tpu as pltpu
from jax.sharding import PartitionSpec as P

HEAD_SIZE = 128
QUERY_PER_GROUP = 2
EPS = 1e-05
THETA = 1000000.0
NEGATIVE = -1e30
CHUNKS = 2
LARGE = int(63.5 * 2**20)
SMALL = int(63.5 * 2**20)
BF = jnp.bfloat16
F32 = jnp.float32


def xchg(value, axis, bit):
    size = lax.axis_size(axis)
    return lax.ppermute(value, axis, [(i, i ^ bit) for i in range(size)])


def dot(left, right, left_dim, right_dim):
    return lax.dot_general(
        left, right, (((left_dim,), (right_dim,)), ((), ())), preferred_element_type=F32
    )


def add(left, right):
    return left.astype(F32) + right.astype(F32)


class Gather:
    def __init__(self, own, rows, shared):
        self.own, self.rows, self.shared = own, rows, shared
        self.came = [xchg(own, "col", 2), xchg(own, "dp", 1), xchg(own, "col", 1)]

    def cross(self, order):
        over_x, over_y, core = order.fence(*self.came)
        if self.shared:
            first, second = halved(over_y, over_x, order)
            diagonal = [xchg(first, "col", 2), xchg(second, "dp", 1)]
        else:
            diagonal = [xchg(over_y, "col", 2)]
        self.arrays = [self.own, core, over_x, over_y]
        self.came = [xchg(over_x, "col", 1), xchg(over_y, "col", 1)] + diagonal

    def fence(self, order, *others):
        values = order.fence(*self.came, *others)
        self.came = values[: len(self.came)]
        return values[len(self.came) :]

    def blocks(self, order, *others):
        own, core, over_x, over_y = self.arrays
        core_x, core_y, *diagonal = self.came
        values = order.fence(*[xchg(item, "col", 1) for item in diagonal], *others)
        other, others = values[: len(diagonal)], values[len(diagonal) :]
        each = self.own.shape[0] // self.rows // len(diagonal)
        streams = []
        for m in range(each * len(diagonal)):
            found = [(item, m) for item in (own, core, over_x, core_x, over_y, core_y)]
            which, place = divmod(m, each)
            streams.append(found + [(diagonal[which], place), (other[which], place)])
        return (streams, *others)


class Scatter:
    def __init__(self, *payloads):
        shape = (2, 2) + payloads[0][0][0].shape[1:]
        self.parts = [
            [[keep.reshape(shape), came.reshape(shape)] for keep, came in parts]
            for parts in payloads
        ]
        self.came = [[], []]

    def send(self, picks, axes, order):
        count = len(self.parts)
        sums = [
            [(item, *pick) for item in parts[m]]
            + [(item, (1, *pick[0]), (p, *pick[1])) for item in self.came[m]]
            for m, pick in enumerate(picks)
            for p, parts in enumerate(self.parts)
        ]
        sent = folded([sums[:count], sums[count:]], order)
        for m, (axis, bit) in enumerate(axes):
            self.came[m].append(xchg(sent[m], axis, bit))

    def first(self, order):
        self.send((((2, 1), (0, 1)), ((1, 2), (1, 0))), (("col", 2), ("dp", 1)), order)

    def second(self, order):
        self.send((((1, 1), (1, 0)), ((1, 1), (0, 1))), (("dp", 1), ("col", 2)), order)

    def terms(self):
        return [
            [
                [(item, (1, 1), (0, 0)) for item in parts[m]]
                + [(item, (1, 1, 1), (p, 0, 0)) for item in self.came[m]]
                for m in range(2)
            ]
            for p, parts in enumerate(self.parts)
        ]


def dp_groups():
    size = lax.axis_size("dp")
    return [[i for i in range(size) if i % 2 == low] for low in (0, 1)]


def gather_weight(mine, came, low, order):
    pair = paired(mine, came, low, order)
    full = lax.all_gather(pair, "row", axis=1, tiled=True)
    if lax.axis_size("dp") > 2:
        full = lax.all_gather(full, "dp", axis=0, tiled=True, axis_index_groups=dp_groups())
    return full.reshape(-1, full.shape[-1])


def start_scatter(grad):
    size, rows = lax.axis_size("dp"), lax.axis_size("row")
    grad = grad.reshape((size, rows) + grad.shape[1:])
    if size > 2:
        grad = lax.psum_scatter(
            grad, "dp", scatter_dimension=0, tiled=True, axis_index_groups=dp_groups()
        )
    return grad


def end_scatter(pair):
    sent = lax.dynamic_index_in_dim(pair, 1 - lax.axis_index("dp") % 2, 0, keepdims=False)
    return pair, xchg(sent, "dp", 1)


def scatter_weight(grad):
    grad = start_scatter(grad)
    grad = grad.reshape(2, -1, grad.shape[-1])
    return end_scatter(lax.psum_scatter(grad, "row", scatter_dimension=1, tiled=True))


class Chain:
    def __init__(self, grad):
        self.grad = start_scatter(grad)
        self.rows = lax.axis_size("row")
        self.step = 1
        self.came = ()
        far = self.rows - 1
        self.send(self.block(far), self.block(-far))

    def place(self, offset):
        return jnp.clip(lax.axis_index("row") + offset, 0, self.rows - 1).astype(jnp.int32)

    def block(self, offset):
        return lax.dynamic_index_in_dim(self.grad, self.place(offset), 1, keepdims=False)

    def send(self, up, down):
        far = self.rows - self.step
        self.came = (
            lax.ppermute(up, "row", [(i, i + 1) for i in range(self.step)]),
            lax.ppermute(down, "row", [(i, i - 1) for i in range(far, self.rows)]),
        )

    def advance(self, order):
        self.step += 1
        far = self.rows - self.step
        places = jnp.stack((self.place(far), self.place(-far)))
        _, _, n, d = self.grad.shape
        part = pl.BlockSpec((1, n, d), lambda p, at: (p, 0, 0))

        def picked(which):
            return pl.BlockSpec((1, 1, n, d), lambda p, at: (p, at[which], 0, 0))

        def kernel(at_ref, up_ref, down_ref, first_ref, second_ref, *out_refs):
            if far:
                out_refs[0][...] = add(first_ref[0], up_ref[...]).astype(BF)
                out_refs[1][...] = add(second_ref[0], down_ref[...]).astype(BF)
            else:
                out_refs[0][...] = (add(first_ref[0], up_ref[...]) + down_ref[...].astype(F32)).astype(BF)

        count = 2 if far else 1
        outs = order.call(
            "advance",
            kernel,
            (2,),
            [part, part, picked(0), picked(1)],
            [part] * count,
            [shaped(2, n, d)] * count,
            (places, *self.came, self.grad, self.grad),
            prefetch=1,
            moved=24 * n * d,
        )
        if far:
            self.send(*outs)
            return None
        return end_scatter(outs[0])


def sum_over_col(value):
    return sum([xchg(value, "col", mask) for mask in range(1, lax.axis_size("col"))], value)


def rope_tables(positions):
    freqs = THETA ** (-jnp.arange(HEAD_SIZE // 2, dtype=F32) * 2.0 / HEAD_SIZE)
    angles = positions.astype(F32)[:, None] * freqs[None, :]
    cosine, sine = jnp.cos(angles), jnp.sin(angles)
    return jnp.concatenate((cosine, cosine), axis=1), jnp.concatenate((-sine, sine), axis=1)


class Order:
    def __init__(self):
        self.last = ()

    def wait(self, *values):
        self.last = self.last + values

    def fence(self, *values):
        return self.call(
            "fence",
            lambda *refs: None,
            (1,),
            [pl.BlockSpec(memory_space=pl.ANY)] * len(values),
            [pl.BlockSpec(memory_space=pl.ANY)] * len(values),
            [shaped(*value.shape, dtype=value.dtype) for value in values],
            values,
            aliases={i: i for i in range(len(values))},
        )

    def call(
        self, name, kernel, grid, in_specs, out_specs, out_shape, args, scratch=(), flops=0, moved=0, prefetch=0, aliases=None, large=False
    ):
        last = [token for token in self.last if all(token is not arg for arg in args)]
        tokens = len(last)
        count = len(args)

        def run(*refs):
            kernel(*refs[:count], *refs[count + tokens :])

        outs = pl.pallas_call(
            run,
            grid_spec=pltpu.PrefetchScalarGridSpec(
                num_scalar_prefetch=prefetch,
                grid=grid,
                in_specs=list(in_specs) + [pl.BlockSpec(memory_space=pl.ANY)] * tokens,
                out_specs=out_specs,
                scratch_shapes=list(scratch),
            ),
            out_shape=out_shape,
            name=name,
            input_output_aliases=aliases or {},
            compiler_params=pltpu.CompilerParams(vmem_limit_bytes=LARGE if large else SMALL),
            cost_estimate=pl.CostEstimate(flops=flops, bytes_accessed=moved, transcendentals=0),
        )(*args, *last)
        self.last = (outs[0] if isinstance(outs, (list, tuple)) else outs,)
        return outs


def shaped(*shape, dtype=BF):
    return jax.ShapeDtypeStruct(shape, dtype)


def block_spec(block, shape, index):
    _, place = block
    return pl.BlockSpec(shape, lambda *at: (place * index(*at)[1] + index(*at)[0], index(*at)[2]))


def arrays(blocks):
    return [item for item, _ in blocks]


def whole(shape):
    return pl.BlockSpec(shape, lambda *_: (0,) * len(shape))


SCALARS = pl.BlockSpec(memory_space=pltpu.SMEM)


def prepare_attn_kernel(low_ref, qkv_ref, out_ref, gain_ref, mine_ref, sent_ref):
    wide = qkv_ref.shape[1] // 2
    tall = out_ref.shape[0] // 2
    for part, ref in ((low_ref[0], mine_ref), (1 - low_ref[0], sent_ref)):
        columns = qkv_ref[:, pl.ds(pl.multiple_of(part * wide, wide), wide)]
        ref[:, :wide] = (columns.astype(F32) * gain_ref[...]).astype(BF)
        ref[:, wide:] = out_ref[pl.ds(pl.multiple_of(part * tall, tall), tall), :].T


def prepare_attn(low, wqkv, wo, gain, order):
    d = wqkv.shape[0]
    out = shaped(d, wqkv.shape[1] // 2 + wo.shape[0] // 2)
    return order.call(
        "prepare_attn",
        prepare_attn_kernel,
        (1,),
        [SCALARS] + [whole(item.shape) for item in (wqkv, wo, gain)],
        [whole(out.shape)] * 2,
        [out, out],
        (low, wqkv, wo, gain),
        moved=4 * (wqkv.size + wo.size),
    )


def prepare_ffn_kernel(chunks, cut, low_ref, w1_ref, w3_ref, w2_ref, gain_ref, *refs):
    units = w1_ref.shape[1] // 2
    gain = gain_ref[...]
    for at, chunk in enumerate(chunks):
        for part, ref in ((low_ref[0], refs[2 * at]), (1 - low_ref[0], refs[2 * at + 1])):
            place = pl.ds(pl.multiple_of(part * units + chunk * cut, cut), cut)
            ref[:, :cut] = (w1_ref[:, place].astype(F32) * gain).astype(BF)
            ref[:, cut : 2 * cut] = (w3_ref[:, place].astype(F32) * gain).astype(BF)
            ref[:, 2 * cut :] = w2_ref[place, :].T


def prepare_ffn(chunks, cut, low, w1, w3, w2, gain, order):
    out = shaped(w1.shape[0], 3 * cut)
    outs = order.call(
        "prepare_ffn",
        lambda *refs: prepare_ffn_kernel(chunks, cut, *refs),
        (1,),
        [SCALARS] + [whole(item.shape) for item in (w1, w3, w2, gain)],
        [whole(out.shape)] * (2 * len(chunks)),
        [out] * (2 * len(chunks)),
        (low, w1, w3, w2, gain),
        moved=12 * w1.size,
    )
    return [(outs[2 * i], outs[2 * i + 1]) for i in range(len(chunks))]


def paired_kernel(low_ref, mine_ref, came_ref, out_ref):
    out_ref[pl.ds(low_ref[0], 1)] = mine_ref[...][None]
    out_ref[pl.ds(1 - low_ref[0], 1)] = came_ref[...][None]


def paired(mine, came, low, order):
    out = shaped(2, *mine.shape)
    return order.call(
        "paired",
        paired_kernel,
        (1,),
        [SCALARS, whole(mine.shape), whole(mine.shape)],
        whole(out.shape),
        out,
        (low, mine, came),
        moved=8 * mine.size,
    )


def inverse_rms(values):
    return lax.rsqrt(jnp.mean(values * values, axis=-1, keepdims=True) + EPS)


def by_rows(kernel, ins, outs, order, scalars=None, steps=4):
    def spec(item):
        item, lead, at = item if isinstance(item, tuple) else (item, item.shape[:-2], None)
        at = at or (0,) * len(lead)
        return pl.BlockSpec(lead + (item.shape[-2] // steps, item.shape[-1]), lambda l: at + (l, 0))

    extra = [] if scalars is None else [scalars]
    args = [item[0] if isinstance(item, tuple) else item for item in ins]
    return order.call(
        "by_rows",
        kernel,
        (steps,),
        [SCALARS] * len(extra) + [spec(item) for item in ins],
        [spec(item) for item in outs],
        outs,
        (*extra, *args),
        moved=4 * sum(item.size for item in (*args, *outs)),
    )


def first_norm(inputs, order):
    def kernel(in_ref, out_ref):
        values = in_ref[...].astype(F32)
        out_ref[...] = (values * inverse_rms(values)).astype(BF)

    return by_rows(kernel, [inputs], [shaped(*inputs.shape)], order)[0]


def halved(first, second, order):
    half, width = first.shape[0] // 2, first.shape[1]

    def kernel(*refs):
        for ref, out_ref in zip(refs[:2], refs[2:]):
            out_ref[...] = ref[...]

    part = (half // 4, width)
    out = pl.BlockSpec(part, lambda l: (l, 0))
    return order.call(
        "halved",
        kernel,
        (4,),
        [out, pl.BlockSpec(part, lambda l: (4 + l, 0))],
        [out] * 2,
        [shaped(half, width)] * 2,
        (first, second),
        moved=8 * half * width,
    )


def total_of(refs):
    values = [ref[...].astype(F32) for ref in refs]
    return sum(value.reshape(value.shape[-2:]) for value in values)


def folded(groups, order):
    counts = [[len(items) for items in lists] for lists in groups]
    total = sum(sum(sizes) for sizes in counts)

    def kernel(*refs):
        start = 0
        for out_ref, sizes in zip(refs[total:], counts):
            for p, size in enumerate(sizes):
                values = [ref[...].astype(F32) for ref in refs[start : start + size]]
                shape = out_ref.shape[1:]
                out_ref[p] = sum(value.reshape(shape) for value in values).astype(BF)
                start += size

    outs = [shaped(len(lists), *lists[0][0][1], *lists[0][0][0].shape[-2:]) for lists in groups]
    ins = [item for lists in groups for items in lists for item in items]
    return by_rows(kernel, ins, outs, order, steps=2)


def with_terms(kernel, ins, outs, terms, order):
    count = len(ins)
    sizes = [len(items) for items in terms]

    def run(*refs):
        start = count
        for m, size in enumerate(sizes):
            total = total_of(refs[start : start + size])
            kernel(m, total, refs[:count], refs[count + sum(sizes) :])
            start += size

    return by_rows(run, [*ins, *[item for items in terms for item in items]], outs, order)


def second_norm(inputs, terms, cotangent, scalars, order):
    micro = inputs.shape[0]
    count = sum(len(items) for items in terms)

    def kernel(scalar_ref, in_ref, cot_ref, *refs):
        out_ref, residual_ref = refs[count:]
        start = 0
        for m, items in enumerate(terms):
            values = in_ref[m].astype(F32) + total_of(refs[start : start + len(items)])
            start += len(items)
            residual_ref[m] = values
            out_ref[m] = (values * inverse_rms(values)).astype(BF)
            first = scalar_ref[0] + pl.program_id(0) * in_ref.shape[1]
            places = first + lax.broadcasted_iota(jnp.int32, in_ref.shape[1:], 0)
            valid = places < scalar_ref[1 + m]
            out_ref[micro + m] = jnp.where(valid, cot_ref[m].astype(F32), 0.0).astype(BF)

    outs = [shaped(2 * micro, *inputs.shape[1:]), shaped(*inputs.shape, dtype=F32)]
    ins = [inputs, cotangent, *[item for items in terms for item in items]]
    return by_rows(kernel, ins, outs, order, scalars)


def norm_back(values, scaled):
    inverse = inverse_rms(values)
    inner = jnp.mean(scaled * values, axis=-1, keepdims=True)
    return inverse * scaled - values * (inverse * inverse * inverse) * inner


def second_norm_back(residual, upstream, terms, order):
    def kernel(m, total, ins, outs):
        grad = ins[1][m].astype(F32) + norm_back(ins[0][m], total)
        outs[0][m] = grad.astype(BF)
        outs[1][m] = grad

    outs = [shaped(*residual.shape), shaped(*residual.shape, dtype=F32)]
    return with_terms(kernel, [residual, upstream], outs, terms, order)


def finished(inputs, upstream, residual, terms, order):
    micro = inputs.shape[0]
    sizes = [[len(items) for items in payload] for payload in terms]

    def kernel(in_ref, up_ref, residual_ref, *refs):
        grad_ref, out_ref = refs[-2:]
        start = 0
        for m in range(micro):
            total = total_of(refs[start : start + sizes[0][m]])
            start += sizes[0][m]
            grad_ref[m] = (up_ref[m] + norm_back(in_ref[m].astype(F32), total)).astype(BF)
        for m in range(micro):
            total = total_of(refs[start : start + sizes[1][m]])
            start += sizes[1][m]
            out_ref[m] = (residual_ref[m] + total).astype(BF)

    ins = [inputs, upstream, residual] + [item for payload in terms for items in payload for item in items]
    return by_rows(kernel, ins, [shaped(*inputs.shape)] * 2, order)


def head_probs(query, keys, me, length, rows):
    places = query.shape[0]
    scores = dot(query, keys, 1, 1) * HEAD_SIZE ** (-0.5)
    queried = lax.broadcasted_iota(jnp.int32, (places, places), 0)
    keyed = lax.broadcasted_iota(jnp.int32, (places, places), 1)
    queried = ((queried // rows) ^ me) * rows + queried % rows
    keyed = ((keyed // rows) ^ me) * rows + keyed % rows
    scores = jnp.where((keyed <= queried) & (keyed < length), scores, NEGATIVE)
    expo = jnp.exp(scores - jnp.max(scores, axis=-1, keepdims=True))
    return expo * (1.0 / jnp.sum(expo, axis=-1, keepdims=True))


def turn(values, cosine, sine):
    return values * cosine + pltpu.roll(values, HEAD_SIZE // 2, 1) * sine


def joined(refs):
    return jnp.concatenate([ref[...] for ref in refs], axis=0)


def put_blocks(value, y, pairs, keep_ref, send_ref):
    rows = keep_ref.shape[1]
    for x in range(pairs):
        start = 2 * x * rows
        keep_ref[y * pairs + x] = value[start : start + rows].astype(BF)
        send_ref[y * pairs + x] = value[start + rows : start + 2 * rows].astype(BF)


def head_at(index):
    return slice(index * HEAD_SIZE, (index + 1) * HEAD_SIZE)


def attend_kernel(count, groups, scalar_ref, *refs):
    blocks = refs[:count]
    cos_ref, sin_ref, w_ref, keep_ref, send_ref, q_ref, k_ref, v_ref, a_ref = refs[count:]
    rows = blocks[0].shape[0]
    cols = count // 2
    span = (QUERY_PER_GROUP + 2) * HEAD_SIZE
    cosine, sine = cos_ref[...], sin_ref[...]
    for y in (0, 1):
        projected = dot(joined(blocks[y * cols : (y + 1) * cols]), w_ref[:, : groups * span], 1, 0)
        for g in range(groups):
            part = projected[:, g * span : (g + 1) * span]
            keys = turn(part[:, -2 * HEAD_SIZE : -HEAD_SIZE], cosine, sine).astype(BF)
            values = part[:, -HEAD_SIZE:].astype(BF)
            k_ref[y, :, head_at(g)] = keys
            v_ref[y, :, head_at(g)] = values
            for r in range(QUERY_PER_GROUP):
                query = turn(part[:, head_at(r)], cosine, sine).astype(BF)
                probs = head_probs(query, keys, scalar_ref[0], scalar_ref[1 + y], rows).astype(BF)
                at = head_at(g * QUERY_PER_GROUP + r)
                q_ref[y, :, at] = query
                a_ref[y, :, at] = dot(probs, values, 1, 0).astype(BF)
        put_blocks(dot(a_ref[y], w_ref[:, groups * span :], 1, 1), y, cols // 2, keep_ref, send_ref)


def attend(blocks, rows, scalars, cosine, sine, weights, groups, order):
    count = len(blocks)
    width = blocks[0][0].shape[1]
    places = count // 2 * rows
    head = groups * HEAD_SIZE
    sizes = (QUERY_PER_GROUP * head, head, head, QUERY_PER_GROUP * head)
    outs = [(count // 2, rows, width)] * 2 + [(2, places, size) for size in sizes]
    return order.call(
        "attend",
        lambda *refs: attend_kernel(count, groups, *refs),
        (1,),
        [SCALARS]
        + [block_spec(block, (rows, width), lambda _: (0, 1, 0)) for block in blocks]
        + [whole(item.shape) for item in (cosine, sine, weights)],
        [whole(shape) for shape in outs],
        [jax.ShapeDtypeStruct(shape, BF) for shape in outs],
        flops=4 * places * weights.size + 16 * places * places * QUERY_PER_GROUP * head,
        moved=8 * places * width + 2 * weights.size,
        args=(scalars, *arrays(blocks), cosine, sine, weights),
        large=True,
    )


def attend_back_kernel(count, groups, scalar_ref, *refs):
    pieces = refs[:count]
    cos_ref, sin_ref, w_ref, q_ref, k_ref, v_ref, keep_ref, send_ref, grad_ref = refs[count:]
    rows = pieces[0].shape[0]
    cols = count // 2
    span = (QUERY_PER_GROUP + 2) * HEAD_SIZE
    scale = HEAD_SIZE ** (-0.5)
    cosine, sine = cos_ref[...], -sin_ref[...]
    for y in (0, 1):
        piece = joined(pieces[y * cols : (y + 1) * cols])
        grad_out = dot(piece, w_ref[:, groups * span :], 1, 0).astype(BF)
        parts = []
        for g in range(groups):
            keys, values = k_ref[y, :, head_at(g)], v_ref[y, :, head_at(g)]
            keys_grad, values_grad = 0.0, 0.0
            for r in range(QUERY_PER_GROUP):
                at = head_at(g * QUERY_PER_GROUP + r)
                query, upstream = q_ref[y, :, at], grad_out[:, at]
                probs = head_probs(query, keys, scalar_ref[0], scalar_ref[1 + y], rows)
                grad_probs = dot(upstream, values, 1, 1)
                values_grad = values_grad + dot(probs.astype(BF), upstream, 0, 0)
                inner = jnp.sum(probs * grad_probs, axis=-1, keepdims=True)
                grad_scores = (probs * (grad_probs - inner)).astype(BF)
                parts.append(turn(dot(grad_scores, keys, 1, 0) * scale, cosine, sine))
                keys_grad = keys_grad + dot(grad_scores, query, 0, 0)
            parts.extend((turn(keys_grad * scale, cosine, sine), values_grad))
        grad_proj = jnp.concatenate([part.astype(BF) for part in parts], axis=1)
        grad_ref[y] = grad_proj
        put_blocks(dot(grad_proj, w_ref[:, : groups * span], 1, 1), y, cols // 2, keep_ref, send_ref)


def attend_back(pieces, rows, scalars, cosine, sine, weights, saved, groups, order):
    count = len(pieces)
    width = pieces[0][0].shape[1]
    places = count // 2 * rows
    span = groups * (QUERY_PER_GROUP + 2) * HEAD_SIZE
    outs = [(count // 2, rows, width)] * 2 + [(2, places, span)]
    return order.call(
        "attend_back",
        lambda *refs: attend_back_kernel(count, groups, *refs),
        (1,),
        [SCALARS]
        + [block_spec(block, (rows, width), lambda _: (0, 1, 0)) for block in pieces]
        + [whole(item.shape) for item in (cosine, sine, weights, *saved)],
        [whole(shape) for shape in outs],
        [jax.ShapeDtypeStruct(shape, BF) for shape in outs],
        flops=4 * places * weights.size + 48 * places * places * groups * HEAD_SIZE,
        moved=8 * places * width + 2 * weights.size,
        args=(scalars, *arrays(pieces), cosine, sine, weights, *saved),
        large=True,
    )


def units_kernel(count, cut, *refs):
    rows_refs, piece_refs = refs[:count], refs[count : 2 * count]
    w_ref, pair_ref, hidden_ref = refs[2 * count :]
    gate_up = dot(joined(rows_refs), w_ref[:, : 2 * cut], 1, 0)
    hidden_grad = dot(joined(piece_refs), w_ref[:, 2 * cut :], 1, 0)
    gate, up = gate_up[:, :cut], gate_up[:, cut:]
    sigma = 1.0 / (1.0 + jnp.exp(-gate))
    swish = gate * sigma
    hidden_ref[...] = (swish * up).astype(BF).reshape(hidden_ref.shape)
    pair_ref[..., :cut] = (
        (hidden_grad * up * sigma * (1.0 + gate * (1.0 - sigma))).astype(BF).reshape(hidden_ref.shape)
    )
    pair_ref[..., cut:] = (hidden_grad * swish).astype(BF).reshape(hidden_ref.shape)


def units(rows, pieces, places, weights, order):
    count = len(rows)
    width = weights.shape[0]
    cut = weights.shape[1] // 3
    part = places // 4
    return order.call(
        "units",
        lambda *refs: units_kernel(count, cut, *refs),
        (4,),
        [block_spec(block, (part, width), lambda l: (l, 4, 0)) for block in (*rows, *pieces)]
        + [whole(weights.shape)],
        [pl.BlockSpec((count, part, size), lambda l: (0, l, 0)) for size in (2 * cut, cut)],
        [shaped(count, places, size) for size in (2 * cut, cut)],
        flops=2 * count * places * weights.size,
        moved=4 * count * places * width,
        args=(*arrays(rows), *arrays(pieces), weights),
        large=True,
    )


def grads_kernel(counts, *refs):
    grad_ref = refs[-1]
    size = grad_ref.shape[2]
    start = at = 0
    lefts = refs[sum(n for n, _ in counts) :]
    for n, k in counts:
        rows = joined(refs[start : start + n])
        left = jnp.concatenate([ref[...] for ref in lefts[:k]], axis=0)
        start, lefts = start + n, lefts[k:]
        product = dot(left, rows, 0, 0).astype(BF)
        for block in range(grad_ref.shape[0]):
            grad_ref[block, at : at + product.shape[0]] = product[:, block * size : (block + 1) * size]
        at += product.shape[0]


def weight_grads(products, places, owners, order, total=None, into=None):
    rows = [block for blocks, _ in products for block in blocks]
    lefts = [left for _, items in products for left in items]
    counts = [(len(blocks), len(items)) for blocks, items in products]
    width = rows[0][0].shape[1]
    tile = width // 4
    part = sum(items[0].shape[1] for _, items in products)
    total = total or part
    at = 0 if into is None else total // part - 1
    tokens = len(products[0][0]) * places
    args = (*arrays(rows), *lefts) + (() if into is None else (into,))
    return order.call(
        "weight_grads",
        lambda *refs: grads_kernel(counts, *refs),
        (4,),
        [block_spec(block, (places, tile), lambda t: (0, 1, t)) for block in rows]
        + [whole(left.shape) for left in lefts]
        + [pl.BlockSpec(memory_space=pl.ANY)] * (into is not None),
        pl.BlockSpec((owners // 4, part, width // owners), lambda t: (t, at, 0)),
        shaped(owners, total, width // owners),
        flops=2 * tokens * part * width,
        moved=2 * len(products) * tokens * width,
        args=args,
        aliases={} if into is None else {len(args) - 1: 0},
        large=True,
    )


def back_kernel(count, split, added, *refs):
    lefts, weights = refs[:count], refs[count : 2 * count]
    refs = refs[2 * count :]
    total = refs[0][...] if added else None
    refs = refs[1:] if added else refs
    for left, weight in zip(lefts, weights):
        product = dot(left[...].reshape(-1, left.shape[-1]), weight[...], 1, 1)
        total = product if total is None else total + product
    if split:
        put_blocks(total, 0, refs[0].shape[0], *refs)
    else:
        refs[0][...] = total


def back(lefts, weights, lo, order, before=None, stream=None):
    count, places, depth = lefts[0].shape
    width = weights[0].shape[0]
    added, split = before is not None, stream is not None
    first = 2 * stream if split else 0
    half = pl.BlockSpec((2, places, width), lambda t: (t, 0, 0))
    flat = pl.BlockSpec((4 * places, width), lambda t: (first + t, 0))
    halves = shaped(4, places, width)
    steps = 2 if split else count // 4
    return order.call(
        "back",
        lambda *refs: back_kernel(len(lefts), split, added, *refs),
        (steps,),
        [pl.BlockSpec((4, places, depth), lambda t: (first + t, 0, 0))] * len(lefts)
        + [pl.BlockSpec((width, depth), lambda t: (0, lo // depth))] * len(weights)
        + ([flat] if added else []),
        [half, half] if split else flat,
        [halves, halves] if split else shaped(count * places, width, dtype=F32),
        flops=8 * steps * places * depth * width * len(lefts),
        moved=16 * steps * places * width,
        args=(*lefts, *weights, *((before,) if added else ())),
        large=True,
    )


def finish_ffn_kernel(count, cut, low_ref, *refs):
    pairs, cames = refs[:count], refs[count : 2 * count]
    w1_ref, w3_ref, gain_ref, grad1_ref, grad3_ref, grad2_ref, sum_ref = refs[2 * count :]
    units = w1_ref.shape[1] // 2
    gain, total = gain_ref[...], 0.0
    for chunk in range(count):
        for part, value in (
            (low_ref[0], pairs[chunk][low_ref[0]]),
            (1 - low_ref[0], cames[chunk][...]),
        ):
            place = pl.ds(pl.multiple_of(part * units + chunk * cut, cut), cut)
            value = value.astype(F32)
            first, second = value[:cut].T, value[cut : 2 * cut].T
            grad2_ref[place, :] = value[2 * cut :]
            grad1_ref[:, place] = first * gain
            grad3_ref[:, place] = second * gain
            product = first * w1_ref[:, place].astype(F32) + second * w3_ref[:, place].astype(F32)
            total = total + jnp.sum(product, axis=1, keepdims=True)
    sum_ref[...] = as_row(total)


def as_row(column):
    return jnp.broadcast_to(column, (column.shape[0], 128)).T[:1]


def finish_ffn(low, parts, w1, w3, w2, gain, order):
    count = len(parts)
    args = [pair for pair, _ in parts] + [came for _, came in parts] + [w1, w3, gain]
    outs = [shaped(*shape, dtype=F32) for shape in (w1.shape, w3.shape, w2.shape, gain.shape[::-1])]
    return order.call(
        "finish_ffn",
        lambda *refs: finish_ffn_kernel(count, parts[0][1].shape[0] // 3, *refs),
        (1,),
        [SCALARS] + [whole(item.shape) for item in args],
        [whole(item.shape) for item in outs],
        outs,
        (low, *args),
        moved=24 * w1.size,
        large=True,
    )


def finish_attn_kernel(low_ref, pair_ref, came_ref, w_ref, gain_ref, grad_ref, out_ref, sum_ref):
    wide = w_ref.shape[1] // 2
    tall = out_ref.shape[0] // 2
    gain, total = gain_ref[...], 0.0
    for part, value in ((low_ref[0], pair_ref[low_ref[0]]), (1 - low_ref[0], came_ref[...])):
        columns = pl.ds(pl.multiple_of(part * wide, wide), wide)
        value = value.astype(F32)
        first = value[:wide].T
        grad_ref[:, columns] = first * gain
        out_ref[pl.ds(pl.multiple_of(part * tall, tall), tall), :] = value[wide:]
        total = total + jnp.sum(first * w_ref[:, columns].astype(F32), axis=1, keepdims=True)
    sum_ref[...] = as_row(total)


def finish_attn(low, part, wqkv, wo, gain, order):
    args = [*part, wqkv, gain]
    outs = [shaped(*shape, dtype=F32) for shape in (wqkv.shape, wo.shape, gain.shape[::-1])]
    return order.call(
        "finish_attn",
        finish_attn_kernel,
        (1,),
        [SCALARS] + [whole(item.shape) for item in args],
        [whole(item.shape) for item in outs],
        outs,
        (low, *args),
        moved=12 * wqkv.size,
    )


def body(inputs, lengths, wqkv, wo, w1, w3, w2, attn_gain, ffn_gain, cotangent):
    micro, _, rows, width = inputs.shape
    cols = lax.axis_size("col")
    places = cols * rows
    me = lax.axis_index("col")
    groups = wqkv.shape[1] // ((QUERY_PER_GROUP + 2) * HEAD_SIZE) // 2
    cut = w1.shape[1] // 2 // CHUNKS
    d = wqkv.shape[0]
    owners = width // d
    streams = range(micro)
    inputs, cotangent = inputs[:, 0], cotangent[:, 0]
    order = Order()
    low = (lax.axis_index("dp") % 2).astype(jnp.int32)[None]
    attn_gain, ffn_gain = attn_gain.astype(F32)[:, None], ffn_gain.astype(F32)[:, None]

    def prepared(*chunks):
        return prepare_ffn(chunks, cut, low, w1, w3, w2, ffn_gain, order)

    positions = (
        (jnp.arange(cols, dtype=jnp.int32) ^ me)[:, None] * rows
        + jnp.arange(rows, dtype=jnp.int32)[None, :]
    ).reshape(places)
    cosine, sine = rope_tables(positions)
    other_lengths = xchg(lengths, "dp", 1)
    scalars = [
        jnp.concatenate((me.astype(jnp.int32)[None], lengths[m], other_lengths[m])) for m in streams
    ]
    own_scalars = jnp.concatenate(((me * rows).astype(jnp.int32)[None], lengths.reshape(micro)))

    mine, sent = prepare_attn(low, wqkv, wo, attn_gain, order)
    normed1 = first_norm(inputs, order)
    attn_w = gather_weight(mine, xchg(sent, "dp", 1), low, order)
    attn_gather = Gather(normed1.reshape(-1, width), rows, False)
    attn_gather.cross(order)
    ((mine, sent),) = prepared(0)
    order.wait(cosine, sine, *scalars)
    (came,) = attn_gather.fence(order, xchg(sent, "dp", 1))
    ffn_ws = [gather_weight(mine, came, low, order)]
    (attn_rows,) = attn_gather.blocks(order)
    ((mine, sent),) = prepared(1)

    def run_attend(m):
        return attend(attn_rows[m], rows, scalars[m], cosine, sine, attn_w, groups, order)

    ahead = [run_attend(0), run_attend(1)]
    came, *sends = order.fence(xchg(sent, "dp", 1), *[item[1] for item in ahead])
    scatter = Scatter([(item[0], xchg(send, "col", 1)) for item, send in zip(ahead, sends)])
    ffn_ws.append(gather_weight(mine, came, low, order))
    scatter.first(order)
    scatter.second(order)
    normed2, residual = second_norm(inputs, scatter.terms()[0], cotangent, own_scalars, order)
    ffn_gather = Gather(normed2.reshape(-1, width), rows, True)
    ffn_gather.cross(order)
    ffn_gather.fence(order)
    (blocks,) = ffn_gather.blocks(order)
    all_rows, all_pieces = sum(blocks[:micro], []), sum(blocks[micro:], [])
    upstream = (normed2, (micro,), (1,))

    pairs, hiddens = [], []

    def run_units(chunk):
        pair, hidden = units(all_rows, all_pieces, rows, ffn_ws[chunk], order)
        pairs.append(pair)
        hiddens.append(hidden)

    def pair_grads(chunk):
        left = pairs[chunk].reshape(-1, 2 * cut)
        return weight_grads([(all_rows, [left])], rows, owners, order, total=3 * cut)

    def hidden_grads(chunk, into):
        left = hiddens[chunk].reshape(-1, cut)
        return weight_grads([(all_pieces, [left])], rows, owners, order, total=3 * cut, into=into)

    run_units(0)
    ffn_grads = [scatter_weight(hidden_grads(0, pair_grads(0)))]
    early = back(pairs, ffn_ws[:1], 0, order)
    run_units(1)
    halves = [
        back(pairs[1:], ffn_ws[1:], 0, order, before=early, stream=m) for m in streams
    ]
    scatter = Scatter([(keep, xchg(send, "col", 1)) for keep, send in halves])
    scatter.first(order)
    part = pair_grads(1)
    scatter.second(order)
    grads = hidden_grads(1, part)
    attn_up, residual_grad = second_norm_back(residual, upstream, scatter.terms()[0], order)
    attn_gather = Gather(attn_up.reshape(-1, width), rows, True)
    ffn_grads.append(scatter_weight(order.fence(grads)[0]))
    halves = [back(hiddens, ffn_ws, 2 * cut, order, stream=0)]
    attn_gather.cross(order)
    halves.append(back(hiddens, ffn_ws, 2 * cut, order, stream=1))
    attn_gather.fence(order)
    attn_pieces, *sends = attn_gather.blocks(order, *[send for _, send in halves])
    halves = [(keep, send) for (keep, _), send in zip(halves, sends)]

    def run_back(m):
        return attend_back(
            attn_pieces[m], rows, scalars[m], cosine, sine, attn_w, ahead[m][2:5], groups, order
        )

    def arrived(part):
        return part[0], order.fence(part[1])[0]

    out_sent = [(keep, xchg(send, "col", 1)) for keep, send in halves]
    behind = [run_back(0), run_back(1)]
    pair, came = ffn_grads[0]
    came, *values = order.fence(came, *[item for _, item in out_sent], *[item[1] for item in behind])
    ffn_grads[0] = (pair, came)
    out_parts = [(keep, item) for (keep, _), item in zip(out_sent, values)]
    attn_parts = [(item[0], xchg(send, "col", 1)) for item, send in zip(behind, values[micro:])]
    scatter = Scatter(attn_parts, out_parts)
    scatter.first(order)
    attn_grads = weight_grads(
        [
            (sum(attn_rows, []), [item[2].reshape(2 * places, -1) for item in behind]),
            (sum(attn_pieces, []), [item[5].reshape(2 * places, -1) for item in ahead]),
        ],
        rows,
        owners,
        order,
    )
    chain = Chain(attn_grads)
    chain.advance(order)
    scatter.second(order)
    chain.advance(order)
    ffn_grads[1] = arrived(ffn_grads[1])
    attn_part = chain.advance(order)
    source_grad, result = finished(inputs, residual_grad, residual, scatter.terms(), order)
    w1_grad, w3_grad, w2_grad, ffn_sum = finish_ffn(low, ffn_grads, w1, w3, w2, ffn_gain, order)
    ffn_sum = sum_over_col(ffn_sum)[0]
    wqkv_grad, wo_grad, attn_sum = finish_attn(low, attn_part, wqkv, wo, attn_gain, order)
    attn_sum = sum_over_col(attn_sum)[0]
    return (
        result[:, None],
        source_grad[:, None],
        attn_sum,
        ffn_sum,
        wqkv_grad,
        wo_grad,
        w1_grad,
        w3_grad,
        w2_grad,
    )


def solution(mesh):
    tokens = P(None, ("dp", "row"), "col", None)
    in_specs = (
        tokens,
        P(None, ("dp", "row")),
        P(("dp", "row"), "col"),
        P("col", ("dp", "row")),
        P(("dp", "row"), "col"),
        P(("dp", "row"), "col"),
        P("col", ("dp", "row")),
        P(("dp", "row")),
        P(("dp", "row")),
        tokens,
    )
    out_specs = (
        tokens,
        tokens,
        P(("dp", "row")),
        P(("dp", "row")),
        P(("dp", "row"), "col"),
        P("col", ("dp", "row")),
        P(("dp", "row"), "col"),
        P(("dp", "row"), "col"),
        P("col", ("dp", "row")),
    )
    return jax.shard_map(body, mesh=mesh, in_specs=in_specs, out_specs=out_specs, check_vma=False)
```

```python
import jax
import jax.numpy as jnp
from jax import lax
from jax.experimental import pallas as pl
from jax.experimental.pallas import tpu as pltpu
from jax.sharding import PartitionSpec as P

HEAD_SIZE = 128
QUERY_PER_GROUP = 2
EPS = 1e-05
THETA = 1000000.0
NEGATIVE = -1e30
CHUNKS = 2
VMEM = 127 * 2**19
BF = jnp.bfloat16
F32 = jnp.float32


def xchg(value, axis, bit):
    size = lax.axis_size(axis)
    return lax.ppermute(value, axis, [(i, i ^ bit) for i in range(size)])


def dot(left, right, left_dim, right_dim):
    return lax.dot_general(
        left, right, (((left_dim,), (right_dim,)), ((), ())), preferred_element_type=F32
    )


def add(left, right):
    return left.astype(F32) + right.astype(F32)


class Gather:
    def __init__(self, own, rows, shared):
        self.own, self.rows, self.shared = own, rows, shared
        self.came = [xchg(own, "col", 2), xchg(own, "dp", 1), xchg(own, "col", 1)]

    def cross(self, order):
        over_x, over_y, core = order.fence(*self.came)
        if self.shared:
            first, second = halved(over_y, over_x, order)
            diagonal = [xchg(first, "col", 2), xchg(second, "dp", 1)]
        else:
            diagonal = [xchg(over_y, "col", 2)]
        self.arrays = [self.own, core, over_x, over_y]
        self.came = [xchg(over_x, "col", 1), xchg(over_y, "col", 1)] + diagonal

    def fence(self, order, *others):
        values = order.fence(*self.came, *others)
        self.came = values[: len(self.came)]
        return values[len(self.came) :]

    def blocks(self, order, *others):
        own, core, over_x, over_y = self.arrays
        core_x, core_y, *diagonal = self.came
        values = order.fence(*[xchg(item, "col", 1) for item in diagonal], *others)
        other, others = values[: len(diagonal)], values[len(diagonal) :]
        each = self.own.shape[0] // self.rows // len(diagonal)
        streams = []
        for m in range(each * len(diagonal)):
            found = [(item, m) for item in (own, core, over_x, core_x, over_y, core_y)]
            which, place = divmod(m, each)
            streams.append(found + [(diagonal[which], place), (other[which], place)])
        return (streams, *others)


class Scatter:
    def __init__(self, *payloads):
        shape = (2, 2) + payloads[0][0][0].shape[1:]
        self.parts = [
            [[keep.reshape(shape), came.reshape(shape)] for keep, came in parts]
            for parts in payloads
        ]
        self.came = [[], []]

    def send(self, picks, axes, order):
        count = len(self.parts)
        sums = [
            [(item, *pick) for item in parts[m]]
            + [(item, (1, *pick[0]), (p, *pick[1])) for item in self.came[m]]
            for m, pick in enumerate(picks)
            for p, parts in enumerate(self.parts)
        ]
        sent = folded([sums[:count], sums[count:]], order)
        for m, (axis, bit) in enumerate(axes):
            self.came[m].append(xchg(sent[m], axis, bit))

    def first(self, order):
        self.send((((2, 1), (0, 1)), ((1, 2), (1, 0))), (("col", 2), ("dp", 1)), order)

    def second(self, order):
        self.send((((1, 1), (1, 0)), ((1, 1), (0, 1))), (("dp", 1), ("col", 2)), order)

    def terms(self):
        return [
            [
                [(item, (1, 1), (0, 0)) for item in parts[m]]
                + [(item, (1, 1, 1), (p, 0, 0)) for item in self.came[m]]
                for m in range(2)
            ]
            for p, parts in enumerate(self.parts)
        ]


def dp_groups():
    size = lax.axis_size("dp")
    return [[i for i in range(size) if i % 2 == low] for low in (0, 1)]


def gather_weight(mine, came, low, order):
    pair = paired(mine, came, low, order)
    full = lax.all_gather(pair, "row", axis=1, tiled=True)
    if lax.axis_size("dp") > 2:
        full = lax.all_gather(full, "dp", axis=0, tiled=True, axis_index_groups=dp_groups())
    return full.reshape(-1, full.shape[-1])


def start_scatter(grad):
    size, rows = lax.axis_size("dp"), lax.axis_size("row")
    grad = grad.reshape((size, rows) + grad.shape[1:])
    if size > 2:
        grad = lax.psum_scatter(
            grad, "dp", scatter_dimension=0, tiled=True, axis_index_groups=dp_groups()
        )
    return grad


def for_partner(pair, low, order):
    _, n, d = pair.shape

    def kernel(low_ref, pair_ref, out_ref):
        out_ref[...] = pair_ref[0]

    return order.call(
        "for_partner",
        kernel,
        (2,),
        [pl.BlockSpec((1, n // 2, d), lambda t, low: (1 - low[0], t, 0))],
        pl.BlockSpec((n // 2, d), lambda t, low: (t, 0)),
        shaped(n, d),
        (low, pair),
        prefetch=1,
        moved=4 * n * d,
    )


def scatter_weight(grad):
    grad = start_scatter(grad)
    grad = grad.reshape(2, -1, grad.shape[-1])
    return lax.psum_scatter(grad, "row", scatter_dimension=1, tiled=True)


class Chain:
    def __init__(self, grad):
        self.grad = start_scatter(grad)
        self.rows = lax.axis_size("row")
        self.step = 1
        self.came = ()
        far = self.rows - 1
        self.send(self.block(far), self.block(-far))

    def place(self, offset):
        return jnp.clip(lax.axis_index("row") + offset, 0, self.rows - 1).astype(jnp.int32)

    def block(self, offset):
        return lax.dynamic_index_in_dim(self.grad, self.place(offset), 1, keepdims=False)

    def send(self, up, down):
        far = self.rows - self.step
        self.came = (
            lax.ppermute(up, "row", [(i, i + 1) for i in range(self.step)]),
            lax.ppermute(down, "row", [(i, i - 1) for i in range(far, self.rows)]),
        )

    def advance(self, order):
        self.step += 1
        far = self.rows - self.step
        places = jnp.stack((self.place(far), self.place(-far)))
        _, _, n, d = self.grad.shape
        part = pl.BlockSpec((1, n, d), lambda p, at: (p, 0, 0))

        def picked(which):
            return pl.BlockSpec((1, 1, n, d), lambda p, at: (p, at[which], 0, 0))

        def kernel(at_ref, up_ref, down_ref, first_ref, second_ref, *out_refs):
            if far:
                out_refs[0][...] = add(first_ref[0], up_ref[...]).astype(BF)
                out_refs[1][...] = add(second_ref[0], down_ref[...]).astype(BF)
            else:
                out_refs[0][...] = (add(first_ref[0], up_ref[...]) + down_ref[...].astype(F32)).astype(BF)

        count = 2 if far else 1
        outs = order.call(
            "advance",
            kernel,
            (2,),
            [part, part, picked(0), picked(1)],
            [part] * count,
            [shaped(2, n, d)] * count,
            (places, *self.came, self.grad, self.grad),
            prefetch=1,
            moved=24 * n * d,
        )
        if far:
            self.send(*outs)
            return None
        return outs[0]


def sum_over_col(value):
    return sum([xchg(value, "col", mask) for mask in range(1, lax.axis_size("col"))], value)


def rope_tables(positions):
    freqs = THETA ** (-jnp.arange(HEAD_SIZE // 2, dtype=F32) * 2.0 / HEAD_SIZE)
    angles = positions.astype(F32)[:, None] * freqs[None, :]
    cosine, sine = jnp.cos(angles), jnp.sin(angles)
    return jnp.concatenate((cosine, cosine), axis=1), jnp.concatenate((-sine, sine), axis=1)


class Order:
    def __init__(self):
        self.last = ()

    def wait(self, *values):
        self.last = self.last + values

    def fence(self, *values):
        return self.call(
            "fence",
            lambda *refs: None,
            (1,),
            [pl.BlockSpec(memory_space=pl.ANY)] * len(values),
            [pl.BlockSpec(memory_space=pl.ANY)] * len(values),
            [shaped(*value.shape, dtype=value.dtype) for value in values],
            values,
            aliases={i: i for i in range(len(values))},
        )

    def call(
        self, name, kernel, grid, in_specs, out_specs, out_shape, args, scratch=(), flops=0, moved=0, prefetch=0, aliases=None
    ):
        last = [token for token in self.last if all(token is not arg for arg in args)]
        tokens = len(last)
        count = len(args)

        def run(*refs):
            kernel(*refs[:count], *refs[count + tokens :])

        outs = pl.pallas_call(
            run,
            grid_spec=pltpu.PrefetchScalarGridSpec(
                num_scalar_prefetch=prefetch,
                grid=grid,
                in_specs=list(in_specs) + [pl.BlockSpec(memory_space=pl.ANY)] * tokens,
                out_specs=out_specs,
                scratch_shapes=list(scratch),
            ),
            out_shape=out_shape,
            name=name,
            input_output_aliases=aliases or {},
            compiler_params=pltpu.CompilerParams(vmem_limit_bytes=VMEM),
            cost_estimate=pl.CostEstimate(flops=flops, bytes_accessed=moved, transcendentals=0),
        )(*args, *last)
        self.last = (outs[0] if isinstance(outs, (list, tuple)) else outs,)
        return outs


def shaped(*shape, dtype=BF):
    return jax.ShapeDtypeStruct(shape, dtype)


def block_spec(block, shape, index):
    _, place = block
    return pl.BlockSpec(shape, lambda *at: (place * index(*at)[1] + index(*at)[0], index(*at)[2]))


def arrays(blocks):
    return [item for item, _ in blocks]


def whole(shape):
    return pl.BlockSpec(shape, lambda *_: (0,) * len(shape))


SCALARS = pl.BlockSpec(memory_space=pltpu.SMEM)


def prepare_attn_kernel(low_ref, qkv_ref, out_ref, gain_ref, mine_ref, sent_ref):
    wide = qkv_ref.shape[1] // 2
    tall = out_ref.shape[0] // 2
    for part, ref in ((low_ref[0], mine_ref), (1 - low_ref[0], sent_ref)):
        columns = qkv_ref[:, pl.ds(pl.multiple_of(part * wide, wide), wide)]
        ref[:, :wide] = (columns.astype(F32) * gain_ref[...]).astype(BF)
        ref[:, wide:] = out_ref[pl.ds(pl.multiple_of(part * tall, tall), tall), :].T


def prepare_attn(low, wqkv, wo, gain, order):
    d = wqkv.shape[0]
    out = shaped(d, wqkv.shape[1] // 2 + wo.shape[0] // 2)
    return order.call(
        "prepare_attn",
        prepare_attn_kernel,
        (1,),
        [SCALARS] + [whole(item.shape) for item in (wqkv, wo, gain)],
        [whole(out.shape)] * 2,
        [out, out],
        (low, wqkv, wo, gain),
        moved=4 * (wqkv.size + wo.size),
    )


def prepare_ffn_kernel(chunks, cut, low_ref, w1_ref, w3_ref, w2_ref, gain_ref, *refs):
    units = w1_ref.shape[1] // 2
    gain = gain_ref[...]
    for at, chunk in enumerate(chunks):
        for part, ref in ((low_ref[0], refs[2 * at]), (1 - low_ref[0], refs[2 * at + 1])):
            place = pl.ds(pl.multiple_of(part * units + chunk * cut, cut), cut)
            ref[:, :cut] = (w1_ref[:, place].astype(F32) * gain).astype(BF)
            ref[:, cut : 2 * cut] = (w3_ref[:, place].astype(F32) * gain).astype(BF)
            ref[:, 2 * cut :] = w2_ref[place, :].T


def prepare_ffn(chunks, cut, low, w1, w3, w2, gain, order):
    out = shaped(w1.shape[0], 3 * cut)
    outs = order.call(
        "prepare_ffn",
        lambda *refs: prepare_ffn_kernel(chunks, cut, *refs),
        (1,),
        [SCALARS] + [whole(item.shape) for item in (w1, w3, w2, gain)],
        [whole(out.shape)] * (2 * len(chunks)),
        [out] * (2 * len(chunks)),
        (low, w1, w3, w2, gain),
        moved=12 * w1.size,
    )
    return [(outs[2 * i], outs[2 * i + 1]) for i in range(len(chunks))]


def paired_kernel(low_ref, mine_ref, came_ref, out_ref):
    out_ref[pl.ds(low_ref[0], 1)] = mine_ref[...][None]
    out_ref[pl.ds(1 - low_ref[0], 1)] = came_ref[...][None]


def paired(mine, came, low, order):
    out = shaped(2, *mine.shape)
    return order.call(
        "paired",
        paired_kernel,
        (1,),
        [SCALARS, whole(mine.shape), whole(mine.shape)],
        whole(out.shape),
        out,
        (low, mine, came),
        moved=8 * mine.size,
    )


def inverse_rms(values):
    return lax.rsqrt(jnp.mean(values * values, axis=-1, keepdims=True) + EPS)


def by_rows(kernel, ins, outs, order, scalars=None, steps=4):
    def spec(item):
        item, lead, at = item if isinstance(item, tuple) else (item, item.shape[:-2], None)
        at = at or (0,) * len(lead)
        return pl.BlockSpec(lead + (item.shape[-2] // steps, item.shape[-1]), lambda l: at + (l, 0))

    extra = [] if scalars is None else [scalars]
    args = [item[0] if isinstance(item, tuple) else item for item in ins]
    return order.call(
        "by_rows",
        kernel,
        (steps,),
        [SCALARS] * len(extra) + [spec(item) for item in ins],
        [spec(item) for item in outs],
        outs,
        (*extra, *args),
        moved=4 * sum(item.size for item in (*args, *outs)),
    )


def first_norm(inputs, order):
    def kernel(in_ref, out_ref):
        values = in_ref[...].astype(F32)
        out_ref[...] = (values * inverse_rms(values)).astype(BF)

    return by_rows(kernel, [inputs], [shaped(*inputs.shape)], order)[0]


def halved(first, second, order):
    half, width = first.shape[0] // 2, first.shape[1]

    def kernel(*refs):
        for ref, out_ref in zip(refs[:2], refs[2:]):
            out_ref[...] = ref[...]

    part = (half // 4, width)
    out = pl.BlockSpec(part, lambda l: (l, 0))
    return order.call(
        "halved",
        kernel,
        (4,),
        [out, pl.BlockSpec(part, lambda l: (4 + l, 0))],
        [out] * 2,
        [shaped(half, width)] * 2,
        (first, second),
        moved=8 * half * width,
    )


def total_of(refs):
    values = [ref[...].astype(F32) for ref in refs]
    return sum(value.reshape(value.shape[-2:]) for value in values)


def folded(groups, order):
    counts = [[len(items) for items in lists] for lists in groups]
    total = sum(sum(sizes) for sizes in counts)

    def kernel(*refs):
        start = 0
        for out_ref, sizes in zip(refs[total:], counts):
            for p, size in enumerate(sizes):
                values = [ref[...].astype(F32) for ref in refs[start : start + size]]
                shape = out_ref.shape[1:]
                out_ref[p] = sum(value.reshape(shape) for value in values).astype(BF)
                start += size

    outs = [shaped(len(lists), *lists[0][0][1], *lists[0][0][0].shape[-2:]) for lists in groups]
    ins = [item for lists in groups for items in lists for item in items]
    return by_rows(kernel, ins, outs, order, steps=2)


def with_terms(kernel, ins, outs, terms, order):
    count = len(ins)
    sizes = [len(items) for items in terms]

    def run(*refs):
        start = count
        for m, size in enumerate(sizes):
            total = total_of(refs[start : start + size])
            kernel(m, total, refs[:count], refs[count + sum(sizes) :])
            start += size

    return by_rows(run, [*ins, *[item for items in terms for item in items]], outs, order)


def second_norm(inputs, terms, cotangent, scalars, order):
    micro = inputs.shape[0]
    count = sum(len(items) for items in terms)

    def kernel(scalar_ref, in_ref, cot_ref, *refs):
        out_ref, residual_ref = refs[count:]
        start = 0
        for m, items in enumerate(terms):
            values = in_ref[m].astype(F32) + total_of(refs[start : start + len(items)])
            start += len(items)
            residual_ref[m] = values
            out_ref[m] = (values * inverse_rms(values)).astype(BF)
            first = scalar_ref[0] + pl.program_id(0) * in_ref.shape[1]
            places = first + lax.broadcasted_iota(jnp.int32, in_ref.shape[1:], 0)
            valid = places < scalar_ref[1 + m]
            out_ref[micro + m] = jnp.where(valid, cot_ref[m].astype(F32), 0.0).astype(BF)

    outs = [shaped(2 * micro, *inputs.shape[1:]), shaped(*inputs.shape, dtype=F32)]
    ins = [inputs, cotangent, *[item for items in terms for item in items]]
    return by_rows(kernel, ins, outs, order, scalars)


def norm_back(values, scaled):
    inverse = inverse_rms(values)
    inner = jnp.mean(scaled * values, axis=-1, keepdims=True)
    return inverse * scaled - values * (inverse * inverse * inverse) * inner


def second_norm_back(residual, upstream, terms, order):
    def kernel(m, total, ins, outs):
        grad = ins[1][m].astype(F32) + norm_back(ins[0][m], total)
        outs[0][m] = grad.astype(BF)
        outs[1][m] = grad

    outs = [shaped(*residual.shape), shaped(*residual.shape, dtype=F32)]
    return with_terms(kernel, [residual, upstream], outs, terms, order)


def finished(inputs, upstream, residual, terms, order):
    micro = inputs.shape[0]
    sizes = [[len(items) for items in payload] for payload in terms]

    def kernel(in_ref, up_ref, residual_ref, *refs):
        grad_ref, out_ref = refs[-2:]
        start = 0
        for m in range(micro):
            total = total_of(refs[start : start + sizes[0][m]])
            start += sizes[0][m]
            grad_ref[m] = (up_ref[m] + norm_back(in_ref[m].astype(F32), total)).astype(BF)
        for m in range(micro):
            total = total_of(refs[start : start + sizes[1][m]])
            start += sizes[1][m]
            out_ref[m] = (residual_ref[m] + total).astype(BF)

    ins = [inputs, upstream, residual] + [item for payload in terms for items in payload for item in items]
    return by_rows(kernel, ins, [shaped(*inputs.shape)] * 2, order)


def head_probs(query, keys, me, length, rows):
    places = query.shape[0]
    scores = dot(query, keys, 1, 1) * HEAD_SIZE ** (-0.5)
    queried = lax.broadcasted_iota(jnp.int32, (places, places), 0)
    keyed = lax.broadcasted_iota(jnp.int32, (places, places), 1)
    queried = ((queried // rows) ^ me) * rows + queried % rows
    keyed = ((keyed // rows) ^ me) * rows + keyed % rows
    scores = jnp.where((keyed <= queried) & (keyed < length), scores, NEGATIVE)
    expo = jnp.exp(scores - jnp.max(scores, axis=-1, keepdims=True))
    return expo * (1.0 / jnp.sum(expo, axis=-1, keepdims=True))


def turn(values, cosine, sine):
    return values * cosine + pltpu.roll(values, HEAD_SIZE // 2, 1) * sine


def joined(refs):
    return jnp.concatenate([ref[...] for ref in refs], axis=0)


def put_blocks(value, y, pairs, keep_ref, send_ref):
    rows = keep_ref.shape[1]
    for x in range(pairs):
        start = 2 * x * rows
        keep_ref[y * pairs + x] = value[start : start + rows].astype(BF)
        send_ref[y * pairs + x] = value[start + rows : start + 2 * rows].astype(BF)


def head_at(index):
    return slice(index * HEAD_SIZE, (index + 1) * HEAD_SIZE)


def attend_kernel(count, groups, scalar_ref, *refs):
    blocks = refs[:count]
    cos_ref, sin_ref, w_ref, keep_ref, send_ref, q_ref, k_ref, v_ref, a_ref = refs[count:]
    rows = blocks[0].shape[0]
    cols = count // 2
    span = (QUERY_PER_GROUP + 2) * HEAD_SIZE
    cosine, sine = cos_ref[...], sin_ref[...]
    for y in (0, 1):
        projected = dot(joined(blocks[y * cols : (y + 1) * cols]), w_ref[:, : groups * span], 1, 0)
        for g in range(groups):
            part = projected[:, g * span : (g + 1) * span]
            keys = turn(part[:, -2 * HEAD_SIZE : -HEAD_SIZE], cosine, sine).astype(BF)
            values = part[:, -HEAD_SIZE:].astype(BF)
            k_ref[y, :, head_at(g)] = keys
            v_ref[y, :, head_at(g)] = values
            for r in range(QUERY_PER_GROUP):
                query = turn(part[:, head_at(r)], cosine, sine).astype(BF)
                probs = head_probs(query, keys, scalar_ref[0], scalar_ref[1 + y], rows).astype(BF)
                at = head_at(g * QUERY_PER_GROUP + r)
                q_ref[y, :, at] = query
                a_ref[y, :, at] = dot(probs, values, 1, 0).astype(BF)
        put_blocks(dot(a_ref[y], w_ref[:, groups * span :], 1, 1), y, cols // 2, keep_ref, send_ref)


def attend(blocks, rows, scalars, cosine, sine, weights, groups, order):
    count = len(blocks)
    width = blocks[0][0].shape[1]
    places = count // 2 * rows
    head = groups * HEAD_SIZE
    sizes = (QUERY_PER_GROUP * head, head, head, QUERY_PER_GROUP * head)
    outs = [(count // 2, rows, width)] * 2 + [(2, places, size) for size in sizes]
    return order.call(
        "attend",
        lambda *refs: attend_kernel(count, groups, *refs),
        (1,),
        [SCALARS]
        + [block_spec(block, (rows, width), lambda _: (0, 1, 0)) for block in blocks]
        + [whole(item.shape) for item in (cosine, sine, weights)],
        [whole(shape) for shape in outs],
        [jax.ShapeDtypeStruct(shape, BF) for shape in outs],
        flops=4 * places * weights.size + 16 * places * places * QUERY_PER_GROUP * head,
        moved=8 * places * width + 2 * weights.size,
        args=(scalars, *arrays(blocks), cosine, sine, weights),
    )


def attend_back_kernel(count, groups, scalar_ref, *refs):
    pieces = refs[:count]
    cos_ref, sin_ref, w_ref, q_ref, k_ref, v_ref, keep_ref, send_ref, grad_ref = refs[count:]
    rows = pieces[0].shape[0]
    cols = count // 2
    span = (QUERY_PER_GROUP + 2) * HEAD_SIZE
    scale = HEAD_SIZE ** (-0.5)
    cosine, sine = cos_ref[...], -sin_ref[...]
    for y in (0, 1):
        piece = joined(pieces[y * cols : (y + 1) * cols])
        grad_out = dot(piece, w_ref[:, groups * span :], 1, 0).astype(BF)
        parts = []
        for g in range(groups):
            keys, values = k_ref[y, :, head_at(g)], v_ref[y, :, head_at(g)]
            keys_grad, values_grad = 0.0, 0.0
            for r in range(QUERY_PER_GROUP):
                at = head_at(g * QUERY_PER_GROUP + r)
                query, upstream = q_ref[y, :, at], grad_out[:, at]
                probs = head_probs(query, keys, scalar_ref[0], scalar_ref[1 + y], rows)
                grad_probs = dot(upstream, values, 1, 1)
                values_grad = values_grad + dot(probs.astype(BF), upstream, 0, 0)
                inner = jnp.sum(probs * grad_probs, axis=-1, keepdims=True)
                grad_scores = (probs * (grad_probs - inner)).astype(BF)
                parts.append(turn(dot(grad_scores, keys, 1, 0) * scale, cosine, sine))
                keys_grad = keys_grad + dot(grad_scores, query, 0, 0)
            parts.extend((turn(keys_grad * scale, cosine, sine), values_grad))
        grad_proj = jnp.concatenate([part.astype(BF) for part in parts], axis=1)
        grad_ref[y] = grad_proj
        put_blocks(dot(grad_proj, w_ref[:, : groups * span], 1, 1), y, cols // 2, keep_ref, send_ref)


def attend_back(pieces, rows, scalars, cosine, sine, weights, saved, groups, order):
    count = len(pieces)
    width = pieces[0][0].shape[1]
    places = count // 2 * rows
    span = groups * (QUERY_PER_GROUP + 2) * HEAD_SIZE
    outs = [(count // 2, rows, width)] * 2 + [(2, places, span)]
    return order.call(
        "attend_back",
        lambda *refs: attend_back_kernel(count, groups, *refs),
        (1,),
        [SCALARS]
        + [block_spec(block, (rows, width), lambda _: (0, 1, 0)) for block in pieces]
        + [whole(item.shape) for item in (cosine, sine, weights, *saved)],
        [whole(shape) for shape in outs],
        [jax.ShapeDtypeStruct(shape, BF) for shape in outs],
        flops=4 * places * weights.size + 48 * places * places * groups * HEAD_SIZE,
        moved=8 * places * width + 2 * weights.size,
        args=(scalars, *arrays(pieces), cosine, sine, weights, *saved),
    )


def units_kernel(count, cut, *refs):
    rows_refs, piece_refs = refs[:count], refs[count : 2 * count]
    w_ref, pair_ref, hidden_ref = refs[2 * count :]
    gate_up = dot(joined(rows_refs), w_ref[:, : 2 * cut], 1, 0)
    hidden_grad = dot(joined(piece_refs), w_ref[:, 2 * cut :], 1, 0)
    gate, up = gate_up[:, :cut], gate_up[:, cut:]
    sigma = 1.0 / (1.0 + jnp.exp(-gate))
    swish = gate * sigma
    hidden_ref[...] = (swish * up).astype(BF).reshape(hidden_ref.shape)
    pair_ref[..., :cut] = (
        (hidden_grad * up * sigma * (1.0 + gate * (1.0 - sigma))).astype(BF).reshape(hidden_ref.shape)
    )
    pair_ref[..., cut:] = (hidden_grad * swish).astype(BF).reshape(hidden_ref.shape)


def units(rows, pieces, places, weights, order):
    count = len(rows)
    width = weights.shape[0]
    cut = weights.shape[1] // 3
    part = places // 4
    return order.call(
        "units",
        lambda *refs: units_kernel(count, cut, *refs),
        (4,),
        [block_spec(block, (part, width), lambda l: (l, 4, 0)) for block in (*rows, *pieces)]
        + [whole(weights.shape)],
        [pl.BlockSpec((count, part, size), lambda l: (0, l, 0)) for size in (2 * cut, cut)],
        [shaped(count, places, size) for size in (2 * cut, cut)],
        flops=2 * count * places * weights.size,
        moved=4 * count * places * width,
        args=(*arrays(rows), *arrays(pieces), weights),
    )


def grads_kernel(counts, *refs):
    grad_ref = refs[-1]
    size = grad_ref.shape[2]
    start = at = 0
    lefts = refs[sum(n for n, _ in counts) :]
    for n, k in counts:
        rows = joined(refs[start : start + n])
        left = jnp.concatenate([ref[...] for ref in lefts[:k]], axis=0)
        start, lefts = start + n, lefts[k:]
        product = dot(left, rows, 0, 0).astype(BF)
        for block in range(grad_ref.shape[0]):
            grad_ref[block, at : at + product.shape[0]] = product[:, block * size : (block + 1) * size]
        at += product.shape[0]


def weight_grads(products, places, owners, order, total=None, into=None):
    rows = [block for blocks, _ in products for block in blocks]
    lefts = [left for _, items in products for left in items]
    counts = [(len(blocks), len(items)) for blocks, items in products]
    width = rows[0][0].shape[1]
    tile = width // 4
    part = sum(items[0].shape[1] for _, items in products)
    total = total or part
    at = 0 if into is None else total // part - 1
    tokens = len(products[0][0]) * places
    args = (*arrays(rows), *lefts) + (() if into is None else (into,))
    return order.call(
        "weight_grads",
        lambda *refs: grads_kernel(counts, *refs),
        (4,),
        [block_spec(block, (places, tile), lambda t: (0, 1, t)) for block in rows]
        + [whole(left.shape) for left in lefts]
        + [pl.BlockSpec(memory_space=pl.ANY)] * (into is not None),
        pl.BlockSpec((owners // 4, part, width // owners), lambda t: (t, at, 0)),
        shaped(owners, total, width // owners),
        flops=2 * tokens * part * width,
        moved=2 * len(products) * tokens * width,
        args=args,
        aliases={} if into is None else {len(args) - 1: 0},
    )


def back_kernel(count, split, added, *refs):
    lefts, weights = refs[:count], refs[count : 2 * count]
    refs = refs[2 * count :]
    total = refs[0][...] if added else None
    refs = refs[1:] if added else refs
    for left, weight in zip(lefts, weights):
        product = dot(left[...].reshape(-1, left.shape[-1]), weight[...], 1, 1)
        total = product if total is None else total + product
    if split:
        put_blocks(total, 0, refs[0].shape[0], *refs)
    else:
        refs[0][...] = total


def back(lefts, weights, lo, order, before=None, stream=None):
    count, places, depth = lefts[0].shape
    width = weights[0].shape[0]
    added, split = before is not None, stream is not None
    first = 2 * stream if split else 0
    half = pl.BlockSpec((2, places, width), lambda t: (t, 0, 0))
    flat = pl.BlockSpec((4 * places, width), lambda t: (first + t, 0))
    halves = shaped(4, places, width)
    steps = 2 if split else count // 4
    return order.call(
        "back",
        lambda *refs: back_kernel(len(lefts), split, added, *refs),
        (steps,),
        [pl.BlockSpec((4, places, depth), lambda t: (first + t, 0, 0))] * len(lefts)
        + [pl.BlockSpec((width, depth), lambda t: (0, lo // depth))] * len(weights)
        + ([flat] if added else []),
        [half, half] if split else flat,
        [halves, halves] if split else shaped(count * places, width, dtype=F32),
        flops=8 * steps * places * depth * width * len(lefts),
        moved=16 * steps * places * width,
        args=(*lefts, *weights, *((before,) if added else ())),
    )


def finish_ffn_kernel(count, cut, low_ref, *refs):
    pairs, cames = refs[:count], refs[count : 2 * count]
    w1_ref, w3_ref, gain_ref, grad1_ref, grad3_ref, grad2_ref, sum_ref = refs[2 * count :]
    units = w1_ref.shape[1] // 2
    gain, total = gain_ref[...], 0.0
    for chunk in range(count):
        for part, value in (
            (low_ref[0], pairs[chunk][low_ref[0]]),
            (1 - low_ref[0], cames[chunk][...]),
        ):
            place = pl.ds(pl.multiple_of(part * units + chunk * cut, cut), cut)
            value = value.astype(F32)
            first, second = value[:cut].T, value[cut : 2 * cut].T
            grad2_ref[place, :] = value[2 * cut :]
            grad1_ref[:, place] = first * gain
            grad3_ref[:, place] = second * gain
            product = first * w1_ref[:, place].astype(F32) + second * w3_ref[:, place].astype(F32)
            total = total + jnp.sum(product, axis=1, keepdims=True)
    sum_ref[...] = as_row(total)


def as_row(column):
    return jnp.broadcast_to(column, (column.shape[0], 128)).T[:1]


def finish_ffn(low, parts, w1, w3, w2, gain, order):
    count = len(parts)
    args = [pair for pair, _ in parts] + [came for _, came in parts] + [w1, w3, gain]
    outs = [shaped(*shape, dtype=F32) for shape in (w1.shape, w3.shape, w2.shape, gain.shape[::-1])]
    return order.call(
        "finish_ffn",
        lambda *refs: finish_ffn_kernel(count, parts[0][1].shape[0] // 3, *refs),
        (1,),
        [SCALARS] + [whole(item.shape) for item in args],
        [whole(item.shape) for item in outs],
        outs,
        (low, *args),
        moved=24 * w1.size,
    )


def finish_attn_kernel(low_ref, pair_ref, came_ref, w_ref, gain_ref, grad_ref, out_ref, sum_ref):
    wide = w_ref.shape[1] // 2
    tall = out_ref.shape[0] // 2
    gain, total = gain_ref[...], 0.0
    for part, value in ((low_ref[0], pair_ref[low_ref[0]]), (1 - low_ref[0], came_ref[...])):
        columns = pl.ds(pl.multiple_of(part * wide, wide), wide)
        value = value.astype(F32)
        first = value[:wide].T
        grad_ref[:, columns] = first * gain
        out_ref[pl.ds(pl.multiple_of(part * tall, tall), tall), :] = value[wide:]
        total = total + jnp.sum(first * w_ref[:, columns].astype(F32), axis=1, keepdims=True)
    sum_ref[...] = as_row(total)


def finish_attn(low, pair, came, wqkv, wo, gain, order):
    args = [pair, came, wqkv, gain]
    outs = [shaped(*shape, dtype=F32) for shape in (wqkv.shape, wo.shape, gain.shape[::-1])]
    return order.call(
        "finish_attn",
        finish_attn_kernel,
        (1,),
        [SCALARS] + [whole(item.shape) for item in args],
        [whole(item.shape) for item in outs],
        outs,
        (low, *args),
        moved=12 * wqkv.size,
    )


def body(inputs, lengths, wqkv, wo, w1, w3, w2, attn_gain, ffn_gain, cotangent):
    micro, _, rows, width = inputs.shape
    cols = lax.axis_size("col")
    places = cols * rows
    me = lax.axis_index("col")
    groups = wqkv.shape[1] // ((QUERY_PER_GROUP + 2) * HEAD_SIZE) // 2
    cut = w1.shape[1] // 2 // CHUNKS
    d = wqkv.shape[0]
    owners = width // d
    streams = range(micro)
    inputs, cotangent = inputs[:, 0], cotangent[:, 0]
    order = Order()
    low = (lax.axis_index("dp") % 2).astype(jnp.int32)[None]
    attn_gain, ffn_gain = attn_gain.astype(F32)[:, None], ffn_gain.astype(F32)[:, None]

    def prepared(*chunks):
        return prepare_ffn(chunks, cut, low, w1, w3, w2, ffn_gain, order)

    positions = (
        (jnp.arange(cols, dtype=jnp.int32) ^ me)[:, None] * rows
        + jnp.arange(rows, dtype=jnp.int32)[None, :]
    ).reshape(places)
    cosine, sine = rope_tables(positions)
    other_lengths = xchg(lengths, "dp", 1)
    scalars = [
        jnp.concatenate((me.astype(jnp.int32)[None], lengths[m], other_lengths[m])) for m in streams
    ]
    own_scalars = jnp.concatenate(((me * rows).astype(jnp.int32)[None], lengths.reshape(micro)))

    mine, sent = prepare_attn(low, wqkv, wo, attn_gain, order)
    normed1 = first_norm(inputs, order)
    attn_w = gather_weight(mine, xchg(sent, "dp", 1), low, order)
    attn_gather = Gather(normed1.reshape(-1, width), rows, False)
    attn_gather.cross(order)
    ((mine, sent),) = prepared(0)
    order.wait(cosine, sine, *scalars)
    (came,) = attn_gather.fence(order, xchg(sent, "dp", 1))
    ffn_ws = [gather_weight(mine, came, low, order)]
    (attn_rows,) = attn_gather.blocks(order)
    ((mine, sent),) = prepared(1)

    def run_attend(m):
        return attend(attn_rows[m], rows, scalars[m], cosine, sine, attn_w, groups, order)

    ahead = [run_attend(0), run_attend(1)]
    came, *sends = order.fence(xchg(sent, "dp", 1), *[item[1] for item in ahead])
    scatter = Scatter([(item[0], xchg(send, "col", 1)) for item, send in zip(ahead, sends)])
    ffn_ws.append(gather_weight(mine, came, low, order))
    scatter.first(order)
    scatter.second(order)
    normed2, residual = second_norm(inputs, scatter.terms()[0], cotangent, own_scalars, order)
    ffn_gather = Gather(normed2.reshape(-1, width), rows, True)
    ffn_gather.cross(order)
    ffn_gather.fence(order)
    (blocks,) = ffn_gather.blocks(order)
    all_rows, all_pieces = sum(blocks[:micro], []), sum(blocks[micro:], [])
    upstream = (normed2, (micro,), (1,))

    pairs, hiddens = [], []

    def run_units(chunk):
        pair, hidden = units(all_rows, all_pieces, rows, ffn_ws[chunk], order)
        pairs.append(pair)
        hiddens.append(hidden)

    def pair_grads(chunk):
        left = pairs[chunk].reshape(-1, 2 * cut)
        return weight_grads([(all_rows, [left])], rows, owners, order, total=3 * cut)

    def hidden_grads(chunk, into):
        left = hiddens[chunk].reshape(-1, cut)
        return weight_grads([(all_pieces, [left])], rows, owners, order, total=3 * cut, into=into)

    run_units(0)
    ffn_grads = [scatter_weight(hidden_grads(0, pair_grads(0)))]
    early = back(pairs, ffn_ws[:1], 0, order)
    run_units(1)
    halves = [back(pairs[1:], ffn_ws[1:], 0, order, before=early, stream=0)]
    first_came = xchg(halves[0][1], "col", 1)
    halves.append(back(pairs[1:], ffn_ws[1:], 0, order, before=early, stream=1))
    first_came, second_sent = order.fence(first_came, halves[1][1])
    scatter = Scatter([(halves[0][0], first_came), (halves[1][0], xchg(second_sent, "col", 1))])
    scatter.first(order)
    part = pair_grads(1)
    scatter.second(order)
    grads = hidden_grads(1, part)
    attn_up, residual_grad = second_norm_back(residual, upstream, scatter.terms()[0], order)
    attn_gather = Gather(attn_up.reshape(-1, width), rows, True)
    ffn_grads.append(scatter_weight(order.fence(grads)[0]))
    halves = [back(hiddens, ffn_ws, 2 * cut, order, stream=0)]
    sent = for_partner(ffn_grads[0], low, order)
    attn_gather.cross(order)
    halves.append(back(hiddens, ffn_ws, 2 * cut, order, stream=1))
    attn_gather.fence(order)
    attn_pieces, sent, *sends = attn_gather.blocks(order, sent, *[send for _, send in halves])
    halves = [(keep, send) for (keep, _), send in zip(halves, sends)]

    def run_back(m):
        return attend_back(
            attn_pieces[m], rows, scalars[m], cosine, sine, attn_w, ahead[m][2:5], groups, order
        )

    out_sent = [(keep, xchg(send, "col", 1)) for keep, send in halves]
    came = xchg(sent, "dp", 1)
    behind = [run_back(0)]
    first_came = xchg(behind[0][1], "col", 1)
    behind.append(run_back(1))
    came, first_came, second_sent, *values = order.fence(
        came, first_came, behind[1][1], *[item for _, item in out_sent]
    )
    ffn_parts = [(ffn_grads[0], came)]
    out_parts = [(keep, item) for (keep, _), item in zip(out_sent, values)]
    attn_parts = [(behind[0][0], first_came), (behind[1][0], xchg(second_sent, "col", 1))]
    scatter = Scatter(attn_parts, out_parts)
    scatter.first(order)
    attn_grads = weight_grads(
        [
            (sum(attn_rows, []), [item[2].reshape(2 * places, -1) for item in behind]),
            (sum(attn_pieces, []), [item[5].reshape(2 * places, -1) for item in ahead]),
        ],
        rows,
        owners,
        order,
    )
    chain = Chain(attn_grads)
    sent = for_partner(ffn_grads[1], low, order)
    chain.advance(order)
    (came,) = order.fence(xchg(sent, "dp", 1))
    ffn_parts.append((ffn_grads[1], came))
    scatter.second(order)
    chain.advance(order)
    source_grad, result = finished(inputs, residual_grad, residual, scatter.terms(), order)
    attn_pair = chain.advance(order)
    attn_came = xchg(for_partner(attn_pair, low, order), "dp", 1)
    w1_grad, w3_grad, w2_grad, ffn_sum = finish_ffn(low, ffn_parts, w1, w3, w2, ffn_gain, order)
    ffn_sum = sum_over_col(ffn_sum)[0]
    wqkv_grad, wo_grad, attn_sum = finish_attn(low, attn_pair, attn_came, wqkv, wo, attn_gain, order)
    attn_sum = sum_over_col(attn_sum)[0]
    return (
        result[:, None],
        source_grad[:, None],
        attn_sum,
        ffn_sum,
        wqkv_grad,
        wo_grad,
        w1_grad,
        w3_grad,
        w2_grad,
    )


def solution(mesh):
    tokens = P(None, ("dp", "row"), "col", None)
    in_specs = (
        tokens,
        P(None, ("dp", "row")),
        P(("dp", "row"), "col"),
        P("col", ("dp", "row")),
        P(("dp", "row"), "col"),
        P(("dp", "row"), "col"),
        P("col", ("dp", "row")),
        P(("dp", "row")),
        P(("dp", "row")),
        tokens,
    )
    out_specs = (
        tokens,
        tokens,
        P(("dp", "row")),
        P(("dp", "row")),
        P(("dp", "row"), "col"),
        P("col", ("dp", "row")),
        P(("dp", "row"), "col"),
        P(("dp", "row"), "col"),
        P("col", ("dp", "row")),
    )
    return jax.shard_map(body, mesh=mesh, in_specs=in_specs, out_specs=out_specs, check_vma=False)
```

```python
import jax
import jax.numpy as jnp
from jax import lax
from jax.experimental import pallas as pl
from jax.experimental.pallas import tpu as pltpu
from jax.sharding import PartitionSpec as P

HEAD_SIZE = 128
QUERY_PER_GROUP = 2
EPS = 1e-05
THETA = 1000000.0
NEGATIVE = -1e30
CHUNKS = 2
VMEM = 127 * 2**19
BF = jnp.bfloat16
F32 = jnp.float32


def xchg(value, axis, bit):
    size = lax.axis_size(axis)
    return lax.ppermute(value, axis, [(i, i ^ bit) for i in range(size)])


def dot(left, right, left_dim, right_dim):
    return lax.dot_general(
        left, right, (((left_dim,), (right_dim,)), ((), ())), preferred_element_type=F32
    )


def add(left, right):
    return left.astype(F32) + right.astype(F32)


class Gather:
    def __init__(self, own, rows, shared):
        self.own, self.rows, self.shared = own, rows, shared
        self.came = [xchg(own, "col", 2), xchg(own, "dp", 1), xchg(own, "col", 1)]

    def cross(self, order):
        over_x, over_y, core = order.fence(*self.came)
        if self.shared:
            first, second = halved(over_y, over_x, order)
            diagonal = [xchg(first, "col", 2), xchg(second, "dp", 1)]
        else:
            diagonal = [xchg(over_y, "col", 2)]
        self.arrays = [self.own, core, over_x, over_y]
        self.came = [xchg(over_x, "col", 1), xchg(over_y, "col", 1)] + diagonal

    def fence(self, order, *others):
        values = order.fence(*self.came, *others)
        self.came = values[: len(self.came)]
        return values[len(self.came) :]

    def blocks(self, order, *others):
        own, core, over_x, over_y = self.arrays
        core_x, core_y, *diagonal = self.came
        values = order.fence(*[xchg(item, "col", 1) for item in diagonal], *others)
        other, others = values[: len(diagonal)], values[len(diagonal) :]
        each = self.own.shape[0] // self.rows // len(diagonal)
        streams = []
        for m in range(each * len(diagonal)):
            found = [(item, m) for item in (own, core, over_x, core_x, over_y, core_y)]
            which, place = divmod(m, each)
            streams.append(found + [(diagonal[which], place), (other[which], place)])
        return (streams, *others)


class Scatter:
    def __init__(self, *payloads):
        shape = (2, 2) + payloads[0][0][0].shape[1:]
        self.parts = [
            [[keep.reshape(shape), came.reshape(shape)] for keep, came in parts]
            for parts in payloads
        ]
        self.came = [[], []]

    def send(self, picks, axes, order):
        count = len(self.parts)
        sums = [
            [(item, *pick) for item in parts[m]]
            + [(item, (1, *pick[0]), (p, *pick[1])) for item in self.came[m]]
            for m, pick in enumerate(picks)
            for p, parts in enumerate(self.parts)
        ]
        sent = folded([sums[:count], sums[count:]], order)
        for m, (axis, bit) in enumerate(axes):
            self.came[m].append(xchg(sent[m], axis, bit))

    def first(self, order):
        self.send((((2, 1), (0, 1)), ((1, 2), (1, 0))), (("col", 2), ("dp", 1)), order)

    def second(self, order):
        self.send((((1, 1), (1, 0)), ((1, 1), (0, 1))), (("dp", 1), ("col", 2)), order)

    def terms(self):
        return [
            [
                [(item, (1, 1), (0, 0)) for item in parts[m]]
                + [(item, (1, 1, 1), (p, 0, 0)) for item in self.came[m]]
                for m in range(2)
            ]
            for p, parts in enumerate(self.parts)
        ]


def dp_groups():
    size = lax.axis_size("dp")
    return [[i for i in range(size) if i % 2 == low] for low in (0, 1)]


def gather_weight(mine, came, low, order):
    pair = paired(mine, came, low, order)
    full = lax.all_gather(pair, "row", axis=1, tiled=True)
    if lax.axis_size("dp") > 2:
        full = lax.all_gather(full, "dp", axis=0, tiled=True, axis_index_groups=dp_groups())
    return full.reshape(-1, full.shape[-1])


def start_scatter(grad):
    size, rows = lax.axis_size("dp"), lax.axis_size("row")
    grad = grad.reshape((size, rows) + grad.shape[1:])
    if size > 2:
        grad = lax.psum_scatter(
            grad, "dp", scatter_dimension=0, tiled=True, axis_index_groups=dp_groups()
        )
    return grad


def for_partner(pair, low, order):
    _, n, d = pair.shape

    def kernel(low_ref, pair_ref, out_ref):
        out_ref[...] = pair_ref[0]

    return order.call(
        "for_partner",
        kernel,
        (2,),
        [pl.BlockSpec((1, n // 2, d), lambda t, low: (1 - low[0], t, 0))],
        pl.BlockSpec((n // 2, d), lambda t, low: (t, 0)),
        shaped(n, d),
        (low, pair),
        prefetch=1,
        moved=4 * n * d,
    )


def scatter_weight(grad):
    grad = start_scatter(grad)
    grad = grad.reshape(2, -1, grad.shape[-1])
    return lax.psum_scatter(grad, "row", scatter_dimension=1, tiled=True)


def sum_over_col(value):
    return sum([xchg(value, "col", mask) for mask in range(1, lax.axis_size("col"))], value)


def rope_tables(positions):
    freqs = THETA ** (-jnp.arange(HEAD_SIZE // 2, dtype=F32) * 2.0 / HEAD_SIZE)
    angles = positions.astype(F32)[:, None] * freqs[None, :]
    cosine, sine = jnp.cos(angles), jnp.sin(angles)
    return jnp.concatenate((cosine, cosine), axis=1), jnp.concatenate((-sine, sine), axis=1)


class Order:
    def __init__(self):
        self.last = ()

    def wait(self, *values):
        self.last = self.last + values

    def fence(self, *values):
        return self.call(
            "fence",
            lambda *refs: None,
            (1,),
            [pl.BlockSpec(memory_space=pl.ANY)] * len(values),
            [pl.BlockSpec(memory_space=pl.ANY)] * len(values),
            [shaped(*value.shape, dtype=value.dtype) for value in values],
            values,
            aliases={i: i for i in range(len(values))},
        )

    def call(
        self, name, kernel, grid, in_specs, out_specs, out_shape, args, scratch=(), flops=0, moved=0, prefetch=0, aliases=None
    ):
        last = [token for token in self.last if all(token is not arg for arg in args)]
        tokens = len(last)
        count = len(args)

        def run(*refs):
            kernel(*refs[:count], *refs[count + tokens :])

        outs = pl.pallas_call(
            run,
            grid_spec=pltpu.PrefetchScalarGridSpec(
                num_scalar_prefetch=prefetch,
                grid=grid,
                in_specs=list(in_specs) + [pl.BlockSpec(memory_space=pl.ANY)] * tokens,
                out_specs=out_specs,
                scratch_shapes=list(scratch),
            ),
            out_shape=out_shape,
            name=name,
            input_output_aliases=aliases or {},
            compiler_params=pltpu.CompilerParams(vmem_limit_bytes=VMEM),
            cost_estimate=pl.CostEstimate(flops=flops, bytes_accessed=moved, transcendentals=0),
        )(*args, *last)
        self.last = (outs[0] if isinstance(outs, (list, tuple)) else outs,)
        return outs


def shaped(*shape, dtype=BF):
    return jax.ShapeDtypeStruct(shape, dtype)


def block_spec(block, shape, index):
    _, place = block
    return pl.BlockSpec(shape, lambda *at: (place * index(*at)[1] + index(*at)[0], index(*at)[2]))


def arrays(blocks):
    return [item for item, _ in blocks]


def whole(shape):
    return pl.BlockSpec(shape, lambda *_: (0,) * len(shape))


SCALARS = pl.BlockSpec(memory_space=pltpu.SMEM)


def prepare_attn_kernel(low_ref, qkv_ref, out_ref, gain_ref, mine_ref, sent_ref):
    wide = qkv_ref.shape[1] // 2
    tall = out_ref.shape[0] // 2
    for part, ref in ((low_ref[0], mine_ref), (1 - low_ref[0], sent_ref)):
        columns = qkv_ref[:, pl.ds(pl.multiple_of(part * wide, wide), wide)]
        ref[:, :wide] = (columns.astype(F32) * gain_ref[...]).astype(BF)
        ref[:, wide:] = out_ref[pl.ds(pl.multiple_of(part * tall, tall), tall), :].T


def prepare_attn(low, wqkv, wo, gain, order):
    d = wqkv.shape[0]
    out = shaped(d, wqkv.shape[1] // 2 + wo.shape[0] // 2)
    return order.call(
        "prepare_attn",
        prepare_attn_kernel,
        (1,),
        [SCALARS] + [whole(item.shape) for item in (wqkv, wo, gain)],
        [whole(out.shape)] * 2,
        [out, out],
        (low, wqkv, wo, gain),
        moved=4 * (wqkv.size + wo.size),
    )


def prepare_ffn_kernel(chunks, cut, low_ref, w1_ref, w3_ref, w2_ref, gain_ref, *refs):
    units = w1_ref.shape[1] // 2
    gain = gain_ref[...]
    for at, chunk in enumerate(chunks):
        for part, ref in ((low_ref[0], refs[2 * at]), (1 - low_ref[0], refs[2 * at + 1])):
            place = pl.ds(pl.multiple_of(part * units + chunk * cut, cut), cut)
            ref[:, :cut] = (w1_ref[:, place].astype(F32) * gain).astype(BF)
            ref[:, cut : 2 * cut] = (w3_ref[:, place].astype(F32) * gain).astype(BF)
            ref[:, 2 * cut :] = w2_ref[place, :].T


def prepare_ffn(chunks, cut, low, w1, w3, w2, gain, order):
    out = shaped(w1.shape[0], 3 * cut)
    outs = order.call(
        "prepare_ffn",
        lambda *refs: prepare_ffn_kernel(chunks, cut, *refs),
        (1,),
        [SCALARS] + [whole(item.shape) for item in (w1, w3, w2, gain)],
        [whole(out.shape)] * (2 * len(chunks)),
        [out] * (2 * len(chunks)),
        (low, w1, w3, w2, gain),
        moved=12 * w1.size,
    )
    return [(outs[2 * i], outs[2 * i + 1]) for i in range(len(chunks))]


def paired_kernel(low_ref, mine_ref, came_ref, out_ref):
    out_ref[pl.ds(low_ref[0], 1)] = mine_ref[...][None]
    out_ref[pl.ds(1 - low_ref[0], 1)] = came_ref[...][None]


def paired(mine, came, low, order):
    out = shaped(2, *mine.shape)
    return order.call(
        "paired",
        paired_kernel,
        (1,),
        [SCALARS, whole(mine.shape), whole(mine.shape)],
        whole(out.shape),
        out,
        (low, mine, came),
        moved=8 * mine.size,
    )


def inverse_rms(values):
    return lax.rsqrt(jnp.mean(values * values, axis=-1, keepdims=True) + EPS)


def by_rows(kernel, ins, outs, order, scalars=None, steps=4):
    def spec(item):
        item, lead, at = item if isinstance(item, tuple) else (item, item.shape[:-2], None)
        at = at or (0,) * len(lead)
        return pl.BlockSpec(lead + (item.shape[-2] // steps, item.shape[-1]), lambda l: at + (l, 0))

    extra = [] if scalars is None else [scalars]
    args = [item[0] if isinstance(item, tuple) else item for item in ins]
    return order.call(
        "by_rows",
        kernel,
        (steps,),
        [SCALARS] * len(extra) + [spec(item) for item in ins],
        [spec(item) for item in outs],
        outs,
        (*extra, *args),
        moved=4 * sum(item.size for item in (*args, *outs)),
    )


def first_norm(inputs, order):
    def kernel(in_ref, out_ref):
        values = in_ref[...].astype(F32)
        out_ref[...] = (values * inverse_rms(values)).astype(BF)

    return by_rows(kernel, [inputs], [shaped(*inputs.shape)], order)[0]


def halved(first, second, order):
    half, width = first.shape[0] // 2, first.shape[1]

    def kernel(*refs):
        for ref, out_ref in zip(refs[:2], refs[2:]):
            out_ref[...] = ref[...]

    part = (half // 4, width)
    out = pl.BlockSpec(part, lambda l: (l, 0))
    return order.call(
        "halved",
        kernel,
        (4,),
        [out, pl.BlockSpec(part, lambda l: (4 + l, 0))],
        [out] * 2,
        [shaped(half, width)] * 2,
        (first, second),
        moved=8 * half * width,
    )


def total_of(refs):
    values = [ref[...].astype(F32) for ref in refs]
    return sum(value.reshape(value.shape[-2:]) for value in values)


def folded(groups, order):
    counts = [[len(items) for items in lists] for lists in groups]
    total = sum(sum(sizes) for sizes in counts)

    def kernel(*refs):
        start = 0
        for out_ref, sizes in zip(refs[total:], counts):
            for p, size in enumerate(sizes):
                values = [ref[...].astype(F32) for ref in refs[start : start + size]]
                shape = out_ref.shape[1:]
                out_ref[p] = sum(value.reshape(shape) for value in values).astype(BF)
                start += size

    outs = [shaped(len(lists), *lists[0][0][1], *lists[0][0][0].shape[-2:]) for lists in groups]
    ins = [item for lists in groups for items in lists for item in items]
    return by_rows(kernel, ins, outs, order, steps=2)


def with_terms(kernel, ins, outs, terms, order):
    count = len(ins)
    sizes = [len(items) for items in terms]

    def run(*refs):
        start = count
        for m, size in enumerate(sizes):
            total = total_of(refs[start : start + size])
            kernel(m, total, refs[:count], refs[count + sum(sizes) :])
            start += size

    return by_rows(run, [*ins, *[item for items in terms for item in items]], outs, order)


def second_norm(inputs, terms, cotangent, scalars, order):
    micro = inputs.shape[0]
    count = sum(len(items) for items in terms)

    def kernel(scalar_ref, in_ref, cot_ref, *refs):
        out_ref, residual_ref = refs[count:]
        start = 0
        for m, items in enumerate(terms):
            values = in_ref[m].astype(F32) + total_of(refs[start : start + len(items)])
            start += len(items)
            residual_ref[m] = values
            out_ref[m] = (values * inverse_rms(values)).astype(BF)
            first = scalar_ref[0] + pl.program_id(0) * in_ref.shape[1]
            places = first + lax.broadcasted_iota(jnp.int32, in_ref.shape[1:], 0)
            valid = places < scalar_ref[1 + m]
            out_ref[micro + m] = jnp.where(valid, cot_ref[m].astype(F32), 0.0).astype(BF)

    outs = [shaped(2 * micro, *inputs.shape[1:]), shaped(*inputs.shape, dtype=F32)]
    ins = [inputs, cotangent, *[item for items in terms for item in items]]
    return by_rows(kernel, ins, outs, order, scalars)


def norm_back(values, scaled):
    inverse = inverse_rms(values)
    inner = jnp.mean(scaled * values, axis=-1, keepdims=True)
    return inverse * scaled - values * (inverse * inverse * inverse) * inner


def second_norm_back(residual, upstream, terms, order):
    def kernel(m, total, ins, outs):
        grad = ins[1][m].astype(F32) + norm_back(ins[0][m], total)
        outs[0][m] = grad.astype(BF)
        outs[1][m] = grad

    outs = [shaped(*residual.shape), shaped(*residual.shape, dtype=F32)]
    return with_terms(kernel, [residual, upstream], outs, terms, order)


def finished(inputs, upstream, residual, terms, order):
    micro = inputs.shape[0]
    sizes = [[len(items) for items in payload] for payload in terms]

    def kernel(in_ref, up_ref, residual_ref, *refs):
        grad_ref, out_ref = refs[-2:]
        start = 0
        for m in range(micro):
            total = total_of(refs[start : start + sizes[0][m]])
            start += sizes[0][m]
            grad_ref[m] = (up_ref[m] + norm_back(in_ref[m].astype(F32), total)).astype(BF)
        for m in range(micro):
            total = total_of(refs[start : start + sizes[1][m]])
            start += sizes[1][m]
            out_ref[m] = (residual_ref[m] + total).astype(BF)

    ins = [inputs, upstream, residual] + [item for payload in terms for items in payload for item in items]
    return by_rows(kernel, ins, [shaped(*inputs.shape)] * 2, order)


def head_probs(query, keys, me, length, rows):
    places = query.shape[0]
    scores = dot(query, keys, 1, 1) * HEAD_SIZE ** (-0.5)
    queried = lax.broadcasted_iota(jnp.int32, (places, places), 0)
    keyed = lax.broadcasted_iota(jnp.int32, (places, places), 1)
    queried = ((queried // rows) ^ me) * rows + queried % rows
    keyed = ((keyed // rows) ^ me) * rows + keyed % rows
    scores = jnp.where((keyed <= queried) & (keyed < length), scores, NEGATIVE)
    expo = jnp.exp(scores - jnp.max(scores, axis=-1, keepdims=True))
    return expo * (1.0 / jnp.sum(expo, axis=-1, keepdims=True))


def turn(values, cosine, sine):
    return values * cosine + pltpu.roll(values, HEAD_SIZE // 2, 1) * sine


def joined(refs):
    return jnp.concatenate([ref[...] for ref in refs], axis=0)


def put_blocks(value, y, pairs, keep_ref, send_ref):
    rows = keep_ref.shape[1]
    for x in range(pairs):
        start = 2 * x * rows
        keep_ref[y * pairs + x] = value[start : start + rows].astype(BF)
        send_ref[y * pairs + x] = value[start + rows : start + 2 * rows].astype(BF)


def head_at(index):
    return slice(index * HEAD_SIZE, (index + 1) * HEAD_SIZE)


def attend_kernel(count, groups, scalar_ref, *refs):
    blocks = refs[:count]
    cos_ref, sin_ref, w_ref, keep_ref, send_ref, q_ref, k_ref, v_ref, a_ref = refs[count:]
    rows = blocks[0].shape[0]
    cols = count // 2
    span = (QUERY_PER_GROUP + 2) * HEAD_SIZE
    cosine, sine = cos_ref[...], sin_ref[...]
    for y in (0, 1):
        projected = dot(joined(blocks[y * cols : (y + 1) * cols]), w_ref[:, : groups * span], 1, 0)
        for g in range(groups):
            part = projected[:, g * span : (g + 1) * span]
            keys = turn(part[:, -2 * HEAD_SIZE : -HEAD_SIZE], cosine, sine).astype(BF)
            values = part[:, -HEAD_SIZE:].astype(BF)
            k_ref[y, :, head_at(g)] = keys
            v_ref[y, :, head_at(g)] = values
            for r in range(QUERY_PER_GROUP):
                query = turn(part[:, head_at(r)], cosine, sine).astype(BF)
                probs = head_probs(query, keys, scalar_ref[0], scalar_ref[1 + y], rows).astype(BF)
                at = head_at(g * QUERY_PER_GROUP + r)
                q_ref[y, :, at] = query
                a_ref[y, :, at] = dot(probs, values, 1, 0).astype(BF)
        put_blocks(dot(a_ref[y], w_ref[:, groups * span :], 1, 1), y, cols // 2, keep_ref, send_ref)


def attend(blocks, rows, scalars, cosine, sine, weights, groups, order):
    count = len(blocks)
    width = blocks[0][0].shape[1]
    places = count // 2 * rows
    head = groups * HEAD_SIZE
    sizes = (QUERY_PER_GROUP * head, head, head, QUERY_PER_GROUP * head)
    outs = [(count // 2, rows, width)] * 2 + [(2, places, size) for size in sizes]
    return order.call(
        "attend",
        lambda *refs: attend_kernel(count, groups, *refs),
        (1,),
        [SCALARS]
        + [block_spec(block, (rows, width), lambda _: (0, 1, 0)) for block in blocks]
        + [whole(item.shape) for item in (cosine, sine, weights)],
        [whole(shape) for shape in outs],
        [jax.ShapeDtypeStruct(shape, BF) for shape in outs],
        flops=4 * places * weights.size + 16 * places * places * QUERY_PER_GROUP * head,
        moved=8 * places * width + 2 * weights.size,
        args=(scalars, *arrays(blocks), cosine, sine, weights),
    )


def attend_back_kernel(count, groups, scalar_ref, *refs):
    pieces = refs[:count]
    cos_ref, sin_ref, w_ref, q_ref, k_ref, v_ref, keep_ref, send_ref, grad_ref = refs[count:]
    rows = pieces[0].shape[0]
    cols = count // 2
    span = (QUERY_PER_GROUP + 2) * HEAD_SIZE
    scale = HEAD_SIZE ** (-0.5)
    cosine, sine = cos_ref[...], -sin_ref[...]
    for y in (0, 1):
        piece = joined(pieces[y * cols : (y + 1) * cols])
        grad_out = dot(piece, w_ref[:, groups * span :], 1, 0).astype(BF)
        parts = []
        for g in range(groups):
            keys, values = k_ref[y, :, head_at(g)], v_ref[y, :, head_at(g)]
            keys_grad, values_grad = 0.0, 0.0
            for r in range(QUERY_PER_GROUP):
                at = head_at(g * QUERY_PER_GROUP + r)
                query, upstream = q_ref[y, :, at], grad_out[:, at]
                probs = head_probs(query, keys, scalar_ref[0], scalar_ref[1 + y], rows)
                grad_probs = dot(upstream, values, 1, 1)
                values_grad = values_grad + dot(probs.astype(BF), upstream, 0, 0)
                inner = jnp.sum(probs * grad_probs, axis=-1, keepdims=True)
                grad_scores = (probs * (grad_probs - inner)).astype(BF)
                parts.append(turn(dot(grad_scores, keys, 1, 0) * scale, cosine, sine))
                keys_grad = keys_grad + dot(grad_scores, query, 0, 0)
            parts.extend((turn(keys_grad * scale, cosine, sine), values_grad))
        grad_proj = jnp.concatenate([part.astype(BF) for part in parts], axis=1)
        grad_ref[y] = grad_proj
        put_blocks(dot(grad_proj, w_ref[:, : groups * span], 1, 1), y, cols // 2, keep_ref, send_ref)


def attend_back(pieces, rows, scalars, cosine, sine, weights, saved, groups, order):
    count = len(pieces)
    width = pieces[0][0].shape[1]
    places = count // 2 * rows
    span = groups * (QUERY_PER_GROUP + 2) * HEAD_SIZE
    outs = [(count // 2, rows, width)] * 2 + [(2, places, span)]
    return order.call(
        "attend_back",
        lambda *refs: attend_back_kernel(count, groups, *refs),
        (1,),
        [SCALARS]
        + [block_spec(block, (rows, width), lambda _: (0, 1, 0)) for block in pieces]
        + [whole(item.shape) for item in (cosine, sine, weights, *saved)],
        [whole(shape) for shape in outs],
        [jax.ShapeDtypeStruct(shape, BF) for shape in outs],
        flops=4 * places * weights.size + 48 * places * places * groups * HEAD_SIZE,
        moved=8 * places * width + 2 * weights.size,
        args=(scalars, *arrays(pieces), cosine, sine, weights, *saved),
    )


def units_kernel(count, cut, *refs):
    rows_refs, piece_refs = refs[:count], refs[count : 2 * count]
    w_ref, pair_ref, hidden_ref = refs[2 * count :]
    gate_up = dot(joined(rows_refs), w_ref[:, : 2 * cut], 1, 0)
    hidden_grad = dot(joined(piece_refs), w_ref[:, 2 * cut :], 1, 0)
    gate, up = gate_up[:, :cut], gate_up[:, cut:]
    sigma = 1.0 / (1.0 + jnp.exp(-gate))
    swish = gate * sigma
    hidden_ref[...] = (swish * up).astype(BF).reshape(hidden_ref.shape)
    pair_ref[..., :cut] = (
        (hidden_grad * up * sigma * (1.0 + gate * (1.0 - sigma))).astype(BF).reshape(hidden_ref.shape)
    )
    pair_ref[..., cut:] = (hidden_grad * swish).astype(BF).reshape(hidden_ref.shape)


def units(rows, pieces, places, weights, order):
    count = len(rows)
    width = weights.shape[0]
    cut = weights.shape[1] // 3
    part = places // 4
    return order.call(
        "units",
        lambda *refs: units_kernel(count, cut, *refs),
        (4,),
        [block_spec(block, (part, width), lambda l: (l, 4, 0)) for block in (*rows, *pieces)]
        + [whole(weights.shape)],
        [pl.BlockSpec((count, part, size), lambda l: (0, l, 0)) for size in (2 * cut, cut)],
        [shaped(count, places, size) for size in (2 * cut, cut)],
        flops=2 * count * places * weights.size,
        moved=4 * count * places * width,
        args=(*arrays(rows), *arrays(pieces), weights),
    )


def grads_kernel(counts, *refs):
    grad_ref = refs[-1]
    size = grad_ref.shape[2]
    start = at = 0
    lefts = refs[sum(n for n, _ in counts) :]
    for n, k in counts:
        rows = joined(refs[start : start + n])
        left = jnp.concatenate([ref[...] for ref in lefts[:k]], axis=0)
        start, lefts = start + n, lefts[k:]
        product = dot(left, rows, 0, 0).astype(BF)
        for block in range(grad_ref.shape[0]):
            grad_ref[block, at : at + product.shape[0]] = product[:, block * size : (block + 1) * size]
        at += product.shape[0]


def weight_grads(products, places, owners, order, total=None, into=None):
    rows = [block for blocks, _ in products for block in blocks]
    lefts = [left for _, items in products for left in items]
    counts = [(len(blocks), len(items)) for blocks, items in products]
    width = rows[0][0].shape[1]
    tile = width // 4
    part = sum(items[0].shape[1] for _, items in products)
    total = total or part
    at = 0 if into is None else total // part - 1
    tokens = len(products[0][0]) * places
    args = (*arrays(rows), *lefts) + (() if into is None else (into,))
    return order.call(
        "weight_grads",
        lambda *refs: grads_kernel(counts, *refs),
        (4,),
        [block_spec(block, (places, tile), lambda t: (0, 1, t)) for block in rows]
        + [whole(left.shape) for left in lefts]
        + [pl.BlockSpec(memory_space=pl.ANY)] * (into is not None),
        pl.BlockSpec((owners // 4, part, width // owners), lambda t: (t, at, 0)),
        shaped(owners, total, width // owners),
        flops=2 * tokens * part * width,
        moved=2 * len(products) * tokens * width,
        args=args,
        aliases={} if into is None else {len(args) - 1: 0},
    )


def back_kernel(count, split, added, *refs):
    lefts, weights = refs[:count], refs[count : 2 * count]
    refs = refs[2 * count :]
    total = refs[0][...] if added else None
    refs = refs[1:] if added else refs
    for left, weight in zip(lefts, weights):
        product = dot(left[...].reshape(-1, left.shape[-1]), weight[...], 1, 1)
        total = product if total is None else total + product
    if split:
        put_blocks(total, 0, refs[0].shape[0], *refs)
    else:
        refs[0][...] = total


def back(lefts, weights, lo, order, before=None, stream=None):
    count, places, depth = lefts[0].shape
    width = weights[0].shape[0]
    added, split = before is not None, stream is not None
    first = 2 * stream if split else 0
    half = pl.BlockSpec((2, places, width), lambda t: (t, 0, 0))
    flat = pl.BlockSpec((4 * places, width), lambda t: (first + t, 0))
    halves = shaped(4, places, width)
    steps = 2 if split else count // 4
    return order.call(
        "back",
        lambda *refs: back_kernel(len(lefts), split, added, *refs),
        (steps,),
        [pl.BlockSpec((4, places, depth), lambda t: (first + t, 0, 0))] * len(lefts)
        + [pl.BlockSpec((width, depth), lambda t: (0, lo // depth))] * len(weights)
        + ([flat] if added else []),
        [half, half] if split else flat,
        [halves, halves] if split else shaped(count * places, width, dtype=F32),
        flops=8 * steps * places * depth * width * len(lefts),
        moved=16 * steps * places * width,
        args=(*lefts, *weights, *((before,) if added else ())),
    )


def finish_ffn_kernel(count, cut, low_ref, *refs):
    pairs, cames = refs[:count], refs[count : 2 * count]
    w1_ref, w3_ref, gain_ref, grad1_ref, grad3_ref, grad2_ref, sum_ref = refs[2 * count :]
    units = w1_ref.shape[1] // 2
    gain, total = gain_ref[...], 0.0
    for chunk in range(count):
        for part, value in (
            (low_ref[0], pairs[chunk][low_ref[0]]),
            (1 - low_ref[0], cames[chunk][...]),
        ):
            place = pl.ds(pl.multiple_of(part * units + chunk * cut, cut), cut)
            value = value.astype(F32)
            first, second = value[:cut].T, value[cut : 2 * cut].T
            grad2_ref[place, :] = value[2 * cut :]
            grad1_ref[:, place] = first * gain
            grad3_ref[:, place] = second * gain
            product = first * w1_ref[:, place].astype(F32) + second * w3_ref[:, place].astype(F32)
            total = total + jnp.sum(product, axis=1, keepdims=True)
    sum_ref[...] = as_row(total)


def as_row(column):
    return jnp.broadcast_to(column, (column.shape[0], 128)).T[:1]


def finish_ffn(low, parts, w1, w3, w2, gain, order):
    count = len(parts)
    args = [pair for pair, _ in parts] + [came for _, came in parts] + [w1, w3, gain]
    outs = [shaped(*shape, dtype=F32) for shape in (w1.shape, w3.shape, w2.shape, gain.shape[::-1])]
    return order.call(
        "finish_ffn",
        lambda *refs: finish_ffn_kernel(count, parts[0][1].shape[0] // 3, *refs),
        (1,),
        [SCALARS] + [whole(item.shape) for item in args],
        [whole(item.shape) for item in outs],
        outs,
        (low, *args),
        moved=24 * w1.size,
    )


def finish_attn_kernel(low_ref, pair_ref, came_ref, w_ref, gain_ref, grad_ref, out_ref, sum_ref):
    wide = w_ref.shape[1] // 2
    tall = out_ref.shape[0] // 2
    gain, total = gain_ref[...], 0.0
    for part, value in ((low_ref[0], pair_ref[low_ref[0]]), (1 - low_ref[0], came_ref[...])):
        columns = pl.ds(pl.multiple_of(part * wide, wide), wide)
        value = value.astype(F32)
        first = value[:wide].T
        grad_ref[:, columns] = first * gain
        out_ref[pl.ds(pl.multiple_of(part * tall, tall), tall), :] = value[wide:]
        total = total + jnp.sum(first * w_ref[:, columns].astype(F32), axis=1, keepdims=True)
    sum_ref[...] = as_row(total)


def finish_attn(low, pair, came, wqkv, wo, gain, order):
    args = [pair, came, wqkv, gain]
    outs = [shaped(*shape, dtype=F32) for shape in (wqkv.shape, wo.shape, gain.shape[::-1])]
    return order.call(
        "finish_attn",
        finish_attn_kernel,
        (1,),
        [SCALARS] + [whole(item.shape) for item in args],
        [whole(item.shape) for item in outs],
        outs,
        (low, *args),
        moved=12 * wqkv.size,
    )


def body(inputs, lengths, wqkv, wo, w1, w3, w2, attn_gain, ffn_gain, cotangent):
    micro, _, rows, width = inputs.shape
    cols = lax.axis_size("col")
    places = cols * rows
    me = lax.axis_index("col")
    groups = wqkv.shape[1] // ((QUERY_PER_GROUP + 2) * HEAD_SIZE) // 2
    cut = w1.shape[1] // 2 // CHUNKS
    d = wqkv.shape[0]
    owners = width // d
    streams = range(micro)
    inputs, cotangent = inputs[:, 0], cotangent[:, 0]
    order = Order()
    low = (lax.axis_index("dp") % 2).astype(jnp.int32)[None]
    attn_gain, ffn_gain = attn_gain.astype(F32)[:, None], ffn_gain.astype(F32)[:, None]

    def prepared(*chunks):
        return prepare_ffn(chunks, cut, low, w1, w3, w2, ffn_gain, order)

    positions = (
        (jnp.arange(cols, dtype=jnp.int32) ^ me)[:, None] * rows
        + jnp.arange(rows, dtype=jnp.int32)[None, :]
    ).reshape(places)
    cosine, sine = rope_tables(positions)
    other_lengths = xchg(lengths, "dp", 1)
    scalars = [
        jnp.concatenate((me.astype(jnp.int32)[None], lengths[m], other_lengths[m])) for m in streams
    ]
    own_scalars = jnp.concatenate(((me * rows).astype(jnp.int32)[None], lengths.reshape(micro)))

    mine, sent = prepare_attn(low, wqkv, wo, attn_gain, order)
    normed1 = first_norm(inputs, order)
    attn_w = gather_weight(mine, xchg(sent, "dp", 1), low, order)
    attn_gather = Gather(normed1.reshape(-1, width), rows, False)
    attn_gather.cross(order)
    ((mine, sent),) = prepared(0)
    order.wait(cosine, sine, *scalars)
    (came,) = attn_gather.fence(order, xchg(sent, "dp", 1))
    ffn_ws = [gather_weight(mine, came, low, order)]
    (attn_rows,) = attn_gather.blocks(order)
    ((mine, sent),) = prepared(1)

    def run_attend(m):
        return attend(attn_rows[m], rows, scalars[m], cosine, sine, attn_w, groups, order)

    ahead = [run_attend(0), run_attend(1)]
    came, *sends = order.fence(xchg(sent, "dp", 1), *[item[1] for item in ahead])
    scatter = Scatter([(item[0], xchg(send, "col", 1)) for item, send in zip(ahead, sends)])
    ffn_ws.append(gather_weight(mine, came, low, order))
    scatter.first(order)
    scatter.second(order)
    normed2, residual = second_norm(inputs, scatter.terms()[0], cotangent, own_scalars, order)
    ffn_gather = Gather(normed2.reshape(-1, width), rows, True)
    ffn_gather.cross(order)
    ffn_gather.fence(order)
    (blocks,) = ffn_gather.blocks(order)
    all_rows, all_pieces = sum(blocks[:micro], []), sum(blocks[micro:], [])
    upstream = (normed2, (micro,), (1,))

    pairs, hiddens = [], []

    def run_units(chunk):
        pair, hidden = units(all_rows, all_pieces, rows, ffn_ws[chunk], order)
        pairs.append(pair)
        hiddens.append(hidden)

    def pair_grads(chunk):
        left = pairs[chunk].reshape(-1, 2 * cut)
        return weight_grads([(all_rows, [left])], rows, owners, order, total=3 * cut)

    def hidden_grads(chunk, into):
        left = hiddens[chunk].reshape(-1, cut)
        return weight_grads([(all_pieces, [left])], rows, owners, order, total=3 * cut, into=into)

    run_units(0)
    ffn_grads = [scatter_weight(hidden_grads(0, pair_grads(0)))]
    early = back(pairs, ffn_ws[:1], 0, order)
    run_units(1)
    halves = [back(pairs[1:], ffn_ws[1:], 0, order, before=early, stream=0)]
    first_came = xchg(halves[0][1], "col", 1)
    halves.append(back(pairs[1:], ffn_ws[1:], 0, order, before=early, stream=1))
    first_came, second_sent = order.fence(first_came, halves[1][1])
    scatter = Scatter([(halves[0][0], first_came), (halves[1][0], xchg(second_sent, "col", 1))])
    scatter.first(order)
    part = pair_grads(1)
    scatter.second(order)
    grads = hidden_grads(1, part)
    attn_up, residual_grad = second_norm_back(residual, upstream, scatter.terms()[0], order)
    attn_gather = Gather(attn_up.reshape(-1, width), rows, True)
    ffn_grads.append(scatter_weight(order.fence(grads)[0]))
    halves = [back(hiddens, ffn_ws, 2 * cut, order, stream=0)]
    sent = for_partner(ffn_grads[0], low, order)
    attn_gather.cross(order)
    halves.append(back(hiddens, ffn_ws, 2 * cut, order, stream=1))
    attn_gather.fence(order)
    attn_pieces, sent, *sends = attn_gather.blocks(order, sent, *[send for _, send in halves])
    halves = [(keep, send) for (keep, _), send in zip(halves, sends)]

    def run_back(m):
        return attend_back(
            attn_pieces[m], rows, scalars[m], cosine, sine, attn_w, ahead[m][2:5], groups, order
        )

    out_sent = [(keep, xchg(send, "col", 1)) for keep, send in halves]
    came = xchg(sent, "dp", 1)
    behind = [run_back(0)]
    first_came = xchg(behind[0][1], "col", 1)
    behind.append(run_back(1))
    came, first_came, second_sent, *values = order.fence(
        came, first_came, behind[1][1], *[item for _, item in out_sent]
    )
    ffn_parts = [(ffn_grads[0], came)]
    out_parts = [(keep, item) for (keep, _), item in zip(out_sent, values)]
    attn_parts = [(behind[0][0], first_came), (behind[1][0], xchg(second_sent, "col", 1))]
    scatter, out_scatter = Scatter(attn_parts), Scatter(out_parts)
    scatter.first(order)
    attn_grads = weight_grads(
        [
            (sum(attn_rows, []), [item[2].reshape(2 * places, -1) for item in behind]),
            (sum(attn_pieces, []), [item[5].reshape(2 * places, -1) for item in ahead]),
        ],
        rows,
        owners,
        order,
    )
    out_scatter.first(order)
    scatter.second(order)
    attn_pair = scatter_weight(order.fence(attn_grads)[0])
    sent = for_partner(ffn_grads[1], low, order)
    out_scatter.second(order)
    (came,) = order.fence(xchg(sent, "dp", 1))
    ffn_parts.append((ffn_grads[1], came))
    w1_grad, w3_grad, w2_grad, ffn_sum = finish_ffn(low, ffn_parts, w1, w3, w2, ffn_gain, order)
    ffn_sum = sum_over_col(ffn_sum)[0]
    terms = scatter.terms() + out_scatter.terms()
    sent = for_partner(attn_pair, low, order)
    source_grad, result = finished(inputs, residual_grad, residual, terms, order)
    attn_came = xchg(sent, "dp", 1)
    wqkv_grad, wo_grad, attn_sum = finish_attn(low, attn_pair, attn_came, wqkv, wo, attn_gain, order)
    attn_sum = sum_over_col(attn_sum)[0]
    return (
        result[:, None],
        source_grad[:, None],
        attn_sum,
        ffn_sum,
        wqkv_grad,
        wo_grad,
        w1_grad,
        w3_grad,
        w2_grad,
    )


def solution(mesh):
    tokens = P(None, ("dp", "row"), "col", None)
    in_specs = (
        tokens,
        P(None, ("dp", "row")),
        P(("dp", "row"), "col"),
        P("col", ("dp", "row")),
        P(("dp", "row"), "col"),
        P(("dp", "row"), "col"),
        P("col", ("dp", "row")),
        P(("dp", "row")),
        P(("dp", "row")),
        tokens,
    )
    out_specs = (
        tokens,
        tokens,
        P(("dp", "row")),
        P(("dp", "row")),
        P(("dp", "row"), "col"),
        P("col", ("dp", "row")),
        P(("dp", "row"), "col"),
        P(("dp", "row"), "col"),
        P("col", ("dp", "row")),
    )
    return jax.shard_map(body, mesh=mesh, in_specs=in_specs, out_specs=out_specs, check_vma=False)
```

```python
import jax
import jax.numpy as jnp
from jax import lax
from jax.experimental import pallas as pl
from jax.experimental.pallas import tpu as pltpu
from jax.sharding import PartitionSpec as P

HEAD_SIZE = 128
QUERY_PER_GROUP = 2
EPS = 1e-05
THETA = 1000000.0
NEGATIVE = -1e30
CHUNKS = 2
VMEM = 64 * 2**20
BF = jnp.bfloat16
F32 = jnp.float32


def xchg(value, axis, bit):
    size = lax.axis_size(axis)
    return lax.ppermute(value, axis, [(i, i ^ bit) for i in range(size)])


def dot(left, right, left_dim, right_dim):
    return lax.dot_general(
        left, right, (((left_dim,), (right_dim,)), ((), ())), preferred_element_type=F32
    )


def add(left, right):
    return left.astype(F32) + right.astype(F32)


class Gather:
    def __init__(self, own, rows, shared):
        self.own, self.rows, self.shared = own, rows, shared
        self.came = [xchg(own, "col", 2), xchg(own, "dp", 1), xchg(own, "col", 1)]

    def cross(self, order):
        over_x, over_y, core = order.fence(*self.came)
        if self.shared:
            first, second = halved(over_y, over_x, order)
            diagonal = [xchg(first, "col", 2), xchg(second, "dp", 1)]
        else:
            diagonal = [xchg(over_y, "col", 2)]
        self.arrays = [self.own, core, over_x, over_y]
        self.came = [xchg(over_x, "col", 1), xchg(over_y, "col", 1)] + diagonal

    def fence(self, order, *others):
        values = order.fence(*self.came, *others)
        self.came = values[: len(self.came)]
        return values[len(self.came) :]

    def blocks(self, order, *others):
        own, core, over_x, over_y = self.arrays
        core_x, core_y, *diagonal = self.came
        values = order.fence(*[xchg(item, "col", 1) for item in diagonal], *others)
        other, others = values[: len(diagonal)], values[len(diagonal) :]
        each = self.own.shape[0] // self.rows // len(diagonal)
        streams = []
        for m in range(each * len(diagonal)):
            found = [(item, m) for item in (own, core, over_x, core_x, over_y, core_y)]
            which, place = divmod(m, each)
            streams.append(found + [(diagonal[which], place), (other[which], place)])
        return (streams, *others)


class Scatter:
    def __init__(self, *payloads):
        shape = (2, 2) + payloads[0][0][0].shape[1:]
        self.parts = [
            [[keep.reshape(shape), came.reshape(shape)] for keep, came in parts]
            for parts in payloads
        ]
        self.came = [[], []]

    def send(self, picks, axes, order):
        count = len(self.parts)
        sums = [
            [(item, *pick) for item in parts[m]]
            + [(item, (1, *pick[0]), (p, *pick[1])) for item in self.came[m]]
            for m, pick in enumerate(picks)
            for p, parts in enumerate(self.parts)
        ]
        sent = folded([sums[:count], sums[count:]], order)
        for m, (axis, bit) in enumerate(axes):
            self.came[m].append(xchg(sent[m], axis, bit))

    def first(self, order):
        self.send((((2, 1), (0, 1)), ((1, 2), (1, 0))), (("col", 2), ("dp", 1)), order)

    def second(self, order):
        self.send((((1, 1), (1, 0)), ((1, 1), (0, 1))), (("dp", 1), ("col", 2)), order)

    def terms(self):
        return [
            [
                [(item, (1, 1), (0, 0)) for item in parts[m]]
                + [(item, (1, 1, 1), (p, 0, 0)) for item in self.came[m]]
                for m in range(2)
            ]
            for p, parts in enumerate(self.parts)
        ]


def dp_groups():
    size = lax.axis_size("dp")
    return [[i for i in range(size) if i % 2 == low] for low in (0, 1)]


def gather_weight(mine, came, low, order):
    pair = paired(mine, came, low, order)
    full = lax.all_gather(pair, "row", axis=1, tiled=True)
    if lax.axis_size("dp") > 2:
        full = lax.all_gather(full, "dp", axis=0, tiled=True, axis_index_groups=dp_groups())
    return full.reshape(-1, full.shape[-1])


def start_scatter(grad):
    size, rows = lax.axis_size("dp"), lax.axis_size("row")
    grad = grad.reshape((size, rows) + grad.shape[1:])
    if size > 2:
        grad = lax.psum_scatter(
            grad, "dp", scatter_dimension=0, tiled=True, axis_index_groups=dp_groups()
        )
    return grad


def for_partner(pair, low, order):
    _, n, d = pair.shape

    def kernel(low_ref, pair_ref, out_ref):
        out_ref[...] = pair_ref[0]

    return order.call(
        "for_partner",
        kernel,
        (2,),
        [pl.BlockSpec((1, n // 2, d), lambda t, low: (1 - low[0], t, 0))],
        pl.BlockSpec((n // 2, d), lambda t, low: (t, 0)),
        shaped(n, d),
        (low, pair),
        prefetch=1,
        moved=4 * n * d,
    )


def scatter_weight(grad):
    grad = start_scatter(grad)
    grad = grad.reshape(2, -1, grad.shape[-1])
    return lax.psum_scatter(grad, "row", scatter_dimension=1, tiled=True)


def sum_over_col(value):
    return sum([xchg(value, "col", mask) for mask in range(1, lax.axis_size("col"))], value)


def rope_tables(positions):
    freqs = THETA ** (-jnp.arange(HEAD_SIZE // 2, dtype=F32) * 2.0 / HEAD_SIZE)
    angles = positions.astype(F32)[:, None] * freqs[None, :]
    cosine, sine = jnp.cos(angles), jnp.sin(angles)
    return jnp.concatenate((cosine, cosine), axis=1), jnp.concatenate((-sine, sine), axis=1)


class Order:
    def __init__(self):
        self.last = ()

    def wait(self, *values):
        self.last = self.last + values

    def fence(self, *values):
        return self.call(
            "fence",
            lambda *refs: None,
            (1,),
            [pl.BlockSpec(memory_space=pl.ANY)] * len(values),
            [pl.BlockSpec(memory_space=pl.ANY)] * len(values),
            [shaped(*value.shape, dtype=value.dtype) for value in values],
            values,
            aliases={i: i for i in range(len(values))},
        )

    def call(
        self, name, kernel, grid, in_specs, out_specs, out_shape, args, scratch=(), flops=0, moved=0, prefetch=0, aliases=None
    ):
        last = [token for token in self.last if all(token is not arg for arg in args)]
        tokens = len(last)
        count = len(args)

        def run(*refs):
            kernel(*refs[:count], *refs[count + tokens :])

        outs = pl.pallas_call(
            run,
            grid_spec=pltpu.PrefetchScalarGridSpec(
                num_scalar_prefetch=prefetch,
                grid=grid,
                in_specs=list(in_specs) + [pl.BlockSpec(memory_space=pl.ANY)] * tokens,
                out_specs=out_specs,
                scratch_shapes=list(scratch),
            ),
            out_shape=out_shape,
            name=name,
            input_output_aliases=aliases or {},
            compiler_params=pltpu.CompilerParams(vmem_limit_bytes=VMEM),
            cost_estimate=pl.CostEstimate(flops=flops, bytes_accessed=moved, transcendentals=0),
        )(*args, *last)
        self.last = (outs[0] if isinstance(outs, (list, tuple)) else outs,)
        return outs


def shaped(*shape, dtype=BF):
    return jax.ShapeDtypeStruct(shape, dtype)


def block_spec(block, shape, index):
    _, place = block
    return pl.BlockSpec(shape, lambda *at: (place * index(*at)[1] + index(*at)[0], index(*at)[2]))


def arrays(blocks):
    return [item for item, _ in blocks]


def whole(shape):
    return pl.BlockSpec(shape, lambda *_: (0,) * len(shape))


SCALARS = pl.BlockSpec(memory_space=pltpu.SMEM)


def prepare_attn_kernel(part_ref, qkv_ref, out_ref, gain_ref, half_ref):
    wide = qkv_ref.shape[1] // 2
    tall = out_ref.shape[0] // 2
    part = part_ref[0]
    columns = qkv_ref[:, pl.ds(pl.multiple_of(part * wide, wide), wide)]
    half_ref[:, :wide] = (columns.astype(F32) * gain_ref[...]).astype(BF)
    half_ref[:, wide:] = out_ref[pl.ds(pl.multiple_of(part * tall, tall), tall), :].T


def prepare_attn(part, wqkv, wo, gain, order):
    d = wqkv.shape[0]
    out = shaped(d, wqkv.shape[1] // 2 + wo.shape[0] // 2)
    return order.call(
        "prepare_attn",
        prepare_attn_kernel,
        (1,),
        [SCALARS] + [whole(item.shape) for item in (wqkv, wo, gain)],
        whole(out.shape),
        out,
        (part, wqkv, wo, gain),
        moved=2 * (wqkv.size + wo.size),
    )


def prepare_ffn_kernel(chunks, cut, low_ref, w1_ref, w3_ref, w2_ref, gain_ref, *refs):
    units = w1_ref.shape[1] // 2
    gain = gain_ref[...]
    for at, chunk in enumerate(chunks):
        for part, ref in ((low_ref[0], refs[2 * at]), (1 - low_ref[0], refs[2 * at + 1])):
            place = pl.ds(pl.multiple_of(part * units + chunk * cut, cut), cut)
            ref[:, :cut] = (w1_ref[:, place].astype(F32) * gain).astype(BF)
            ref[:, cut : 2 * cut] = (w3_ref[:, place].astype(F32) * gain).astype(BF)
            ref[:, 2 * cut :] = w2_ref[place, :].T


def prepare_ffn(chunks, cut, low, w1, w3, w2, gain, order):
    out = shaped(w1.shape[0], 3 * cut)
    outs = order.call(
        "prepare_ffn",
        lambda *refs: prepare_ffn_kernel(chunks, cut, *refs),
        (1,),
        [SCALARS] + [whole(item.shape) for item in (w1, w3, w2, gain)],
        [whole(out.shape)] * (2 * len(chunks)),
        [out] * (2 * len(chunks)),
        (low, w1, w3, w2, gain),
        moved=12 * w1.size,
    )
    return [(outs[2 * i], outs[2 * i + 1]) for i in range(len(chunks))]


def paired_kernel(low_ref, mine_ref, came_ref, out_ref):
    out_ref[pl.ds(low_ref[0], 1)] = mine_ref[...][None]
    out_ref[pl.ds(1 - low_ref[0], 1)] = came_ref[...][None]


def paired(mine, came, low, order):
    out = shaped(2, *mine.shape)
    return order.call(
        "paired",
        paired_kernel,
        (1,),
        [SCALARS, whole(mine.shape), whole(mine.shape)],
        whole(out.shape),
        out,
        (low, mine, came),
        moved=8 * mine.size,
    )


def inverse_rms(values):
    return lax.rsqrt(jnp.mean(values * values, axis=-1, keepdims=True) + EPS)


def by_rows(kernel, ins, outs, order, scalars=None, steps=4):
    def spec(item):
        item, lead, at = item if isinstance(item, tuple) else (item, item.shape[:-2], None)
        at = at or (0,) * len(lead)
        return pl.BlockSpec(lead + (item.shape[-2] // steps, item.shape[-1]), lambda l: at + (l, 0))

    extra = [] if scalars is None else [scalars]
    args = [item[0] if isinstance(item, tuple) else item for item in ins]
    return order.call(
        "by_rows",
        kernel,
        (steps,),
        [SCALARS] * len(extra) + [spec(item) for item in ins],
        [spec(item) for item in outs],
        outs,
        (*extra, *args),
        moved=4 * sum(item.size for item in (*args, *outs)),
    )


def first_norm(inputs, order):
    def kernel(in_ref, out_ref):
        values = in_ref[...].astype(F32)
        out_ref[...] = (values * inverse_rms(values)).astype(BF)

    return by_rows(kernel, [inputs], [shaped(*inputs.shape)], order)[0]


def halved(first, second, order):
    half, width = first.shape[0] // 2, first.shape[1]

    def kernel(*refs):
        for ref, out_ref in zip(refs[:2], refs[2:]):
            out_ref[...] = ref[...]

    part = (half // 4, width)
    out = pl.BlockSpec(part, lambda l: (l, 0))
    return order.call(
        "halved",
        kernel,
        (4,),
        [out, pl.BlockSpec(part, lambda l: (4 + l, 0))],
        [out] * 2,
        [shaped(half, width)] * 2,
        (first, second),
        moved=8 * half * width,
    )


def total_of(refs):
    values = [ref[...].astype(F32) for ref in refs]
    return sum(value.reshape(value.shape[-2:]) for value in values)


def folded(groups, order):
    counts = [[len(items) for items in lists] for lists in groups]
    total = sum(sum(sizes) for sizes in counts)

    def kernel(*refs):
        start = 0
        for out_ref, sizes in zip(refs[total:], counts):
            for p, size in enumerate(sizes):
                values = [ref[...].astype(F32) for ref in refs[start : start + size]]
                shape = out_ref.shape[1:]
                out_ref[p] = sum(value.reshape(shape) for value in values).astype(BF)
                start += size

    outs = [shaped(len(lists), *lists[0][0][1], *lists[0][0][0].shape[-2:]) for lists in groups]
    ins = [item for lists in groups for items in lists for item in items]
    return by_rows(kernel, ins, outs, order, steps=2)


def with_terms(kernel, ins, outs, terms, order):
    count = len(ins)
    sizes = [len(items) for items in terms]

    def run(*refs):
        start = count
        for m, size in enumerate(sizes):
            total = total_of(refs[start : start + size])
            kernel(m, total, refs[:count], refs[count + sum(sizes) :])
            start += size

    return by_rows(run, [*ins, *[item for items in terms for item in items]], outs, order)


def second_norm(inputs, terms, cotangent, scalars, order):
    micro = inputs.shape[0]
    count = sum(len(items) for items in terms)

    def kernel(scalar_ref, in_ref, cot_ref, *refs):
        out_ref, residual_ref = refs[count:]
        start = 0
        for m, items in enumerate(terms):
            values = in_ref[m].astype(F32) + total_of(refs[start : start + len(items)])
            start += len(items)
            residual_ref[m] = values
            out_ref[m] = (values * inverse_rms(values)).astype(BF)
            first = scalar_ref[0] + pl.program_id(0) * in_ref.shape[1]
            places = first + lax.broadcasted_iota(jnp.int32, in_ref.shape[1:], 0)
            valid = places < scalar_ref[1 + m]
            out_ref[micro + m] = jnp.where(valid, cot_ref[m].astype(F32), 0.0).astype(BF)

    outs = [shaped(2 * micro, *inputs.shape[1:]), shaped(*inputs.shape, dtype=F32)]
    ins = [inputs, cotangent, *[item for items in terms for item in items]]
    return by_rows(kernel, ins, outs, order, scalars)


def norm_back(values, scaled):
    inverse = inverse_rms(values)
    inner = jnp.mean(scaled * values, axis=-1, keepdims=True)
    return inverse * scaled - values * (inverse * inverse * inverse) * inner


def second_norm_back(residual, upstream, terms, order):
    def kernel(m, total, ins, outs):
        grad = ins[1][m].astype(F32) + norm_back(ins[0][m], total)
        outs[0][m] = grad.astype(BF)
        outs[1][m] = grad

    outs = [shaped(*residual.shape), shaped(*residual.shape, dtype=F32)]
    return with_terms(kernel, [residual, upstream], outs, terms, order)


def finished(inputs, upstream, residual, terms, order):
    micro = inputs.shape[0]
    sizes = [[len(items) for items in payload] for payload in terms]

    def kernel(in_ref, up_ref, residual_ref, *refs):
        grad_ref, out_ref = refs[-2:]
        start = 0
        for m in range(micro):
            total = total_of(refs[start : start + sizes[0][m]])
            start += sizes[0][m]
            grad_ref[m] = (up_ref[m] + norm_back(in_ref[m].astype(F32), total)).astype(BF)
        for m in range(micro):
            total = total_of(refs[start : start + sizes[1][m]])
            start += sizes[1][m]
            out_ref[m] = (residual_ref[m] + total).astype(BF)

    ins = [inputs, upstream, residual] + [item for payload in terms for items in payload for item in items]
    return by_rows(kernel, ins, [shaped(*inputs.shape)] * 2, order)


def head_probs(query, keys, me, length, rows):
    places = query.shape[0]
    scores = dot(query, keys, 1, 1) * HEAD_SIZE ** (-0.5)
    queried = lax.broadcasted_iota(jnp.int32, (places, places), 0)
    keyed = lax.broadcasted_iota(jnp.int32, (places, places), 1)
    queried = ((queried // rows) ^ me) * rows + queried % rows
    keyed = ((keyed // rows) ^ me) * rows + keyed % rows
    scores = jnp.where((keyed <= queried) & (keyed < length), scores, NEGATIVE)
    expo = jnp.exp(scores - jnp.max(scores, axis=-1, keepdims=True))
    return expo * (1.0 / jnp.sum(expo, axis=-1, keepdims=True))


def turn(values, cosine, sine):
    return values * cosine + pltpu.roll(values, HEAD_SIZE // 2, 1) * sine


def joined(refs):
    return jnp.concatenate([ref[...] for ref in refs], axis=0)


def put_blocks(value, y, pairs, keep_ref, send_ref):
    rows = keep_ref.shape[1]
    for x in range(pairs):
        start = 2 * x * rows
        keep_ref[y * pairs + x] = value[start : start + rows].astype(BF)
        send_ref[y * pairs + x] = value[start + rows : start + 2 * rows].astype(BF)


def head_at(index):
    return slice(index * HEAD_SIZE, (index + 1) * HEAD_SIZE)


def attend_kernel(count, groups, scalar_ref, *refs):
    blocks = refs[:count]
    cos_ref, sin_ref, w_ref, keep_ref, send_ref, q_ref, k_ref, v_ref, a_ref = refs[count:]
    rows = blocks[0].shape[0]
    cols = count // 2
    span = (QUERY_PER_GROUP + 2) * HEAD_SIZE
    cosine, sine = cos_ref[...], sin_ref[...]
    for y in (0, 1):
        projected = dot(joined(blocks[y * cols : (y + 1) * cols]), w_ref[:, : groups * span], 1, 0)
        for g in range(groups):
            part = projected[:, g * span : (g + 1) * span]
            keys = turn(part[:, -2 * HEAD_SIZE : -HEAD_SIZE], cosine, sine).astype(BF)
            values = part[:, -HEAD_SIZE:].astype(BF)
            k_ref[y, :, head_at(g)] = keys
            v_ref[y, :, head_at(g)] = values
            for r in range(QUERY_PER_GROUP):
                query = turn(part[:, head_at(r)], cosine, sine).astype(BF)
                probs = head_probs(query, keys, scalar_ref[0], scalar_ref[1 + y], rows).astype(BF)
                at = head_at(g * QUERY_PER_GROUP + r)
                q_ref[y, :, at] = query
                a_ref[y, :, at] = dot(probs, values, 1, 0).astype(BF)
        put_blocks(dot(a_ref[y], w_ref[:, groups * span :], 1, 1), y, cols // 2, keep_ref, send_ref)


def attend(blocks, rows, scalars, cosine, sine, weights, groups, order):
    count = len(blocks)
    width = blocks[0][0].shape[1]
    places = count // 2 * rows
    head = groups * HEAD_SIZE
    sizes = (QUERY_PER_GROUP * head, head, head, QUERY_PER_GROUP * head)
    outs = [(count // 2, rows, width)] * 2 + [(2, places, size) for size in sizes]
    return order.call(
        "attend",
        lambda *refs: attend_kernel(count, groups, *refs),
        (1,),
        [SCALARS]
        + [block_spec(block, (rows, width), lambda _: (0, 1, 0)) for block in blocks]
        + [whole(item.shape) for item in (cosine, sine, weights)],
        [whole(shape) for shape in outs],
        [jax.ShapeDtypeStruct(shape, BF) for shape in outs],
        flops=4 * places * weights.size + 16 * places * places * QUERY_PER_GROUP * head,
        moved=8 * places * width + 2 * weights.size,
        args=(scalars, *arrays(blocks), cosine, sine, weights),
    )


def attend_back_kernel(count, groups, scalar_ref, *refs):
    pieces = refs[:count]
    cos_ref, sin_ref, w_ref, q_ref, k_ref, v_ref, keep_ref, send_ref, grad_ref = refs[count:]
    rows = pieces[0].shape[0]
    cols = count // 2
    span = (QUERY_PER_GROUP + 2) * HEAD_SIZE
    scale = HEAD_SIZE ** (-0.5)
    cosine, sine = cos_ref[...], -sin_ref[...]
    for y in (0, 1):
        piece = joined(pieces[y * cols : (y + 1) * cols])
        grad_out = dot(piece, w_ref[:, groups * span :], 1, 0).astype(BF)
        parts = []
        for g in range(groups):
            keys, values = k_ref[y, :, head_at(g)], v_ref[y, :, head_at(g)]
            keys_grad, values_grad = 0.0, 0.0
            for r in range(QUERY_PER_GROUP):
                at = head_at(g * QUERY_PER_GROUP + r)
                query, upstream = q_ref[y, :, at], grad_out[:, at]
                probs = head_probs(query, keys, scalar_ref[0], scalar_ref[1 + y], rows)
                grad_probs = dot(upstream, values, 1, 1)
                values_grad = values_grad + dot(probs.astype(BF), upstream, 0, 0)
                inner = jnp.sum(probs * grad_probs, axis=-1, keepdims=True)
                grad_scores = (probs * (grad_probs - inner)).astype(BF)
                parts.append(turn(dot(grad_scores, keys, 1, 0) * scale, cosine, sine))
                keys_grad = keys_grad + dot(grad_scores, query, 0, 0)
            parts.extend((turn(keys_grad * scale, cosine, sine), values_grad))
        grad_proj = jnp.concatenate([part.astype(BF) for part in parts], axis=1)
        grad_ref[y] = grad_proj
        put_blocks(dot(grad_proj, w_ref[:, : groups * span], 1, 1), y, cols // 2, keep_ref, send_ref)


def attend_back(pieces, rows, scalars, cosine, sine, weights, saved, groups, order):
    count = len(pieces)
    width = pieces[0][0].shape[1]
    places = count // 2 * rows
    span = groups * (QUERY_PER_GROUP + 2) * HEAD_SIZE
    outs = [(count // 2, rows, width)] * 2 + [(2, places, span)]
    return order.call(
        "attend_back",
        lambda *refs: attend_back_kernel(count, groups, *refs),
        (1,),
        [SCALARS]
        + [block_spec(block, (rows, width), lambda _: (0, 1, 0)) for block in pieces]
        + [whole(item.shape) for item in (cosine, sine, weights, *saved)],
        [whole(shape) for shape in outs],
        [jax.ShapeDtypeStruct(shape, BF) for shape in outs],
        flops=4 * places * weights.size + 48 * places * places * groups * HEAD_SIZE,
        moved=8 * places * width + 2 * weights.size,
        args=(scalars, *arrays(pieces), cosine, sine, weights, *saved),
    )


def units_kernel(count, cut, *refs):
    rows_refs, piece_refs = refs[:count], refs[count : 2 * count]
    w_ref, pair_ref, hidden_ref = refs[2 * count :]
    gate_up = dot(joined(rows_refs), w_ref[:, : 2 * cut], 1, 0)
    hidden_grad = dot(joined(piece_refs), w_ref[:, 2 * cut :], 1, 0)
    gate, up = gate_up[:, :cut], gate_up[:, cut:]
    sigma = 1.0 / (1.0 + jnp.exp(-gate))
    swish = gate * sigma
    hidden_ref[...] = (swish * up).astype(BF).reshape(hidden_ref.shape)
    pair_ref[..., :cut] = (
        (hidden_grad * up * sigma * (1.0 + gate * (1.0 - sigma))).astype(BF).reshape(hidden_ref.shape)
    )
    pair_ref[..., cut:] = (hidden_grad * swish).astype(BF).reshape(hidden_ref.shape)


def units(rows, pieces, places, weights, order):
    count = len(rows)
    width = weights.shape[0]
    cut = weights.shape[1] // 3
    part = places // 4
    return order.call(
        "units",
        lambda *refs: units_kernel(count, cut, *refs),
        (4,),
        [block_spec(block, (part, width), lambda l: (l, 4, 0)) for block in (*rows, *pieces)]
        + [whole(weights.shape)],
        [pl.BlockSpec((count, part, size), lambda l: (0, l, 0)) for size in (2 * cut, cut)],
        [shaped(count, places, size) for size in (2 * cut, cut)],
        flops=2 * count * places * weights.size,
        moved=4 * count * places * width,
        args=(*arrays(rows), *arrays(pieces), weights),
    )


def grads_kernel(counts, *refs):
    grad_ref = refs[-1]
    size = grad_ref.shape[2]
    start = at = 0
    lefts = refs[sum(n for n, _ in counts) :]
    for n, k in counts:
        rows = joined(refs[start : start + n])
        left = jnp.concatenate([ref[...] for ref in lefts[:k]], axis=0)
        start, lefts = start + n, lefts[k:]
        product = dot(left, rows, 0, 0).astype(BF)
        for block in range(grad_ref.shape[0]):
            grad_ref[block, at : at + product.shape[0]] = product[:, block * size : (block + 1) * size]
        at += product.shape[0]


def weight_grads(products, places, owners, order, total=None, into=None):
    rows = [block for blocks, _ in products for block in blocks]
    lefts = [left for _, items in products for left in items]
    counts = [(len(blocks), len(items)) for blocks, items in products]
    width = rows[0][0].shape[1]
    tile = width // 4
    part = sum(items[0].shape[1] for _, items in products)
    total = total or part
    at = 0 if into is None else total // part - 1
    tokens = len(products[0][0]) * places
    args = (*arrays(rows), *lefts) + (() if into is None else (into,))
    return order.call(
        "weight_grads",
        lambda *refs: grads_kernel(counts, *refs),
        (4,),
        [block_spec(block, (places, tile), lambda t: (0, 1, t)) for block in rows]
        + [whole(left.shape) for left in lefts]
        + [pl.BlockSpec(memory_space=pl.ANY)] * (into is not None),
        pl.BlockSpec((owners // 4, part, width // owners), lambda t: (t, at, 0)),
        shaped(owners, total, width // owners),
        flops=2 * tokens * part * width,
        moved=2 * len(products) * tokens * width,
        args=args,
        aliases={} if into is None else {len(args) - 1: 0},
    )


def back_kernel(count, split, added, *refs):
    lefts, weights = refs[:count], refs[count : 2 * count]
    refs = refs[2 * count :]
    total = refs[0][...] if added else None
    refs = refs[1:] if added else refs
    for left, weight in zip(lefts, weights):
        product = dot(left[...].reshape(-1, left.shape[-1]), weight[...], 1, 1)
        total = product if total is None else total + product
    if split:
        put_blocks(total, 0, refs[0].shape[0], *refs)
    else:
        refs[0][...] = total


def back(lefts, weights, lo, order, before=None, stream=None):
    count, places, depth = lefts[0].shape
    width = weights[0].shape[0]
    added, split = before is not None, stream is not None
    first = 2 * stream if split else 0
    half = pl.BlockSpec((2, places, width), lambda t: (t, 0, 0))
    flat = pl.BlockSpec((4 * places, width), lambda t: (first + t, 0))
    halves = shaped(4, places, width)
    steps = 2 if split else count // 4
    return order.call(
        "back",
        lambda *refs: back_kernel(len(lefts), split, added, *refs),
        (steps,),
        [pl.BlockSpec((4, places, depth), lambda t: (first + t, 0, 0))] * len(lefts)
        + [pl.BlockSpec((width, depth), lambda t: (0, lo // depth))] * len(weights)
        + ([flat] if added else []),
        [half, half] if split else flat,
        [halves, halves] if split else shaped(count * places, width, dtype=F32),
        flops=8 * steps * places * depth * width * len(lefts),
        moved=16 * steps * places * width,
        args=(*lefts, *weights, *((before,) if added else ())),
    )


def finish_ffn_kernel(count, cut, low_ref, *refs):
    pairs, cames = refs[:count], refs[count : 2 * count]
    w1_ref, w3_ref, gain_ref, grad1_ref, grad3_ref, grad2_ref, sum_ref = refs[2 * count :]
    units = w1_ref.shape[1] // 2
    gain, total = gain_ref[...], 0.0
    for chunk in range(count):
        for part, value in (
            (low_ref[0], pairs[chunk][low_ref[0]]),
            (1 - low_ref[0], cames[chunk][...]),
        ):
            place = pl.ds(pl.multiple_of(part * units + chunk * cut, cut), cut)
            value = value.astype(F32)
            first, second = value[:cut].T, value[cut : 2 * cut].T
            grad2_ref[place, :] = value[2 * cut :]
            grad1_ref[:, place] = first * gain
            grad3_ref[:, place] = second * gain
            product = first * w1_ref[:, place].astype(F32) + second * w3_ref[:, place].astype(F32)
            total = total + jnp.sum(product, axis=1, keepdims=True)
    sum_ref[...] = as_row(total)


def as_row(column):
    return jnp.broadcast_to(column, (column.shape[0], 128)).T[:1]


def finish_ffn(low, parts, w1, w3, w2, gain, order):
    count = len(parts)
    args = [pair for pair, _ in parts] + [came for _, came in parts] + [w1, w3, gain]
    outs = [shaped(*shape, dtype=F32) for shape in (w1.shape, w3.shape, w2.shape, gain.shape[::-1])]
    return order.call(
        "finish_ffn",
        lambda *refs: finish_ffn_kernel(count, parts[0][1].shape[0] // 3, *refs),
        (1,),
        [SCALARS] + [whole(item.shape) for item in args],
        [whole(item.shape) for item in outs],
        outs,
        (low, *args),
        moved=24 * w1.size,
    )


def finish_attn_kernel(low_ref, pair_ref, came_ref, w_ref, gain_ref, grad_ref, out_ref, sum_ref):
    wide = w_ref.shape[1] // 2
    tall = out_ref.shape[0] // 2
    gain, total = gain_ref[...], 0.0
    for part, value in ((low_ref[0], pair_ref[low_ref[0]]), (1 - low_ref[0], came_ref[...])):
        columns = pl.ds(pl.multiple_of(part * wide, wide), wide)
        value = value.astype(F32)
        first = value[:wide].T
        grad_ref[:, columns] = first * gain
        out_ref[pl.ds(pl.multiple_of(part * tall, tall), tall), :] = value[wide:]
        total = total + jnp.sum(first * w_ref[:, columns].astype(F32), axis=1, keepdims=True)
    sum_ref[...] = as_row(total)


def finish_attn(low, pair, came, wqkv, wo, gain, order):
    args = [pair, came, wqkv, gain]
    outs = [shaped(*shape, dtype=F32) for shape in (wqkv.shape, wo.shape, gain.shape[::-1])]
    return order.call(
        "finish_attn",
        finish_attn_kernel,
        (1,),
        [SCALARS] + [whole(item.shape) for item in args],
        [whole(item.shape) for item in outs],
        outs,
        (low, *args),
        moved=12 * wqkv.size,
    )


def body(inputs, lengths, wqkv, wo, w1, w3, w2, attn_gain, ffn_gain, cotangent):
    micro, _, rows, width = inputs.shape
    cols = lax.axis_size("col")
    places = cols * rows
    me = lax.axis_index("col")
    groups = wqkv.shape[1] // ((QUERY_PER_GROUP + 2) * HEAD_SIZE) // 2
    cut = w1.shape[1] // 2 // CHUNKS
    d = wqkv.shape[0]
    owners = width // d
    streams = range(micro)
    inputs, cotangent = inputs[:, 0], cotangent[:, 0]
    order = Order()
    low = (lax.axis_index("dp") % 2).astype(jnp.int32)[None]
    attn_gain, ffn_gain = attn_gain.astype(F32)[:, None], ffn_gain.astype(F32)[:, None]

    def prepared(*chunks):
        return prepare_ffn(chunks, cut, low, w1, w3, w2, ffn_gain, order)

    positions = (
        (jnp.arange(cols, dtype=jnp.int32) ^ me)[:, None] * rows
        + jnp.arange(rows, dtype=jnp.int32)[None, :]
    ).reshape(places)
    cosine, sine = rope_tables(positions)
    other_lengths = xchg(lengths, "dp", 1)
    scalars = [
        jnp.concatenate((me.astype(jnp.int32)[None], lengths[m], other_lengths[m])) for m in streams
    ]
    own_scalars = jnp.concatenate(((me * rows).astype(jnp.int32)[None], lengths.reshape(micro)))

    came = xchg(prepare_attn(1 - low, wqkv, wo, attn_gain, order), "dp", 1)
    mine = prepare_attn(low, wqkv, wo, attn_gain, order)
    normed1 = first_norm(inputs, order)
    attn_w = gather_weight(mine, came, low, order)
    attn_gather = Gather(normed1.reshape(-1, width), rows, False)
    attn_gather.cross(order)
    ((mine, sent),) = prepared(0)
    order.wait(cosine, sine, *scalars)
    (came,) = attn_gather.fence(order, xchg(sent, "dp", 1))
    ffn_ws = [gather_weight(mine, came, low, order)]
    (attn_rows,) = attn_gather.blocks(order)
    ((mine, sent),) = prepared(1)

    def run_attend(m):
        return attend(attn_rows[m], rows, scalars[m], cosine, sine, attn_w, groups, order)

    ahead = [run_attend(0), run_attend(1)]
    came, *sends = order.fence(xchg(sent, "dp", 1), *[item[1] for item in ahead])
    scatter = Scatter([(item[0], xchg(send, "col", 1)) for item, send in zip(ahead, sends)])
    ffn_ws.append(gather_weight(mine, came, low, order))
    scatter.first(order)
    scatter.second(order)
    normed2, residual = second_norm(inputs, scatter.terms()[0], cotangent, own_scalars, order)
    ffn_gather = Gather(normed2.reshape(-1, width), rows, True)
    ffn_gather.cross(order)
    ffn_gather.fence(order)
    (blocks,) = ffn_gather.blocks(order)
    all_rows, all_pieces = sum(blocks[:micro], []), sum(blocks[micro:], [])
    upstream = (normed2, (micro,), (1,))

    pairs, hiddens = [], []

    def run_units(chunk):
        pair, hidden = units(all_rows, all_pieces, rows, ffn_ws[chunk], order)
        pairs.append(pair)
        hiddens.append(hidden)

    def pair_grads(chunk):
        left = pairs[chunk].reshape(-1, 2 * cut)
        return weight_grads([(all_rows, [left])], rows, owners, order, total=3 * cut)

    def hidden_grads(chunk, into):
        left = hiddens[chunk].reshape(-1, cut)
        return weight_grads([(all_pieces, [left])], rows, owners, order, total=3 * cut, into=into)

    run_units(0)
    ffn_grads = [scatter_weight(hidden_grads(0, pair_grads(0)))]
    early = back(pairs, ffn_ws[:1], 0, order)
    run_units(1)
    halves = [back(pairs[1:], ffn_ws[1:], 0, order, before=early, stream=0)]
    first_came = xchg(halves[0][1], "col", 1)
    halves.append(back(pairs[1:], ffn_ws[1:], 0, order, before=early, stream=1))
    first_came, second_sent = order.fence(first_came, halves[1][1])
    scatter = Scatter([(halves[0][0], first_came), (halves[1][0], xchg(second_sent, "col", 1))])
    scatter.first(order)
    part = pair_grads(1)
    scatter.second(order)
    grads = hidden_grads(1, part)
    attn_up, residual_grad = second_norm_back(residual, upstream, scatter.terms()[0], order)
    attn_gather = Gather(attn_up.reshape(-1, width), rows, True)
    ffn_grads.append(scatter_weight(order.fence(grads)[0]))
    halves = [back(hiddens, ffn_ws, 2 * cut, order, stream=0)]
    sent = for_partner(ffn_grads[0], low, order)
    attn_gather.cross(order)
    halves.append(back(hiddens, ffn_ws, 2 * cut, order, stream=1))
    attn_gather.fence(order)
    attn_pieces, sent, *sends = attn_gather.blocks(order, sent, *[send for _, send in halves])
    halves = [(keep, send) for (keep, _), send in zip(halves, sends)]

    def run_back(m):
        return attend_back(
            attn_pieces[m], rows, scalars[m], cosine, sine, attn_w, ahead[m][2:5], groups, order
        )

    out_sent = [(keep, xchg(send, "col", 1)) for keep, send in halves]
    came = xchg(sent, "dp", 1)
    behind = [run_back(0)]
    first_came = xchg(behind[0][1], "col", 1)
    behind.append(run_back(1))
    came, first_came, second_sent, *values = order.fence(
        came, first_came, behind[1][1], *[item for _, item in out_sent]
    )
    ffn_parts = [(ffn_grads[0], came)]
    out_parts = [(keep, item) for (keep, _), item in zip(out_sent, values)]
    attn_parts = [(behind[0][0], first_came), (behind[1][0], xchg(second_sent, "col", 1))]
    scatter, out_scatter = Scatter(attn_parts), Scatter(out_parts)
    scatter.first(order)
    attn_grads = weight_grads(
        [
            (sum(attn_rows, []), [item[2].reshape(2 * places, -1) for item in behind]),
            (sum(attn_pieces, []), [item[5].reshape(2 * places, -1) for item in ahead]),
        ],
        rows,
        owners,
        order,
    )
    out_scatter.first(order)
    scatter.second(order)
    attn_pair = scatter_weight(order.fence(attn_grads)[0])
    sent = for_partner(ffn_grads[1], low, order)
    out_scatter.second(order)
    (came,) = order.fence(xchg(sent, "dp", 1))
    ffn_parts.append((ffn_grads[1], came))
    w1_grad, w3_grad, w2_grad, ffn_sum = finish_ffn(low, ffn_parts, w1, w3, w2, ffn_gain, order)
    ffn_sum = sum_over_col(ffn_sum)[0]
    terms = scatter.terms() + out_scatter.terms()
    sent = for_partner(attn_pair, low, order)
    source_grad, result = finished(inputs, residual_grad, residual, terms, order)
    attn_came = xchg(sent, "dp", 1)
    wqkv_grad, wo_grad, attn_sum = finish_attn(low, attn_pair, attn_came, wqkv, wo, attn_gain, order)
    attn_sum = sum_over_col(attn_sum)[0]
    return (
        result[:, None],
        source_grad[:, None],
        attn_sum,
        ffn_sum,
        wqkv_grad,
        wo_grad,
        w1_grad,
        w3_grad,
        w2_grad,
    )


def solution(mesh):
    tokens = P(None, ("dp", "row"), "col", None)
    in_specs = (
        tokens,
        P(None, ("dp", "row")),
        P(("dp", "row"), "col"),
        P("col", ("dp", "row")),
        P(("dp", "row"), "col"),
        P(("dp", "row"), "col"),
        P("col", ("dp", "row")),
        P(("dp", "row")),
        P(("dp", "row")),
        tokens,
    )
    out_specs = (
        tokens,
        tokens,
        P(("dp", "row")),
        P(("dp", "row")),
        P(("dp", "row"), "col"),
        P("col", ("dp", "row")),
        P(("dp", "row"), "col"),
        P(("dp", "row"), "col"),
        P("col", ("dp", "row")),
    )
    return jax.shard_map(body, mesh=mesh, in_specs=in_specs, out_specs=out_specs, check_vma=False)
```
